32 devices in a mesh: dom: 8 (over z, y), feat: 4 (over x, core).
Axes of the slice: x: 2, y: 2, z: 4, core: 2. Of those that a mesh axis runs over, the one named last changes fastest.
Arguments:
- features: bfloat16 [8192, 512], P('dom', 'feat'), may hold values from -6 to 6
- w_self: bfloat16 [512, 512], P('feat'), may hold values from -0.25 to 0.25
- w_neigh: bfloat16 [512, 512], P('feat'), may hold values from -0.25 to 0.25
- degree: int32 [8192], P('dom'), may hold values from 1 to 32
- local_vals: bfloat16 [8, 16, 128, 128], P('dom'), may hold values from 0 to 0.19921875
- local_dst: int32 [8, 16], P('dom'), may hold values from 0 to 7
- local_src: int32 [8, 16], P('dom'), may hold values from 0 to 7
- remote_vals: bfloat16 [8, 6, 8, 128, 128], P('dom'), may hold values from 0 to 0.19921875
- remote_dst: int32 [8, 6, 8], P('dom'), may hold values from 0 to 7
- remote_src: int32 [8, 6, 8], P('dom'), may hold values from 0 to 7
- cotangent: bfloat16 [8192, 512], P('dom', 'feat'), may hold values from -6 to 6
Outputs:
- out: bfloat16 [8192, 512], P('dom', 'feat')
- grad_x: float32 [8192, 512], P('dom', 'feat')
- grad_self: float32 [512, 512], P('feat')
- grad_neigh: float32 [512, 512], P('feat')
The draws below stay inside these ranges and needn't reach their ends.
All inputs are finite; a program needn't handle non-finite values.
Results may differ from the reference program's by a relative error of at most 0.0068.
Values may be sent and summed in bfloat16 or wider, within the bound.
No kernel may reach another device: no remote copies, remote signals or barrier semaphores. Data moves between devices by JAX's collectives and lax.ppermute only.
A program may use at most 64 MiB of HBM per device.

```python
import jax
import jax.numpy as jnp
from jax import lax

D = 512
BLK = 128
RB = 8
LT = 16
ROUNDS = 6
K = 8
NODES = 8192
N_DOM = 8


def place_ends(drawn, rng, least, high):
    extent = drawn.shape
    index_at = [jax.random.randint(jax.random.fold_in(rng, axis), (), 0, extent[axis]) for axis in range(len(extent))]
    drawn = drawn.at[tuple(index_at)].set(least)
    longest = extent.index(max(extent))
    index_at[longest] = (index_at[longest] + 1) % extent[longest]
    return drawn.at[tuple(index_at)].set(high)


def level_of(own_key, dims, split, least, largest):
    factor_of = 1.0
    for dim, blocks in split:
        heights = jax.random.uniform(jax.random.fold_in(jax.random.fold_in(own_key, 6), dim), (blocks,), jnp.float32, least / len(split), largest / len(split))
        factor_of = factor_of * jnp.repeat(jnp.exp(heights), dims[dim] // blocks).reshape((-1,) + (1,) * (len(dims) - 1 - dim))
    return factor_of


def gaussian(stream_key, extent, deviation, reach, shards=(), held_as=jnp.bfloat16):
    array = deviation * jax.random.normal(stream_key, extent, jnp.float32)
    if shards:
        array = array * level_of(stream_key, extent, shards, -0.22, 0.18)
    return jnp.clip(array, -reach, reach).astype(held_as)


def setup_inputs(seed: int = 0) -> dict:
    arg_keys = jax.random.split(jax.random.key(seed), 12)
    features = gaussian(arg_keys[0], (NODES, D), 1.0, 6.0, ((0, 8), (1, 4)))
    w_self = gaussian(arg_keys[1], (D, D), D ** -0.5, 0.25, ((0, 4),))
    w_neigh = gaussian(arg_keys[2], (D, D), D ** -0.5, 0.25, ((0, 4),))
    degree = place_ends(jax.random.randint(arg_keys[3], (NODES,), 1, 33), jax.random.fold_in(arg_keys[3], 1), 1, 32).astype(jnp.int32)
    local_vals = jnp.clip(0.19921875 * jax.random.uniform(arg_keys[4], (N_DOM, LT, BLK, BLK), jnp.float32) ** level_of(arg_keys[4], (N_DOM, LT, BLK, BLK), ((0, 8),), -0.2, 0.2), 0.0, 0.19921875).astype(jnp.bfloat16)
    local_dst = place_ends(jax.random.randint(arg_keys[5], (N_DOM, LT), 0, RB), jax.random.fold_in(arg_keys[5], 1), 0, RB - 1).astype(jnp.int32)
    local_src = place_ends(jax.random.randint(arg_keys[6], (N_DOM, LT), 0, RB), jax.random.fold_in(arg_keys[6], 1), 0, RB - 1).astype(jnp.int32)
    remote_vals = jnp.clip(0.19921875 * jax.random.uniform(arg_keys[7], (N_DOM, ROUNDS, K, BLK, BLK), jnp.float32) ** level_of(arg_keys[7], (N_DOM, ROUNDS, K, BLK, BLK), ((0, 8),), -0.2, 0.2), 0.0, 0.19921875).astype(jnp.bfloat16)
    remote_dst = place_ends(jax.random.randint(arg_keys[8], (N_DOM, ROUNDS, K), 0, RB), jax.random.fold_in(arg_keys[8], 1), 0, RB - 1).astype(jnp.int32)
    remote_src = place_ends(jax.random.randint(arg_keys[9], (N_DOM, ROUNDS, K), 0, RB), jax.random.fold_in(arg_keys[9], 1), 0, RB - 1).astype(jnp.int32)
    cotangent = gaussian(arg_keys[10], (NODES, D), 1.0, 6.0, ((0, 8), (1, 4)))
    return {"features": features, "w_self": w_self, "w_neigh": w_neigh, "degree": degree, "local_vals": local_vals, "local_dst": local_dst, "local_src": local_src, "remote_vals": remote_vals, "remote_dst": remote_dst, "remote_src": remote_src, "cotangent": cotangent}


def onehot(block_ids):
    return (block_ids[:, None] == jnp.arange(RB, dtype=jnp.int32)[None, :]).astype(jnp.float32)


def tile_apply(tiles, blocks):
    return jnp.einsum("kij,kjf->kif", tiles.astype(jnp.float32), blocks.astype(jnp.float32), precision=lax.Precision.HIGHEST)


def tile_apply_back(tiles, blocks):
    return jnp.einsum("kji,kjf->kif", tiles.astype(jnp.float32), blocks.astype(jnp.float32), precision=lax.Precision.HIGHEST)


def spread(parts, block_ids):
    return jnp.einsum("kc,kif->cif", onehot(block_ids), parts, precision=lax.Precision.HIGHEST)


def reference(features, w_self, w_neigh, degree, local_vals, local_dst, local_src, remote_vals, remote_dst, remote_src, cotangent):
    offsets = [(step + 1) * N_DOM // (ROUNDS + 1) for step in range(ROUNDS)]
    blocks = features.reshape(N_DOM, RB, BLK, D)

    def forward_sum(part):
        totals = spread(tile_apply(local_vals[part], blocks[part][local_src[part]]), local_dst[part])
        for step in range(ROUNDS):
            source = (part - offsets[step]) % N_DOM
            piece = tile_apply(remote_vals[source, step], blocks[source][remote_src[source, step]])
            piece = lax.optimization_barrier(piece.astype(jnp.bfloat16)).astype(jnp.float32)
            totals = totals + spread(piece, remote_dst[source, step])
        return totals

    sums = lax.map(forward_sum, jnp.arange(N_DOM, dtype=jnp.int32))
    inverse = 1.0 / degree.astype(jnp.float32)
    agg = (sums.reshape(NODES, D) * inverse[:, None]).astype(jnp.bfloat16)
    pre = jnp.dot(features, w_self, preferred_element_type=jnp.float32) + jnp.dot(agg, w_neigh, preferred_element_type=jnp.float32)
    sigma = jax.nn.sigmoid(pre)
    out = (pre * sigma).astype(jnp.bfloat16)
    dpre = (cotangent.astype(jnp.float32) * sigma * (1.0 + pre * (1.0 - sigma))).astype(jnp.bfloat16)
    grad_self = jnp.dot(features.T, dpre, preferred_element_type=jnp.float32)
    grad_neigh = jnp.dot(agg.T, dpre, preferred_element_type=jnp.float32)
    dx_self = jnp.dot(dpre, w_self.T, preferred_element_type=jnp.float32)
    dagg = jnp.dot(dpre, w_neigh.T, preferred_element_type=jnp.float32)
    dsum = (dagg * inverse[:, None]).astype(jnp.bfloat16).reshape(N_DOM, RB, BLK, D)

    def backward_sum(part):
        totals = spread(tile_apply_back(local_vals[part], dsum[part][local_dst[part]]), local_src[part])
        for step in range(ROUNDS):
            target = (part + offsets[step]) % N_DOM
            picked = dsum[target][remote_dst[part, step]]
            totals = totals + spread(tile_apply_back(remote_vals[part, step], picked), remote_src[part, step])
        return totals

    back = lax.map(backward_sum, jnp.arange(N_DOM, dtype=jnp.int32))
    grad_x = dx_self + back.reshape(NODES, D)
    return (out, grad_x, grad_self, grad_neigh)
```

```python
import functools

import jax
import jax.numpy as jnp
from jax import lax
from jax.experimental import pallas as pl
from jax.experimental.pallas import tpu as pltpu
from jax.sharding import PartitionSpec as P

F32 = jnp.float32
BF16 = jnp.bfloat16
VMEM = pl.BlockSpec(memory_space=pltpu.VMEM)
SMEM = pl.BlockSpec(memory_space=pltpu.SMEM)


def shifted(x, axis, by):
    devices = lax.axis_size(axis)
    return lax.ppermute(x, axis, [(i, (i + by) % devices) for i in range(devices)])


def spread(parts, block_ids, count):
    table = (block_ids[:, None] == jnp.arange(count, dtype=jnp.int32)[None, :]).astype(F32)
    return jnp.einsum("kc,kif->cif", table, parts, precision=lax.Precision.HIGHEST)


def tile_apply(tiles, blocks):
    return jnp.einsum("kij,kjf->kif", tiles, blocks, preferred_element_type=F32)


def tile_apply_back(tiles, blocks):
    return jnp.einsum("kji,kjf->kif", tiles, blocks, preferred_element_type=F32)


def round_offsets(parts_total, rounds):
    return [(step + 1) * parts_total // (rounds + 1) for step in range(rounds)]


def sparse_body(
    features,
    w_self,
    w_neigh,
    degree,
    local_vals,
    local_dst,
    local_src,
    remote_vals,
    remote_dst,
    remote_src,
    cotangent,
):
    rows, width = features.shape
    block = local_vals.shape[-1]
    nblocks = rows // block
    rounds = remote_vals.shape[1]
    parts_total = lax.axis_size("dom")
    offsets = round_offsets(parts_total, rounds)
    blocks = features.reshape(nblocks, block, width)
    totals = spread(
        tile_apply(local_vals[0], jnp.take(blocks, local_src[0], axis=0)), local_dst[0], nblocks
    )
    arrived_ids = []
    for step in range(rounds):
        partial_blocks = tile_apply(
            remote_vals[0, step], jnp.take(blocks, remote_src[0, step], axis=0)
        ).astype(BF16)
        arrived, block_ids = shifted((partial_blocks, remote_dst[0, step]), "dom", offsets[step])
        arrived_ids.append(block_ids)
        totals = totals + spread(arrived.astype(F32), block_ids, nblocks)
    inverse = 1.0 / degree.astype(F32)
    agg = (totals.reshape(rows, width) * inverse[:, None]).astype(BF16)
    stacked = jnp.concatenate([features, agg], axis=1)
    weights = jnp.concatenate([w_self, w_neigh], axis=0)
    pre = lax.psum_scatter(
        lax.dot_general(weights, stacked, (((0,), (1,)), ((), ())), preferred_element_type=F32),
        "feat",
        scatter_dimension=0,
        tiled=True,
    ).T
    sigma = jax.nn.sigmoid(pre)
    out = (pre * sigma).astype(BF16)
    dpre = (cotangent.astype(F32) * sigma * (1.0 + pre * (1.0 - sigma))).astype(BF16)
    dpre_all = lax.all_gather(dpre, "feat", axis=1, tiled=True)
    dz_total = lax.dot_general(
        dpre_all, weights, (((1,), (1,)), ((), ())), preferred_element_type=F32
    )
    grad_local = lax.dot_general(
        stacked, dpre_all, (((0,), (0,)), ((), ())), preferred_element_type=F32
    )
    dx_self = dz_total[:, :width]
    dsum = (dz_total[:, width:] * inverse[:, None]).astype(BF16).reshape(nblocks, block, width)
    grad_all = lax.psum(grad_local, "dom")
    back = spread(
        tile_apply_back(local_vals[0], jnp.take(dsum, local_dst[0], axis=0)), local_src[0], nblocks
    )
    for step in range(rounds):
        picked = jnp.take(dsum, arrived_ids[step], axis=0)
        returned = shifted(picked, "dom", parts_total - offsets[step])
        back = back + spread(
            tile_apply_back(remote_vals[0, step], returned), remote_src[0, step], nblocks
        )
    grad_x = dx_self + back.reshape(rows, width)
    return (out, grad_x, grad_all[:width], grad_all[width:])


def forward_tiles_kernel(
    offsets, me_ref, ldst, lsrc, rdst, rsrc, x_ref, lvals, rvals, send_ref, local_ref, prod, acc
):
    parts_total = send_ref.shape[0]
    nblocks = x_ref.shape[0]
    me = me_ref[0]
    groups = rvals.shape[1]

    def product(tile, src):
        return jnp.dot(tile, x_ref[src], preferred_element_type=F32)

    filled = set(offsets) | {0}
    for offset in range(parts_total):
        if offset not in filled:
            send_ref[lax.rem(me + offset, parts_total)] = jnp.zeros(send_ref.shape[1:], BF16)
    for step, offset in enumerate(offsets):
        slot = step % 2
        for k in range(groups):
            prod[slot, k] = product(rvals[step, k], rsrc[0, step, k])
        acc[slot] = jnp.zeros(acc.shape[1:], F32)
        for k in range(groups):
            dst = rdst[0, step, k]
            acc[slot, dst] = acc[slot, dst] + prod[slot, k]
        send_ref[lax.rem(me + offset, parts_total)] = acc[slot].astype(BF16)
    local_ref[...] = jnp.zeros_like(local_ref)
    tiles = lvals.shape[0]
    for start in range(0, tiles, groups):
        slot = (start // groups + len(offsets)) % 2
        ks = range(start, min(start + groups, tiles))
        for k in ks:
            prod[slot, k - start] = product(lvals[k], lsrc[0, k])
        for k in ks:
            dst = ldst[0, k]
            local_ref[dst] = local_ref[dst] + prod[slot, k - start]
    send_ref[me] = jnp.zeros(send_ref.shape[1:], BF16)


def forward_tiles(offsets, parts_total, me, ldst, lsrc, rdst, rsrc, blocks, lvals, rvals):
    nblocks, block, width = blocks.shape
    groups = rvals.shape[1]
    return pl.pallas_call(
        functools.partial(forward_tiles_kernel, offsets),
        out_shape=(
            jax.ShapeDtypeStruct((parts_total, nblocks, block, width), BF16),
            jax.ShapeDtypeStruct((nblocks, block, width), F32),
        ),
        in_specs=[SMEM] * 5 + [VMEM] * 3,
        out_specs=(VMEM, VMEM),
        scratch_shapes=[
            pltpu.VMEM((2, groups, block, width), F32),
            pltpu.VMEM((2, nblocks, block, width), F32),
        ],
        compiler_params=pltpu.CompilerParams(vmem_limit_bytes=24 * 2**20),
    )(me, ldst, lsrc, rdst, rsrc, blocks, lvals, rvals)


def backward_tiles_kernel(
    offsets, me_ref, ldst, lsrc, rdst, rsrc, d_ref, own_ref, lvals, rvals, grad_ref, prod
):
    parts_total = d_ref.shape[0]
    me = me_ref[0]
    groups = rvals.shape[1]

    def product(tile, blk):
        return lax.dot_general(
            tile, blk, (((0,), (0,)), ((), ())), preferred_element_type=F32
        )

    grad_ref[...] = own_ref[...]
    for step, offset in enumerate(offsets):
        slot = step % 2
        other = lax.rem(me + offset, parts_total)
        for k in range(groups):
            prod[slot, k] = product(rvals[step, k], d_ref[other, rdst[0, step, k]])
        for k in range(groups):
            src = rsrc[0, step, k]
            grad_ref[src] = grad_ref[src] + prod[slot, k]
    tiles = lvals.shape[0]
    for start in range(0, tiles, groups):
        slot = (start // groups + len(offsets)) % 2
        ks = range(start, min(start + groups, tiles))
        for k in ks:
            prod[slot, k - start] = product(lvals[k], d_ref[me, ldst[0, k]])
        for k in ks:
            src = lsrc[0, k]
            grad_ref[src] = grad_ref[src] + prod[slot, k - start]


def backward_tiles(offsets, me, ldst, lsrc, rdst, rsrc, dsum_all, own, lvals, rvals):
    nblocks, block, width = own.shape
    groups = rvals.shape[1]
    return pl.pallas_call(
        functools.partial(backward_tiles_kernel, offsets),
        out_shape=jax.ShapeDtypeStruct((nblocks, block, width), F32),
        in_specs=[SMEM] * 5 + [VMEM] * 4,
        out_specs=VMEM,
        scratch_shapes=[pltpu.VMEM((2, groups, block, width), F32)],
        compiler_params=pltpu.CompilerParams(vmem_limit_bytes=24 * 2**20),
    )(me, ldst, lsrc, rdst, rsrc, dsum_all, own, lvals, rvals)


def joined(ref):
    return jnp.concatenate([ref[j] for j in range(ref.shape[0])], axis=1)


def dense_kernel(f_ref, a_ref, c_ref, ws_ref, wn_ref, inv_ref, out_ref, dpre_ref, dsum_ref):
    feats, _, width = f_ref.shape
    pre = jnp.dot(joined(f_ref), ws_ref[...], preferred_element_type=F32)
    pre = pre + jnp.dot(joined(a_ref), wn_ref[...], preferred_element_type=F32)
    sigma = 1.0 / (1.0 + jnp.exp(-pre))
    out = (pre * sigma).astype(BF16)
    dpre = (joined(c_ref).astype(F32) * sigma * (1.0 + pre * (1.0 - sigma))).astype(BF16)
    dagg = lax.dot_general(
        dpre, wn_ref[...], (((1,), (1,)), ((), ())), preferred_element_type=F32
    )
    dsum = (dagg * inv_ref[...]).astype(BF16)
    dpre_ref[...] = dpre
    for j in range(feats):
        out_ref[j] = out[:, j * width : (j + 1) * width]
        dsum_ref[j] = dsum[:, j * width : (j + 1) * width]


def dense(f_rows, a_rows, c_rows, ws_all, wn_all, inv_rows):
    feats, some, width = f_rows.shape
    return pl.pallas_call(
        dense_kernel,
        out_shape=(
            jax.ShapeDtypeStruct((feats, some, width), BF16),
            jax.ShapeDtypeStruct((some, feats * width), BF16),
            jax.ShapeDtypeStruct((feats, some, width), BF16),
        ),
        in_specs=[VMEM] * 6,
        out_specs=(VMEM, VMEM, VMEM),
        compiler_params=pltpu.CompilerParams(vmem_limit_bytes=24 * 2**20),
    )(f_rows, a_rows, c_rows, ws_all, wn_all, inv_rows)


def swap_feat(x):
    return lax.all_to_all(x, "feat", split_axis=0, concat_axis=0, tiled=True)


def dense_body(
    features,
    w_self,
    w_neigh,
    degree,
    local_vals,
    local_dst,
    local_src,
    remote_vals,
    remote_dst,
    remote_src,
    cotangent,
):
    rows, width = features.shape
    block = local_vals.shape[-1]
    nblocks = rows // block
    rounds = remote_vals.shape[1]
    parts_total = lax.axis_size("dom")
    feats = lax.axis_size("feat")
    some = rows // feats
    offsets = round_offsets(parts_total, rounds)
    me = lax.axis_index("dom").astype(jnp.int32).reshape(1)
    mine = lax.axis_index("feat").astype(jnp.int32)
    inverse = 1.0 / degree.astype(F32)
    inv_rows = lax.dynamic_slice(inverse, (mine * some,), (some,))[:, None]

    weights = lax.all_gather(jnp.stack([w_self, w_neigh]), "feat", axis=1, tiled=True)
    early = swap_feat(
        jnp.stack(
            [features.reshape(feats, some, width), cotangent.reshape(feats, some, width)], axis=1
        )
    )
    ids = (local_dst, local_src, remote_dst, remote_src)
    send, local_sum = forward_tiles(
        offsets,
        parts_total,
        me,
        *ids,
        features.reshape(nblocks, block, width),
        local_vals[0],
        remote_vals[0],
    )
    arrived = lax.psum_scatter(send, "dom", scatter_dimension=0, tiled=True)
    sums = local_sum + arrived[0].astype(F32)
    agg = (sums.reshape(rows, width) * inverse[:, None]).astype(BF16)
    agg_rows = swap_feat(agg.reshape(feats, some, width))
    out_rows, dpre_rows, dsum_rows = dense(
        early[:, 0], agg_rows, early[:, 1], weights[0], weights[1], inv_rows
    )
    dsum = swap_feat(dsum_rows)
    dsum_all = lax.all_gather(dsum.reshape(nblocks, block, width), "dom", axis=0, tiled=False)
    dpre = lax.all_gather(dpre_rows, "feat", axis=0, tiled=True)
    out = swap_feat(out_rows).reshape(rows, width)
    dx_self = lax.dot_general(dpre, w_self, (((1,), (1,)), ((), ())), preferred_element_type=F32)
    grad_local = lax.dot_general(
        jnp.concatenate([features, agg], axis=1),
        dpre,
        (((0,), (0,)), ((), ())),
        preferred_element_type=F32,
    )
    grad_all = lax.psum(grad_local, "dom")
    grad_x = backward_tiles(
        offsets,
        me,
        *ids,
        dsum_all,
        dx_self.reshape(nblocks, block, width),
        local_vals[0],
        remote_vals[0],
    )
    return (out, grad_x.reshape(rows, width), grad_all[:width], grad_all[width:])


def solution(mesh):
    def body(*args):
        rounds = args[7].shape[1]
        nearly_all = mesh.shape["dom"] <= rounds + 2
        return (dense_body if nearly_all else sparse_body)(*args)

    placed = (
        P("dom", "feat"),
        P("feat", None),
        P("feat", None),
        P("dom"),
        P("dom", None, None, None),
        P("dom", None),
        P("dom", None),
        P("dom", None, None, None, None),
        P("dom", None, None),
        P("dom", None, None),
        P("dom", "feat"),
    )
    return jax.shard_map(
        body,
        mesh=mesh,
        in_specs=placed,
        out_specs=(P("dom", "feat"), P("dom", "feat"), P("feat", None), P("feat", None)),
        check_vma=False,
    )
```

```python
import functools

import jax
import jax.numpy as jnp
from jax import lax
from jax.experimental import pallas as pl
from jax.experimental.pallas import tpu as pltpu
from jax.sharding import PartitionSpec as P

F32 = jnp.float32
BF16 = jnp.bfloat16
VMEM = pl.BlockSpec(memory_space=pltpu.VMEM)
SMEM = pl.BlockSpec(memory_space=pltpu.SMEM)


def shifted(x, axis, by):
    devices = lax.axis_size(axis)
    return lax.ppermute(x, axis, [(i, (i + by) % devices) for i in range(devices)])


def spread(parts, block_ids, count):
    table = (block_ids[:, None] == jnp.arange(count, dtype=jnp.int32)[None, :]).astype(F32)
    return jnp.einsum("kc,kif->cif", table, parts, precision=lax.Precision.HIGHEST)


def tile_apply(tiles, blocks):
    return jnp.einsum("kij,kjf->kif", tiles, blocks, preferred_element_type=F32)


def tile_apply_back(tiles, blocks):
    return jnp.einsum("kji,kjf->kif", tiles, blocks, preferred_element_type=F32)


def round_offsets(parts_total, rounds):
    return [(step + 1) * parts_total // (rounds + 1) for step in range(rounds)]


def sparse_body(
    features,
    w_self,
    w_neigh,
    degree,
    local_vals,
    local_dst,
    local_src,
    remote_vals,
    remote_dst,
    remote_src,
    cotangent,
):
    rows, width = features.shape
    block = local_vals.shape[-1]
    nblocks = rows // block
    rounds = remote_vals.shape[1]
    parts_total = lax.axis_size("dom")
    offsets = round_offsets(parts_total, rounds)
    blocks = features.reshape(nblocks, block, width)
    totals = spread(
        tile_apply(local_vals[0], jnp.take(blocks, local_src[0], axis=0)), local_dst[0], nblocks
    )
    arrived_ids = []
    for step in range(rounds):
        partial_blocks = tile_apply(
            remote_vals[0, step], jnp.take(blocks, remote_src[0, step], axis=0)
        ).astype(BF16)
        arrived, block_ids = shifted((partial_blocks, remote_dst[0, step]), "dom", offsets[step])
        arrived_ids.append(block_ids)
        totals = totals + spread(arrived.astype(F32), block_ids, nblocks)
    inverse = 1.0 / degree.astype(F32)
    agg = (totals.reshape(rows, width) * inverse[:, None]).astype(BF16)
    stacked = jnp.concatenate([features, agg], axis=1)
    weights = jnp.concatenate([w_self, w_neigh], axis=0)
    pre = lax.psum_scatter(
        lax.dot_general(weights, stacked, (((0,), (1,)), ((), ())), preferred_element_type=F32),
        "feat",
        scatter_dimension=0,
        tiled=True,
    ).T
    sigma = jax.nn.sigmoid(pre)
    out = (pre * sigma).astype(BF16)
    dpre = (cotangent.astype(F32) * sigma * (1.0 + pre * (1.0 - sigma))).astype(BF16)
    dpre_all = lax.all_gather(dpre, "feat", axis=1, tiled=True)
    dz_total = lax.dot_general(
        dpre_all, weights, (((1,), (1,)), ((), ())), preferred_element_type=F32
    )
    grad_local = lax.dot_general(
        stacked, dpre_all, (((0,), (0,)), ((), ())), preferred_element_type=F32
    )
    dx_self = dz_total[:, :width]
    dsum = (dz_total[:, width:] * inverse[:, None]).astype(BF16).reshape(nblocks, block, width)
    grad_all = lax.psum(grad_local, "dom")
    back = spread(
        tile_apply_back(local_vals[0], jnp.take(dsum, local_dst[0], axis=0)), local_src[0], nblocks
    )
    for step in range(rounds):
        picked = jnp.take(dsum, arrived_ids[step], axis=0)
        returned = shifted(picked, "dom", parts_total - offsets[step])
        back = back + spread(
            tile_apply_back(remote_vals[0, step], returned), remote_src[0, step], nblocks
        )
    grad_x = dx_self + back.reshape(rows, width)
    return (out, grad_x, grad_all[:width], grad_all[width:])


def tile_counts(rvals, lvals):
    return rvals.shape[0], rvals.shape[1], lvals.shape[0]


def round_of(offset, offsets):
    step, known = jnp.int32(0), offset < 0
    for at, this in enumerate(offsets):
        step = jnp.where(offset == this, at, step)
        known = known | (offset == this)
    return step, known


def crossed_block(block_id, mine, per_feat):
    return ((block_id // per_feat) ^ mine) * per_feat + block_id % per_feat


def tile_groups(masks, offsets, parts_total, me, rounds, groups, tiles):
    ids_at = (2, 2 + tiles, 2 + 2 * tiles, 2 + 2 * tiles + rounds * groups)
    jobs = []
    for at, mask in enumerate(masks):
        if mask == 0:
            for first in range(0, tiles, groups):
                count = min(groups, tiles - first)
                jobs.append((at, None, None, first, count, ids_at[0] + first, ids_at[1] + first))
        else:
            offset = lax.rem((me ^ mask) - me + parts_total, parts_total)
            step, known = round_of(offset, offsets)
            base = step * groups
            jobs.append((at, step, known, None, groups, ids_at[2] + base, ids_at[3] + base))
    return jobs


def tiles_kernel(
    masks, offsets, parts_total, per_feat, me_ref, lvals, rvals, *refs
):
    back = per_feat is not None
    rounds, groups, tiles = tile_counts(rvals, lvals)
    me, mine = me_ref[0], me_ref[1]
    jobs = tile_groups(masks, offsets, parts_total, me, rounds, groups, tiles)
    held, prod, acc, sems = refs[-4:]
    if back:
        own_ref, grad_ref = refs[len(masks)], refs[len(masks) + 1]
        blocks = refs[: len(masks)]
        sinks = [grad_ref] * len(masks)
    else:
        blocks = [refs[0]] * len(masks)
        sinks = refs[1 : 1 + len(masks)]
    copies = []
    for slot, (at, step, known, first, count, dst_at, src_at) in enumerate(jobs):
        source = lvals.at[pl.ds(first, count)] if step is None else rvals.at[step]
        copy = pltpu.make_async_copy(source, held.at[slot, pl.ds(0, count)], sems.at[slot])
        copy.start()
        copies.append(copy)
    if back:
        acc[0] = own_ref[...]
    total = 0
    for slot, (at, step, known, first, count, dst_at, src_at) in enumerate(jobs):
        copies[slot].wait()
        half = slot % 2
        read_at, write_at = (dst_at, src_at) if back else (src_at, dst_at)
        for k in range(count):
            block_id = me_ref[read_at + k]
            if back:
                block_id = crossed_block(block_id, mine, per_feat)
            block = blocks[at][block_id]
            if back:
                product = lax.dot_general(
                    held[slot, k], block, (((0,), (0,)), ((), ())), preferred_element_type=F32
                )
            else:
                product = jnp.dot(held[slot, k], block, preferred_element_type=F32)
            prod[half, k] = product if known is None else jnp.where(known, product, 0.0)
        fresh = not back and (slot == 0 or jobs[slot - 1][0] != at)
        if fresh:
            total = at % 2
            acc[total] = jnp.zeros(acc.shape[1:], F32)
        for k in range(count):
            into = me_ref[write_at + k]
            acc[total, into] = acc[total, into] + prod[half, k]
        last = slot == len(jobs) - 1 or jobs[slot + 1][0] != at
        if last and (not back or slot == len(jobs) - 1):
            sinks[at][...] = acc[total].astype(sinks[at].dtype)


def tiles_call(masks, offsets, parts_total, per_feat, me, lvals, rvals, blocks, sinks):
    rounds, groups, tiles = tile_counts(rvals, lvals)
    nblocks, block, width = blocks[0].shape
    slots = sum(-(-tiles // groups) if mask == 0 else 1 for mask in masks)
    flops = 2 * slots * groups * block * block * width
    return pl.pallas_call(
        functools.partial(tiles_kernel, masks, offsets, parts_total, per_feat),
        out_shape=sinks,
        in_specs=[SMEM] + [pl.BlockSpec(memory_space=pltpu.HBM)] * 2 + [VMEM] * len(blocks),
        out_specs=jax.tree.map(lambda _: VMEM, sinks),
        scratch_shapes=[
            pltpu.VMEM((slots, groups, block, block), BF16),
            pltpu.VMEM((2, groups, block, width), F32),
            pltpu.VMEM((2, nblocks, block, width), F32),
            pltpu.SemaphoreType.DMA((slots,)),
        ],
        compiler_params=pltpu.CompilerParams(vmem_limit_bytes=24 * 2**20),
        cost_estimate=pl.CostEstimate(
            flops=4 * flops,
            bytes_accessed=slots * groups * block * block * 2 + 4 * rounds * nblocks * block * width,
            transcendentals=0,
        ),
    )(me, lvals, rvals, *blocks)


def small_call(kernel, outs, scalars, arrays, scratch=(), flops=10**6):
    size = sum(t.size * t.dtype.itemsize for t in list(arrays) + list(outs))
    return pl.pallas_call(
        kernel,
        out_shape=outs,
        in_specs=[SMEM] * len(scalars) + [VMEM] * len(arrays),
        out_specs=[VMEM] * len(outs),
        scratch_shapes=scratch,
        compiler_params=pltpu.CompilerParams(vmem_limit_bytes=24 * 2**20),
        cost_estimate=pl.CostEstimate(flops=flops, bytes_accessed=size, transcendentals=0),
    )(*scalars, *arrays)


def agg_kernel(feats, me_ref, inv_ref, keep_ref, *refs):
    mine = me_ref[1]
    far_refs, agg_ref, piece_refs = refs[: -1 - feats], refs[-1 - feats], refs[-feats:]
    per_feat = piece_refs[0].shape[0]
    sums = keep_ref[...]
    for ref in far_refs:
        sums = sums + ref[...].astype(F32)
    agg_ref[...] = (sums * inv_ref[...]).astype(BF16)
    for mask, piece in enumerate(piece_refs):
        piece[...] = agg_ref[pl.ds((mine ^ mask) * per_feat, per_feat)]


def joined(parts):
    return jnp.concatenate(parts, axis=1)


def dense_kernel(me_ref, early_ref, w_ref, inv_ref, *refs):
    mine = me_ref[1]
    feats, _, some, width = early_ref.shape
    a_refs, dpre_ref = refs[:feats], refs[feats]
    dsum_refs, out_refs = refs[feats + 1 : 2 * feats + 1], refs[2 * feats + 1 : 3 * feats + 1]
    held = refs[-1]
    full = feats * width
    ws = w_ref[0].reshape(full, full)
    wn = w_ref[1].reshape(full, full)
    pre = jnp.dot(joined([early_ref[j, 0] for j in range(feats)]), ws, preferred_element_type=F32)
    for mask in range(feats):
        pre = pre + jnp.dot(
            a_refs[mask][...].reshape(some, width),
            w_ref[1, mine ^ mask],
            preferred_element_type=F32,
        )
    sigma = 1.0 / (1.0 + jnp.exp(-pre))
    out = (pre * sigma).astype(BF16)
    cot = joined([early_ref[j, 1] for j in range(feats)]).astype(F32)
    dpre = (cot * sigma * (1.0 + pre * (1.0 - sigma))).astype(BF16)
    dagg = lax.dot_general(dpre, wn, (((1,), (1,)), ((), ())), preferred_element_type=F32)
    dsum = (dagg * inv_ref[...]).astype(BF16)
    dpre_ref[...] = dpre
    for j in range(feats):
        held[0, j] = dsum[:, j * width : (j + 1) * width]
        held[1, j] = out[:, j * width : (j + 1) * width]
    for mask in range(feats):
        dsum_refs[mask][...] = held[0, mine ^ mask]
        out_refs[mask][...] = held[1, mine ^ mask]


def grad_kernel(near, far, me_ref, f_ref, a_ref, dpre_ref, w_ref, dx_ref, give_ref, keep_ref, held):
    me = me_ref[0]
    dpre = dpre_ref[...]
    width = f_ref.shape[1]
    some = held.shape[1]
    for at, ref in enumerate((f_ref, a_ref)):
        part = lax.dot_general(
            ref[...], dpre, (((0,), (0,)), ((), ())), preferred_element_type=F32
        )
        for j in range(width // some):
            held[at * (width // some) + j] = part[j * some : (j + 1) * some]
    for at, mask in enumerate(far + [0]):
        give_ref[at] = held[me ^ mask ^ near].astype(BF16)
        keep_ref[at] = held[me ^ mask]
    dx_ref[...] = lax.dot_general(
        dpre, w_ref[...], (((1,), (1,)), ((), ())), preferred_element_type=F32
    )


def finish_kernel(near, far, me_ref, *refs):
    me = me_ref[0]
    count = len(far) + 1
    found, other_ref = refs[:count], refs[count]
    self_ref, neigh_ref, held = refs[count + 1 :]
    for at, mask in enumerate(far + [0]):
        held[me ^ mask] = found[at][...].astype(F32)
        held[me ^ mask ^ near] = other_ref[at].astype(F32)
    some = held.shape[1]
    half = held.shape[0] // 2
    for j in range(half):
        self_ref[j * some : (j + 1) * some] = held[j]
        neigh_ref[j * some : (j + 1) * some] = held[half + j]


def place_kernel(me_ref, *refs):
    mine = me_ref[1]
    out_ref = refs[-1]
    for mask, ref in enumerate(refs[:-1]):
        out_ref[mine ^ mask] = ref[...]


def swap_feat(x):
    return lax.all_to_all(x, "feat", split_axis=0, concat_axis=0, tiled=True)


def crossed(x, mask, axis="dom"):
    return lax.ppermute(x, axis, [(i, i ^ mask) for i in range(lax.axis_size(axis))])


def like(shape, dtype):
    return jax.ShapeDtypeStruct(shape, dtype)


def dense_body(
    features,
    w_self,
    w_neigh,
    degree,
    local_vals,
    local_dst,
    local_src,
    remote_vals,
    remote_dst,
    remote_src,
    cotangent,
):
    rows, width = features.shape
    block = local_vals.shape[-1]
    nblocks = rows // block
    rounds = remote_vals.shape[1]
    parts_total = lax.axis_size("dom")
    feats = lax.axis_size("feat")
    some = rows // feats
    per_feat = nblocks // feats
    full = feats * width
    offsets = round_offsets(parts_total, rounds)
    near, far = 1, list(range(parts_total - 2, 0, -2))
    mine = lax.axis_index("feat").astype(jnp.int32)
    inverse = 1.0 / degree.astype(F32)
    inv_rows = lax.dynamic_slice(inverse, (mine * some,), (some,))[:, None]
    me = jnp.concatenate(
        [lax.axis_index("dom").astype(jnp.int32).reshape(1), mine.reshape(1)]
        + [t.reshape(-1) for t in (local_dst, local_src, remote_dst, remote_src)]
    )
    shape = (nblocks, block, width)
    blocks = features.reshape(shape)
    fixed = (me, local_vals[0], remote_vals[0])

    sends = tiles_call(
        [mask ^ near for mask in far + [0]],
        offsets,
        parts_total,
        None,
        *fixed,
        [blocks],
        [like(shape, BF16)] * (len(far) + 1),
    )
    keeps = tiles_call(
        far + [0],
        offsets,
        parts_total,
        None,
        *fixed,
        [blocks],
        [like(shape, F32)] * (len(far) + 1),
    )
    weights = lax.all_gather(jnp.stack([w_self, w_neigh]), "feat", axis=1, tiled=True)
    halves = [keep + crossed(send, near).astype(F32) for keep, send in zip(keeps, sends)]
    given = [half.astype(BF16) for half in halves[:-1]]
    arrived = [crossed(part, mask) for mask, part in zip(far, given)]
    early, _ = lax.optimization_barrier(
        (
            jnp.stack(
                [features.reshape(feats, some, width), cotangent.reshape(feats, some, width)],
                axis=1,
            ),
            given[-1],
        )
    )
    early, weights, arrived = lax.optimization_barrier((swap_feat(early), weights, arrived))
    agg, *agg_pieces = small_call(
        functools.partial(agg_kernel, feats),
        [like(shape, BF16)] + [like((per_feat, block, width), BF16)] * feats,
        [me],
        [inverse.reshape(nblocks, block, 1), halves[-1], *arrived],
    )
    agg_rows = [agg_pieces[0]] + [crossed(agg_pieces[m], m, "feat") for m in range(1, feats)]
    dpre_rows, *pieces = small_call(
        dense_kernel,
        [like((some, full), BF16)] + [like((some, width), BF16)] * (2 * feats),
        [me],
        [early, weights.reshape(2, feats, width, full), inv_rows, *agg_rows],
        [pltpu.VMEM((2, feats, some, width), BF16)],
        6 * some * full * full,
    )
    dsum_pieces, out_pieces = pieces[:feats], pieces[feats:]
    dsum = jnp.concatenate(
        [dsum_pieces[0]] + [crossed(dsum_pieces[m], m, "feat") for m in range(1, feats)], axis=0
    ).reshape(shape)
    found = {0: dsum}
    for mask in far:
        found[mask] = crossed(dsum, mask)
    found[near] = crossed(dsum, near)
    first = far[-1]
    found[first], found[near] = lax.optimization_barrier((found[first], found[near]))
    for mask in far[::-1]:
        found[mask ^ near] = crossed(found[mask], near)
    dpre = lax.all_gather(dpre_rows, "feat", axis=0, tiled=True)
    dpre, out_pieces, _ = lax.optimization_barrier((dpre, out_pieces, found[first]))
    out_all = [out_pieces[0]] + [crossed(out_pieces[m], m, "feat") for m in range(1, feats)]
    (out,) = small_call(place_kernel, [like((feats, some, width), BF16)], [me], out_all)
    piece = 2 * width // parts_total
    dx_self, give, keep = small_call(
        functools.partial(grad_kernel, near, far),
        [
            like((rows, width), F32),
            like((len(far) + 1, piece, full), BF16),
            like((len(far) + 1, piece, full), F32),
        ],
        [me],
        [features, agg.reshape(rows, width), dpre, w_self],
        [pltpu.VMEM((parts_total, piece, full), F32)],
        6 * rows * width * full,
    )
    keep = keep + crossed(give, near).astype(F32)
    total = keep[len(far)]
    for at, mask in enumerate(far):
        total = total + crossed(keep[at].astype(BF16), mask).astype(F32)
    total = total.astype(BF16)
    totals = [crossed(total, mask) for mask in far] + [total]
    grad_self, grad_neigh = small_call(
        functools.partial(finish_kernel, near, far),
        [like((width, full), F32)] * 2,
        [me],
        [*totals, crossed(jnp.stack(totals), near)],
        [pltpu.VMEM((parts_total, piece, full), F32)],
    )
    order = [0, near] + [mask ^ bit for mask in far[::-1] for bit in (0, near)]
    grad_x = tiles_call(
        order,
        offsets,
        parts_total,
        per_feat,
        *fixed,
        [found[mask] for mask in order] + [dx_self.reshape(shape)],
        like(shape, F32),
    )
    return (out.reshape(rows, width), grad_x.reshape(rows, width), grad_self, grad_neigh)


def solution(mesh):
    def body(*args):
        rounds = args[7].shape[1]
        parts_total = mesh.shape["dom"]
        powers = all(n & (n - 1) == 0 for n in mesh.shape.values())
        nearly_all = parts_total <= rounds + 2 and powers
        return (dense_body if nearly_all else sparse_body)(*args)

    placed = (
        P("dom", "feat"),
        P("feat", None),
        P("feat", None),
        P("dom"),
        P("dom", None, None, None),
        P("dom", None),
        P("dom", None),
        P("dom", None, None, None, None),
        P("dom", None, None),
        P("dom", None, None),
        P("dom", "feat"),
    )
    return jax.shard_map(
        body,
        mesh=mesh,
        in_specs=placed,
        out_specs=(P("dom", "feat"), P("dom", "feat"), P("feat", None), P("feat", None)),
        check_vma=False,
    )
```

```python
import functools

import jax
import jax.numpy as jnp
from jax import lax
from jax.experimental import pallas as pl
from jax.experimental.pallas import tpu as pltpu
from jax.sharding import PartitionSpec as P

F32 = jnp.float32
BF16 = jnp.bfloat16
VMEM = pl.BlockSpec(memory_space=pltpu.VMEM)
SMEM = pl.BlockSpec(memory_space=pltpu.SMEM)


def shifted(x, axis, by):
    devices = lax.axis_size(axis)
    return lax.ppermute(x, axis, [(i, (i + by) % devices) for i in range(devices)])


def spread(parts, block_ids, count):
    table = (block_ids[:, None] == jnp.arange(count, dtype=jnp.int32)[None, :]).astype(F32)
    return jnp.einsum("kc,kif->cif", table, parts, precision=lax.Precision.HIGHEST)


def tile_apply(tiles, blocks):
    return jnp.einsum("kij,kjf->kif", tiles, blocks, preferred_element_type=F32)


def tile_apply_back(tiles, blocks):
    return jnp.einsum("kji,kjf->kif", tiles, blocks, preferred_element_type=F32)


def round_offsets(parts_total, rounds):
    return [(step + 1) * parts_total // (rounds + 1) for step in range(rounds)]


def sparse_body(
    features,
    w_self,
    w_neigh,
    degree,
    local_vals,
    local_dst,
    local_src,
    remote_vals,
    remote_dst,
    remote_src,
    cotangent,
):
    rows, width = features.shape
    block = local_vals.shape[-1]
    nblocks = rows // block
    rounds = remote_vals.shape[1]
    parts_total = lax.axis_size("dom")
    offsets = round_offsets(parts_total, rounds)
    blocks = features.reshape(nblocks, block, width)
    totals = spread(
        tile_apply(local_vals[0], jnp.take(blocks, local_src[0], axis=0)), local_dst[0], nblocks
    )
    arrived_ids = []
    for step in range(rounds):
        partial_blocks = tile_apply(
            remote_vals[0, step], jnp.take(blocks, remote_src[0, step], axis=0)
        ).astype(BF16)
        arrived, block_ids = shifted((partial_blocks, remote_dst[0, step]), "dom", offsets[step])
        arrived_ids.append(block_ids)
        totals = totals + spread(arrived.astype(F32), block_ids, nblocks)
    inverse = 1.0 / degree.astype(F32)
    agg = (totals.reshape(rows, width) * inverse[:, None]).astype(BF16)
    stacked = jnp.concatenate([features, agg], axis=1)
    weights = jnp.concatenate([w_self, w_neigh], axis=0)
    pre = lax.psum_scatter(
        lax.dot_general(weights, stacked, (((0,), (1,)), ((), ())), preferred_element_type=F32),
        "feat",
        scatter_dimension=0,
        tiled=True,
    ).T
    sigma = jax.nn.sigmoid(pre)
    out = (pre * sigma).astype(BF16)
    dpre = (cotangent.astype(F32) * sigma * (1.0 + pre * (1.0 - sigma))).astype(BF16)
    dpre_all = lax.all_gather(dpre, "feat", axis=1, tiled=True)
    dz_total = lax.dot_general(
        dpre_all, weights, (((1,), (1,)), ((), ())), preferred_element_type=F32
    )
    grad_local = lax.dot_general(
        stacked, dpre_all, (((0,), (0,)), ((), ())), preferred_element_type=F32
    )
    dx_self = dz_total[:, :width]
    dsum = (dz_total[:, width:] * inverse[:, None]).astype(BF16).reshape(nblocks, block, width)
    grad_all = lax.psum(grad_local, "dom")
    back = spread(
        tile_apply_back(local_vals[0], jnp.take(dsum, local_dst[0], axis=0)), local_src[0], nblocks
    )
    for step in range(rounds):
        picked = jnp.take(dsum, arrived_ids[step], axis=0)
        returned = shifted(picked, "dom", parts_total - offsets[step])
        back = back + spread(
            tile_apply_back(remote_vals[0, step], returned), remote_src[0, step], nblocks
        )
    grad_x = dx_self + back.reshape(rows, width)
    return (out, grad_x, grad_all[:width], grad_all[width:])


def tile_counts(rvals, lvals):
    return rvals.shape[0], rvals.shape[1], lvals.shape[0]


def round_of(offset, offsets):
    step, known = jnp.int32(0), offset < 0
    for at, this in enumerate(offsets):
        step = jnp.where(offset == this, at, step)
        known = known | (offset == this)
    return step, known


def crossed_block(block_id, mine, per_feat):
    return ((block_id // per_feat) ^ mine) * per_feat + block_id % per_feat


def tile_groups(masks, offsets, parts_total, me, groups, tiles, ids):
    ldst, lsrc, rdst, rsrc = ids
    jobs = []
    for at, mask in enumerate(masks):
        if mask == 0:
            for first in range(0, tiles, groups):
                count = min(groups, tiles - first)
                dst = [ldst[0, first + k] for k in range(count)]
                src = [lsrc[0, first + k] for k in range(count)]
                jobs.append((at, None, None, first, dst, src))
        else:
            offset = lax.rem((me ^ mask) - me + parts_total, parts_total)
            step, known = round_of(offset, offsets)
            dst = [rdst[step, 0, k] for k in range(groups)]
            src = [rsrc[step, 0, k] for k in range(groups)]
            jobs.append((at, step, known, None, dst, src))
    return jobs


def tiles_kernel(masks, offsets, parts_total, back, feats, extras, *refs):
    ids, (lvals, rvals), refs = refs[:4], refs[4:6], refs[6:]
    me = lax.axis_index("dom")
    mine = lax.axis_index("feat")
    rounds, groups, tiles = tile_counts(rvals, lvals)
    jobs = tile_groups(masks, offsets, parts_total, me, groups, tiles, ids)
    held, prod, acc, sems = refs[-4:]
    copies = []
    for slot, (at, step, known, first, dst, src) in enumerate(jobs):
        source = lvals.at[pl.ds(first, len(dst))] if step is None else rvals.at[step]
        copy = pltpu.make_async_copy(source, held.at[slot, pl.ds(0, len(dst))], sems.at[slot])
        copy.start()
        copies.append(copy)
    if back:
        own_ref, grad_ref = refs[len(masks)], refs[len(masks) + 1]
        blocks = refs[: len(masks)]
        sinks = [grad_ref] * len(masks)
        acc[0] = own_ref[...]
    else:
        blocks = [refs[0]] * len(masks)
        sinks = refs[1 + extras : 1 + extras + len(masks)]
    if extras:
        pieces = refs[1 + extras + len(masks) : 1 + extras + len(masks) + feats]
        for mask, piece in enumerate(pieces):
            rows = pl.ds((mine ^ mask) * piece.shape[1], piece.shape[1])
            piece[0] = refs[0][rows]
            piece[1] = refs[1][rows]
    total = 0
    for slot, (at, step, known, first, dst, src) in enumerate(jobs):
        copies[slot].wait()
        half = slot % 2
        for k in range(len(dst)):
            if back:
                per_feat = blocks[at].shape[0] // feats
                block = blocks[at][crossed_block(dst[k], mine, per_feat)]
                product = lax.dot_general(
                    held[slot, k], block, (((0,), (0,)), ((), ())), preferred_element_type=F32
                )
            else:
                product = jnp.dot(
                    held[slot, k], blocks[at][src[k]], preferred_element_type=F32
                )
            prod[half, k] = product if known is None else jnp.where(known, product, 0.0)
        fresh = not back and (slot == 0 or jobs[slot - 1][0] != at)
        if fresh:
            total = at % 2
            acc[total] = jnp.zeros(acc.shape[1:], F32)
        for k in range(len(dst)):
            into = src[k] if back else dst[k]
            acc[total, into] = acc[total, into] + prod[half, k]
        last = slot == len(jobs) - 1 or jobs[slot + 1][0] != at
        if last and (not back or slot == len(jobs) - 1):
            sinks[at][...] = acc[total].astype(sinks[at].dtype)


def tiles_call(masks, offsets, parts_total, back, feats, fixed, blocks, sinks, room):
    ids, lvals, rvals = fixed
    rounds, groups, tiles = tile_counts(rvals, lvals)
    nblocks, block, width = blocks[0].shape
    slots = sum(-(-tiles // groups) if mask == 0 else 1 for mask in masks)
    flops = 2 * slots * groups * block * block * width
    extras = 0 if back else len(blocks) - 1
    return pl.pallas_call(
        functools.partial(tiles_kernel, masks, offsets, parts_total, back, feats, extras),
        out_shape=sinks,
        in_specs=[SMEM] * 4
        + [pl.BlockSpec(memory_space=pltpu.HBM)] * 2
        + [VMEM] * len(blocks),
        out_specs=jax.tree.map(lambda _: VMEM, sinks),
        scratch_shapes=[
            pltpu.VMEM((slots, groups, block, block), BF16),
            pltpu.VMEM((2, groups, block, width), F32),
            pltpu.VMEM((2, nblocks, block, width), F32),
            pltpu.SemaphoreType.DMA((slots,)),
        ],
        compiler_params=pltpu.CompilerParams(vmem_limit_bytes=room * 2**20),
        cost_estimate=pl.CostEstimate(
            flops=4 * flops,
            bytes_accessed=slots * groups * block * block * 2 + 4 * rounds * nblocks * block * width,
            transcendentals=0,
        ),
    )(*ids, lvals, rvals, *blocks)


def small_call(kernel, outs, arrays, scratch=(), flops=10**6):
    size = sum(t.size * t.dtype.itemsize for t in list(arrays) + list(outs))
    return pl.pallas_call(
        kernel,
        out_shape=outs,
        in_specs=[VMEM] * len(arrays),
        out_specs=[VMEM] * len(outs),
        scratch_shapes=scratch,
        compiler_params=pltpu.CompilerParams(vmem_limit_bytes=24 * 2**20),
        cost_estimate=pl.CostEstimate(flops=flops, bytes_accessed=size, transcendentals=0),
    )(*arrays)


def agg_kernel(feats, inv_ref, keep_ref, *refs):
    mine = lax.axis_index("feat")
    far_refs, agg_ref, piece_refs = refs[: -1 - feats], refs[-1 - feats], refs[-feats:]
    per_feat = piece_refs[0].shape[0]
    sums = keep_ref[...]
    for ref in far_refs:
        sums = sums + ref[...].astype(F32)
    agg_ref[...] = (sums * inv_ref[...]).astype(BF16)
    for mask, piece in enumerate(piece_refs):
        piece[...] = agg_ref[pl.ds((mine ^ mask) * per_feat, per_feat)]


def joined(parts):
    return jnp.concatenate(parts, axis=1)


def dense_kernel(feats, w_ref, inv_ref, *refs):
    mine = lax.axis_index("feat")
    early_refs, a_refs = refs[:feats], refs[feats : 2 * feats]
    dpre_ref = refs[2 * feats]
    dsum_refs, out_refs = refs[2 * feats + 1 : 3 * feats + 1], refs[3 * feats + 1 : 4 * feats + 1]
    held = refs[-1]
    width, full = w_ref.shape[2:]
    some = held.shape[2]
    pre = jnp.zeros((some, full), F32)
    for mask in range(feats):
        early = early_refs[mask]
        pre = pre + jnp.dot(
            early[0].reshape(some, width), w_ref[0, mine ^ mask], preferred_element_type=F32
        )
        pre = pre + jnp.dot(
            a_refs[mask][...].reshape(some, width),
            w_ref[1, mine ^ mask],
            preferred_element_type=F32,
        )
        held[0, mine ^ mask] = early[1].reshape(some, width)
    sigma = 1.0 / (1.0 + jnp.exp(-pre))
    out = (pre * sigma).astype(BF16)
    cot = joined([held[0, j] for j in range(feats)]).astype(F32)
    dpre = (cot * sigma * (1.0 + pre * (1.0 - sigma))).astype(BF16)
    wn = w_ref[1].reshape(full, full)
    dagg = lax.dot_general(dpre, wn, (((1,), (1,)), ((), ())), preferred_element_type=F32)
    dsum = (dagg * inv_ref[...]).astype(BF16)
    dpre_ref[...] = dpre
    for j in range(feats):
        held[0, j] = dsum[:, j * width : (j + 1) * width]
        held[1, j] = out[:, j * width : (j + 1) * width]
    for mask in range(feats):
        dsum_refs[mask][...] = held[0, mine ^ mask]
        out_refs[mask][...] = held[1, mine ^ mask]


def grad_kernel(near, far, f_ref, a_ref, dpre_ref, w_ref, dx_ref, give_ref, keep_ref, held):
    me = lax.axis_index("dom")
    dpre = dpre_ref[...]
    width = f_ref.shape[1]
    some = held.shape[1]
    for at, ref in enumerate((f_ref, a_ref)):
        part = lax.dot_general(
            ref[...], dpre, (((0,), (0,)), ((), ())), preferred_element_type=F32
        )
        for j in range(width // some):
            held[at * (width // some) + j] = part[j * some : (j + 1) * some]
    for at, mask in enumerate(far + [0]):
        give_ref[at] = held[me ^ mask ^ near].astype(BF16)
        keep_ref[at] = held[me ^ mask]
    dx_ref[...] = lax.dot_general(
        dpre, w_ref[...], (((1,), (1,)), ((), ())), preferred_element_type=F32
    )


def finish_kernel(near, far, *refs):
    me = lax.axis_index("dom")
    count = len(far) + 1
    found, other_ref = refs[:count], refs[count]
    self_ref, neigh_ref, held = refs[count + 1 :]
    for at, mask in enumerate(far + [0]):
        held[me ^ mask] = found[at][...].astype(F32)
        held[me ^ mask ^ near] = other_ref[at].astype(F32)
    some = held.shape[1]
    half = held.shape[0] // 2
    for j in range(half):
        self_ref[j * some : (j + 1) * some] = held[j]
        neigh_ref[j * some : (j + 1) * some] = held[half + j]


def place_kernel(*refs):
    mine = lax.axis_index("feat")
    out_ref = refs[-1]
    for mask, ref in enumerate(refs[:-1]):
        out_ref[mine ^ mask] = ref[...]


def swap_feat(x):
    return lax.all_to_all(x, "feat", split_axis=0, concat_axis=0, tiled=True)


def crossed(x, mask, axis="dom"):
    return lax.ppermute(x, axis, [(i, i ^ mask) for i in range(lax.axis_size(axis))])


def like(shape, dtype):
    return jax.ShapeDtypeStruct(shape, dtype)


def dense_body(
    features,
    w_self,
    w_neigh,
    degree,
    local_vals,
    local_dst,
    local_src,
    remote_vals,
    remote_dst,
    remote_src,
    cotangent,
):
    rows, width = features.shape
    block = local_vals.shape[-1]
    nblocks = rows // block
    rounds = remote_vals.shape[1]
    parts_total = lax.axis_size("dom")
    feats = lax.axis_size("feat")
    some = rows // feats
    per_feat = nblocks // feats
    full = feats * width
    offsets = round_offsets(parts_total, rounds)
    near, far = 1, list(range(parts_total - 2, 0, -2))
    bits = [1 << n for n in range(parts_total.bit_length() - 1)]
    mine = lax.axis_index("feat").astype(jnp.int32)
    inverse = 1.0 / degree.astype(F32)
    inv_rows = lax.dynamic_slice(inverse, (mine * some,), (some,))[:, None]
    ids = (
        local_dst,
        local_src,
        jnp.swapaxes(remote_dst, 0, 1),
        jnp.swapaxes(remote_src, 0, 1),
    )
    shape = (nblocks, block, width)
    blocks = features.reshape(shape)
    fixed = (ids, local_vals[0], remote_vals[0])

    def forward(masks, arrays, sinks):
        return tiles_call(
            masks, offsets, parts_total, False, feats, fixed, arrays, sinks, 62
        )

    sends = forward([mask ^ near for mask in far + [0]], [blocks], [like(shape, BF16)] * (len(far) + 1))
    pair, _ = lax.optimization_barrier((jnp.stack([w_self, w_neigh]), sends[0]))
    weights = lax.all_gather(pair, "feat", axis=1, tiled=True)
    made = forward(
        far + [0],
        [blocks, cotangent.reshape(shape)],
        [like(shape, F32)] * (len(far) + 1) + [like((2, per_feat, block, width), BF16)] * feats,
    )
    keeps, early_pieces = made[: len(far) + 1], made[len(far) + 1 :]
    parts = {mask: [keep] for mask, keep in zip(far + [0], keeps)}
    for mask, send in zip(far + [0], sends):
        parts[mask].append(crossed(send, near).astype(F32))
    for bit in bits[1:]:
        for mask in sorted((m for m in parts if m & bit), reverse=True):
            whole = sum(parts.pop(mask)).astype(BF16)
            parts[mask ^ bit].append(crossed(whole, bit).astype(F32))
    keep, *arrived = parts[0]
    arrived = [part.astype(BF16) for part in arrived]
    early_pieces, _ = lax.optimization_barrier((early_pieces, whole))
    early = [early_pieces[0]] + [crossed(early_pieces[m], m, "feat") for m in range(1, feats)]
    early, weights, arrived = lax.optimization_barrier((early, weights, arrived))
    agg, *agg_pieces = small_call(
        functools.partial(agg_kernel, feats),
        [like(shape, BF16)] + [like((per_feat, block, width), BF16)] * feats,
        [inverse.reshape(nblocks, block, 1), keep, *arrived],
    )
    agg_rows = [agg_pieces[0]] + [crossed(agg_pieces[m], m, "feat") for m in range(1, feats)]
    dpre_rows, *pieces = small_call(
        functools.partial(dense_kernel, feats),
        [like((some, full), BF16)] + [like((some, width), BF16)] * (2 * feats),
        [weights.reshape(2, feats, width, full), inv_rows, *early, *agg_rows],
        [pltpu.VMEM((2, feats, some, width), BF16)],
        6 * some * full * full,
    )
    dsum_pieces, out_pieces = pieces[:feats], pieces[feats:]
    dsum = jnp.concatenate(
        [dsum_pieces[0]] + [crossed(dsum_pieces[m], m, "feat") for m in range(1, feats)], axis=0
    ).reshape(shape)
    found = {0: dsum}
    for bit in bits[::-1]:
        for mask in sorted(found):
            found[mask ^ bit] = crossed(found[mask], bit)
    dpre = lax.all_gather(dpre_rows, "feat", axis=0, tiled=True)
    out_pieces, _ = lax.optimization_barrier((out_pieces, (found[1], found[2])))
    out_all = [out_pieces[0]] + [crossed(out_pieces[m], m, "feat") for m in range(1, feats)]
    (out,) = small_call(place_kernel, [like((feats, some, width), BF16)], out_all)
    dpre, out, _ = lax.optimization_barrier((dpre, out, (found[3], found[4])))
    piece = 2 * width // parts_total
    dx_self, give, keep = small_call(
        functools.partial(grad_kernel, near, far),
        [
            like((rows, width), F32),
            like((len(far) + 1, piece, full), BF16),
            like((len(far) + 1, piece, full), F32),
        ],
        [features, agg.reshape(rows, width), dpre, w_self],
        [pltpu.VMEM((parts_total, piece, full), F32)],
        6 * rows * width * full,
    )
    keep = keep + crossed(give, near).astype(F32)
    keep, _ = lax.optimization_barrier((keep, found[6]))
    total = keep[len(far)]
    for at, mask in enumerate(far):
        total = total + crossed(keep[at].astype(BF16), mask).astype(F32)
    total, _ = lax.optimization_barrier((total.astype(BF16), found[5]))
    totals = [crossed(total, mask) for mask in far] + [total]
    grad_self, grad_neigh = small_call(
        functools.partial(finish_kernel, near, far),
        [like((width, full), F32)] * 2,
        [*totals, crossed(jnp.stack(totals), near)],
        [pltpu.VMEM((parts_total, piece, full), F32)],
    )
    grad_x = dx_self.reshape(shape)
    half = parts_total // 2
    for order in (list(range(half)), list(range(half, parts_total))):
        grad_x = tiles_call(
            order,
            offsets,
            parts_total,
            True,
            feats,
            fixed,
            [found[mask] for mask in order] + [grad_x],
            like(shape, F32),
            24,
        )
    return (out.reshape(rows, width), grad_x.reshape(rows, width), grad_self, grad_neigh)


def solution(mesh):
    def body(*args):
        rounds = args[7].shape[1]
        parts_total = mesh.shape["dom"]
        powers = all(n & (n - 1) == 0 for n in mesh.shape.values())
        nearly_all = parts_total <= rounds + 2 and powers
        return (dense_body if nearly_all else sparse_body)(*args)

    placed = (
        P("dom", "feat"),
        P("feat", None),
        P("feat", None),
        P("dom"),
        P("dom", None, None, None),
        P("dom", None),
        P("dom", None),
        P("dom", None, None, None, None),
        P("dom", None, None),
        P("dom", None, None),
        P("dom", "feat"),
    )
    return jax.shard_map(
        body,
        mesh=mesh,
        in_specs=placed,
        out_specs=(P("dom", "feat"), P("dom", "feat"), P("feat", None), P("feat", None)),
        check_vma=False,
    )
```

```python
import functools

import jax
import jax.numpy as jnp
from jax import lax
from jax.experimental import pallas as pl
from jax.experimental.pallas import tpu as pltpu
from jax.sharding import PartitionSpec as P

F32 = jnp.float32
BF16 = jnp.bfloat16
VMEM = pl.BlockSpec(memory_space=pltpu.VMEM)
SMEM = pl.BlockSpec(memory_space=pltpu.SMEM)


def shifted(x, axis, by):
    devices = lax.axis_size(axis)
    return lax.ppermute(x, axis, [(i, (i + by) % devices) for i in range(devices)])


def spread(parts, block_ids, count):
    table = (block_ids[:, None] == jnp.arange(count, dtype=jnp.int32)[None, :]).astype(F32)
    return jnp.einsum("kc,kif->cif", table, parts, precision=lax.Precision.HIGHEST)


def tile_apply(tiles, blocks):
    return jnp.einsum("kij,kjf->kif", tiles, blocks, preferred_element_type=F32)


def tile_apply_back(tiles, blocks):
    return jnp.einsum("kji,kjf->kif", tiles, blocks, preferred_element_type=F32)


def round_offsets(parts_total, rounds):
    return [(step + 1) * parts_total // (rounds + 1) for step in range(rounds)]


def sparse_body(
    features,
    w_self,
    w_neigh,
    degree,
    local_vals,
    local_dst,
    local_src,
    remote_vals,
    remote_dst,
    remote_src,
    cotangent,
):
    rows, width = features.shape
    block = local_vals.shape[-1]
    nblocks = rows // block
    rounds = remote_vals.shape[1]
    parts_total = lax.axis_size("dom")
    offsets = round_offsets(parts_total, rounds)
    blocks = features.reshape(nblocks, block, width)
    totals = spread(
        tile_apply(local_vals[0], jnp.take(blocks, local_src[0], axis=0)), local_dst[0], nblocks
    )
    arrived_ids = []
    for step in range(rounds):
        partial_blocks = tile_apply(
            remote_vals[0, step], jnp.take(blocks, remote_src[0, step], axis=0)
        ).astype(BF16)
        arrived, block_ids = shifted((partial_blocks, remote_dst[0, step]), "dom", offsets[step])
        arrived_ids.append(block_ids)
        totals = totals + spread(arrived.astype(F32), block_ids, nblocks)
    inverse = 1.0 / degree.astype(F32)
    agg = (totals.reshape(rows, width) * inverse[:, None]).astype(BF16)
    stacked = jnp.concatenate([features, agg], axis=1)
    weights = jnp.concatenate([w_self, w_neigh], axis=0)
    pre = lax.psum_scatter(
        lax.dot_general(weights, stacked, (((0,), (1,)), ((), ())), preferred_element_type=F32),
        "feat",
        scatter_dimension=0,
        tiled=True,
    ).T
    sigma = jax.nn.sigmoid(pre)
    out = (pre * sigma).astype(BF16)
    dpre = (cotangent.astype(F32) * sigma * (1.0 + pre * (1.0 - sigma))).astype(BF16)
    dpre_all = lax.all_gather(dpre, "feat", axis=1, tiled=True)
    dz_total = lax.dot_general(
        dpre_all, weights, (((1,), (1,)), ((), ())), preferred_element_type=F32
    )
    grad_local = lax.dot_general(
        stacked, dpre_all, (((0,), (0,)), ((), ())), preferred_element_type=F32
    )
    dx_self = dz_total[:, :width]
    dsum = (dz_total[:, width:] * inverse[:, None]).astype(BF16).reshape(nblocks, block, width)
    grad_all = lax.psum(grad_local, "dom")
    back = spread(
        tile_apply_back(local_vals[0], jnp.take(dsum, local_dst[0], axis=0)), local_src[0], nblocks
    )
    for step in range(rounds):
        picked = jnp.take(dsum, arrived_ids[step], axis=0)
        returned = shifted(picked, "dom", parts_total - offsets[step])
        back = back + spread(
            tile_apply_back(remote_vals[0, step], returned), remote_src[0, step], nblocks
        )
    grad_x = dx_self + back.reshape(rows, width)
    return (out, grad_x, grad_all[:width], grad_all[width:])


def tile_counts(rvals, lvals):
    return rvals.shape[0], rvals.shape[1], lvals.shape[0]


def round_of(offset, offsets):
    step, known = jnp.int32(0), offset < 0
    for at, this in enumerate(offsets):
        step = jnp.where(offset == this, at, step)
        known = known | (offset == this)
    return step, known


def crossed_block(block_id, mine, per_feat):
    return ((block_id // per_feat) ^ mine) * per_feat + block_id % per_feat


def tile_groups(masks, offsets, parts_total, me, groups, tiles, ids):
    ldst, lsrc, rdst, rsrc = ids
    jobs = []
    for at, mask in enumerate(masks):
        if mask == 0:
            for first in range(0, tiles, groups):
                count = min(groups, tiles - first)
                dst = [ldst[0, first + k] for k in range(count)]
                src = [lsrc[0, first + k] for k in range(count)]
                jobs.append((at, None, None, first, dst, src))
        else:
            offset = lax.rem((me ^ mask) - me + parts_total, parts_total)
            step, known = round_of(offset, offsets)
            dst = [rdst[step, 0, k] for k in range(groups)]
            src = [rsrc[step, 0, k] for k in range(groups)]
            jobs.append((at, step, known, None, dst, src))
    return jobs


def flat(masks):
    return [m for group in masks for m in (group if isinstance(group, list) else [group])]


def tiles_kernel(masks, offsets, parts_total, back, feats, extras, *refs):
    ids, (lvals, rvals), refs = refs[:4], refs[4:6], refs[6:]
    groups_of, masks = masks, flat(masks)
    me = lax.axis_index("dom")
    mine = lax.axis_index("feat")
    rounds, groups, tiles = tile_counts(rvals, lvals)
    jobs = tile_groups(masks, offsets, parts_total, me, groups, tiles, ids)
    held, prod, acc, sems = refs[-4:]
    copies = []
    for slot, (at, step, known, first, dst, src) in enumerate(jobs):
        source = lvals.at[pl.ds(first, len(dst))] if step is None else rvals.at[step]
        copy = pltpu.make_async_copy(source, held.at[slot, pl.ds(0, len(dst))], sems.at[slot])
        copy.start()
        copies.append(copy)
    if back:
        own_ref, grad_ref = refs[len(masks)], refs[len(masks) + 1]
        blocks = refs[: len(masks)]
        sinks = [grad_ref] * len(masks)
        acc[0] = own_ref[...]
    else:
        blocks = [refs[0]] * len(masks)
        sinks, used = [], 1 + extras
        for group in groups_of:
            if isinstance(group, list):
                sinks += [refs[used].at[n] for n in range(len(group))]
            else:
                sinks.append(refs[used])
            used += 1
    if extras:
        pieces, pair = refs[used : used + feats], refs[used + feats]
        pair[0] = refs[2][...]
        pair[1] = refs[3][...]
        for mask, piece in enumerate(pieces):
            rows = pl.ds((mine ^ mask) * piece.shape[1], piece.shape[1])
            piece[0] = refs[0][rows]
            piece[1] = refs[1][rows]
    total = 0
    for slot, (at, step, known, first, dst, src) in enumerate(jobs):
        copies[slot].wait()
        half = slot % 2
        for k in range(len(dst)):
            if back:
                per_feat = blocks[at].shape[0] // feats
                block = blocks[at][crossed_block(dst[k], mine, per_feat)]
                product = lax.dot_general(
                    held[slot, k], block, (((0,), (0,)), ((), ())), preferred_element_type=F32
                )
            else:
                product = jnp.dot(
                    held[slot, k], blocks[at][src[k]], preferred_element_type=F32
                )
            prod[half, k] = product if known is None else jnp.where(known, product, 0.0)
        fresh = not back and (slot == 0 or jobs[slot - 1][0] != at)
        if fresh:
            total = at % 2
            acc[total] = jnp.zeros(acc.shape[1:], F32)
        for k in range(len(dst)):
            into = src[k] if back else dst[k]
            acc[total, into] = acc[total, into] + prod[half, k]
        last = slot == len(jobs) - 1 or jobs[slot + 1][0] != at
        if last and (not back or slot == len(jobs) - 1):
            sinks[at][...] = acc[total].astype(sinks[at].dtype)


def tiles_call(masks, offsets, parts_total, back, feats, fixed, blocks, sinks, room):
    ids, lvals, rvals = fixed
    rounds, groups, tiles = tile_counts(rvals, lvals)
    nblocks, block, width = blocks[0].shape
    slots = sum(-(-tiles // groups) if mask == 0 else 1 for mask in flat(masks))
    flops = 2 * slots * groups * block * block * width
    extras = 0 if back else len(blocks) - 1
    return pl.pallas_call(
        functools.partial(tiles_kernel, masks, offsets, parts_total, back, feats, extras),
        out_shape=sinks,
        in_specs=[SMEM] * 4
        + [pl.BlockSpec(memory_space=pltpu.HBM)] * 2
        + [VMEM] * len(blocks),
        out_specs=jax.tree.map(lambda _: VMEM, sinks),
        scratch_shapes=[
            pltpu.VMEM((slots, groups, block, block), BF16),
            pltpu.VMEM((2, groups, block, width), F32),
            pltpu.VMEM((2, nblocks, block, width), F32),
            pltpu.SemaphoreType.DMA((slots,)),
        ],
        compiler_params=pltpu.CompilerParams(vmem_limit_bytes=room * 2**20),
        cost_estimate=pl.CostEstimate(
            flops=4 * flops,
            bytes_accessed=slots * groups * block * block * 2 + 4 * rounds * nblocks * block * width,
            transcendentals=0,
        ),
    )(*ids, lvals, rvals, *blocks)


def small_call(kernel, outs, arrays, scratch=(), flops=10**6):
    size = sum(t.size * t.dtype.itemsize for t in list(arrays) + list(outs))
    return pl.pallas_call(
        kernel,
        out_shape=outs,
        in_specs=[VMEM] * len(arrays),
        out_specs=[VMEM] * len(outs),
        scratch_shapes=scratch,
        compiler_params=pltpu.CompilerParams(vmem_limit_bytes=24 * 2**20),
        cost_estimate=pl.CostEstimate(flops=flops, bytes_accessed=size, transcendentals=0),
    )(*arrays)


def agg_kernel(feats, inv_ref, keep_ref, *refs):
    mine = lax.axis_index("feat")
    far_refs, agg_ref, piece_refs = refs[: -1 - feats], refs[-1 - feats], refs[-feats:]
    per_feat = piece_refs[0].shape[0]
    sums = keep_ref[...]
    for ref in far_refs:
        sums = sums + ref[...].astype(F32)
    agg_ref[...] = (sums * inv_ref[...]).astype(BF16)
    for mask, piece in enumerate(piece_refs):
        piece[...] = agg_ref[pl.ds((mine ^ mask) * per_feat, per_feat)]


def joined(parts):
    return jnp.concatenate(parts, axis=1)


def dense_kernel(feats, inv_ref, *refs):
    mine = lax.axis_index("feat")
    w_refs, early_refs, a_refs = refs[:feats], refs[feats : 2 * feats], refs[2 * feats : 3 * feats]
    dpre_ref = refs[3 * feats]
    dsum_refs, out_refs = refs[3 * feats + 1 : 4 * feats + 1], refs[4 * feats + 1 : 5 * feats + 1]
    held = refs[-1]
    full = w_refs[0].shape[2]
    some, width = held.shape[1:]
    pre = jnp.zeros((some, full), F32)
    for mask in range(feats):
        early = early_refs[mask]
        pre = pre + jnp.dot(
            early[0].reshape(some, width), w_refs[mask][0], preferred_element_type=F32
        )
        pre = pre + jnp.dot(
            a_refs[mask][...].reshape(some, width), w_refs[mask][1], preferred_element_type=F32
        )
        held[mine ^ mask] = early[1].reshape(some, width)
    sigma = 1.0 / (1.0 + jnp.exp(-pre))
    out = (pre * sigma).astype(BF16)
    cot = joined([held[j] for j in range(feats)]).astype(F32)
    dpre = (cot * sigma * (1.0 + pre * (1.0 - sigma))).astype(BF16)
    dpre_ref[...] = dpre
    for mask in range(feats):
        dagg = lax.dot_general(
            dpre, w_refs[mask][1], (((1,), (1,)), ((), ())), preferred_element_type=F32
        )
        dsum_refs[mask][...] = (dagg * inv_ref[...]).astype(BF16)
    for j in range(feats):
        held[j] = out[:, j * width : (j + 1) * width]
    for mask in range(feats):
        out_refs[mask][...] = held[mine ^ mask]


def grad_kernel(near, far, feats, f_ref, a_ref, w_ref, *refs):
    me = lax.axis_index("dom")
    mine = lax.axis_index("feat")
    dpre_refs, (dx_ref, give_ref, keep_ref, held) = refs[:feats], refs[feats:]
    width = f_ref.shape[1]
    piece = held.shape[1]
    some = dpre_refs[0].shape[0]
    parts = [0.0, 0.0]
    for mask, dpre_ref in enumerate(dpre_refs):
        dpre = dpre_ref[...]
        rows = pl.ds(pl.multiple_of((mine ^ mask) * some, some), some)
        for at, ref in enumerate((f_ref, a_ref)):
            parts[at] = parts[at] + lax.dot_general(
                ref[rows], dpre, (((0,), (0,)), ((), ())), preferred_element_type=F32
            )
        dx_ref[rows] = lax.dot_general(
            dpre, w_ref[...], (((1,), (1,)), ((), ())), preferred_element_type=F32
        )
    for at, part in enumerate(parts):
        for j in range(width // piece):
            held[at * (width // piece) + j] = part[j * piece : (j + 1) * piece]
    for at, mask in enumerate(far + [0]):
        give_ref[at] = held[me ^ mask ^ near].astype(BF16)
        keep_ref[at] = held[me ^ mask]


def finish_kernel(near, far, *refs):
    me = lax.axis_index("dom")
    count = len(far) + 1
    found, other_ref = refs[:count], refs[count]
    self_ref, neigh_ref, held = refs[count + 1 :]
    for at, mask in enumerate(far + [0]):
        held[me ^ mask] = found[at][...].astype(F32)
        held[me ^ mask ^ near] = other_ref[at].astype(F32)
    some = held.shape[1]
    half = held.shape[0] // 2
    for j in range(half):
        self_ref[j * some : (j + 1) * some] = held[j]
        neigh_ref[j * some : (j + 1) * some] = held[half + j]


def place_kernel(*refs):
    mine = lax.axis_index("feat")
    out_ref = refs[-1]
    for mask, ref in enumerate(refs[:-1]):
        out_ref[mine ^ mask] = ref[...]


def swap_feat(x):
    return lax.all_to_all(x, "feat", split_axis=0, concat_axis=0, tiled=True)


def crossed(x, mask, axis="dom"):
    return lax.ppermute(x, axis, [(i, i ^ mask) for i in range(lax.axis_size(axis))])


def like(shape, dtype):
    return jax.ShapeDtypeStruct(shape, dtype)


def dense_body(
    features,
    w_self,
    w_neigh,
    degree,
    local_vals,
    local_dst,
    local_src,
    remote_vals,
    remote_dst,
    remote_src,
    cotangent,
):
    rows, width = features.shape
    block = local_vals.shape[-1]
    nblocks = rows // block
    rounds = remote_vals.shape[1]
    parts_total = lax.axis_size("dom")
    feats = lax.axis_size("feat")
    some = rows // feats
    per_feat = nblocks // feats
    full = feats * width
    offsets = round_offsets(parts_total, rounds)
    near, far = 1, list(range(parts_total - 2, 0, -2))
    bits = [1, 2, 4]
    mine = lax.axis_index("feat").astype(jnp.int32)
    inverse = 1.0 / degree.astype(F32)
    inv_rows = lax.dynamic_slice(inverse, (mine * some,), (some,))[:, None]
    ids = (
        local_dst,
        local_src,
        jnp.swapaxes(remote_dst, 0, 1),
        jnp.swapaxes(remote_src, 0, 1),
    )
    shape = (nblocks, block, width)
    blocks = features.reshape(shape)
    fixed = (ids, local_vals[0], remote_vals[0])

    def forward(masks, arrays, sinks):
        return tiles_call(
            masks, offsets, parts_total, False, feats, fixed, arrays, sinks, 62
        )

    def relayed(x):
        over = crossed(x, 2, "feat")
        return [x, crossed(x, 1, "feat"), over, crossed(over, 1, "feat")]

    def tied(x, *others):
        return lax.optimization_barrier((x, others))[0]

    send_7, sends, send_1, *made = forward(
        [7, [5, 3], 1],
        [blocks, cotangent.reshape(shape), w_self, w_neigh],
        [like(shape, BF16), like((2, *shape), BF16), like(shape, BF16)]
        + [like((2, per_feat, block, width), BF16)] * feats
        + [like((2, width, full), BF16)],
    )
    early_pieces, pair = made[:-1], made[-1]
    keep_6, keep_4 = forward([6, 4], [blocks], [like(shape, F32)] * 2)
    weights = relayed(pair)
    early = [early_pieces[0]] + [crossed(early_pieces[m], m, "feat") for m in range(1, feats)]
    near_6, near_53, near_0 = (crossed(send, near) for send in (send_7, sends, send_1))
    sum_6 = (keep_6 + tied(near_6, weights[2]).astype(F32)).astype(BF16)
    keep_2, keep = forward([2, 0], [tied(blocks, sum_6)], [like(shape, F32)] * 2)
    near_53 = tied(near_53, early)
    sum_4 = (keep_4 + near_53[0].astype(F32) + crossed(sum_6, 2).astype(F32)).astype(BF16)
    far_0 = crossed(sum_4, 4)
    sum_2 = (tied(keep_2, sum_4) + near_53[1].astype(F32)).astype(BF16)
    mid_0 = crossed(sum_2, 2)
    arrived = [near_0, mid_0, far_0]
    early, weights, arrived = lax.optimization_barrier((early, weights, arrived))
    agg, *agg_pieces = small_call(
        functools.partial(agg_kernel, feats),
        [like(shape, BF16)] + [like((per_feat, block, width), BF16)] * feats,
        [inverse.reshape(nblocks, block, 1), keep, *arrived],
    )
    agg_rows = [agg_pieces[0]] + [crossed(agg_pieces[m], m, "feat") for m in range(1, feats)]
    dpre_rows, *pieces = small_call(
        functools.partial(dense_kernel, feats),
        [like((some, full), BF16)] + [like((some, width), BF16)] * (2 * feats),
        [inv_rows, *weights, *early, *agg_rows],
        [pltpu.VMEM((feats, some, width), BF16)],
        6 * some * full * full,
    )
    dsum_pieces, out_pieces = pieces[:feats], pieces[feats:]
    dsum = jnp.concatenate(
        [dsum_pieces[0]] + [crossed(dsum_pieces[m], m, "feat") for m in range(1, feats)], axis=0
    ).reshape(shape)
    found = {0: dsum}
    for bit in bits[::-1]:
        for mask in sorted(found):
            found[mask ^ bit] = crossed(found[mask], bit)
    dpre = relayed(dpre_rows)
    dpre = tied(dpre, found[1], found[2])
    piece = 2 * width // parts_total
    dx_self, give, keep = small_call(
        functools.partial(grad_kernel, near, far, feats),
        [
            like((rows, width), F32),
            like((len(far) + 1, piece, full), BF16),
            like((len(far) + 1, piece, full), F32),
        ],
        [features, agg.reshape(rows, width), w_self, *dpre],
        [pltpu.VMEM((parts_total, piece, full), F32)],
        6 * rows * width * full,
    )
    out_pieces = tied(out_pieces, give)
    out_all = [out_pieces[0]] + [crossed(out_pieces[m], m, "feat") for m in range(1, feats)]
    (out,) = small_call(place_kernel, [like((feats, some, width), BF16)], out_all)
    keep = keep + crossed(give, near).astype(F32)
    keep = tied(keep, found[3], found[4])
    total = keep[len(far)]
    for at, mask in enumerate(far):
        total = total + crossed(keep[at].astype(BF16), mask).astype(F32)
    total, out = tied((total.astype(BF16), out), found[5], found[6])
    totals = [crossed(total, mask) for mask in far] + [total]
    grad_self, grad_neigh = small_call(
        functools.partial(finish_kernel, near, far),
        [like((width, full), F32)] * 2,
        [*totals, crossed(jnp.stack(totals), near)],
        [pltpu.VMEM((parts_total, piece, full), F32)],
    )
    grad_x = dx_self.reshape(shape)
    half = parts_total // 2
    for order in (list(range(half)), list(range(half, parts_total))):
        grad_x = tiles_call(
            order,
            offsets,
            parts_total,
            True,
            feats,
            fixed,
            [found[mask] for mask in order] + [grad_x],
            like(shape, F32),
            24,
        )
    return (out.reshape(rows, width), grad_x.reshape(rows, width), grad_self, grad_neigh)


def solution(mesh):
    def body(*args):
        rounds = args[7].shape[1]
        small = mesh.shape["dom"] == 8 and mesh.shape["feat"] == 4
        nearly_all = mesh.shape["dom"] <= rounds + 2
        return (dense_body if small and nearly_all else sparse_body)(*args)

    placed = (
        P("dom", "feat"),
        P("feat", None),
        P("feat", None),
        P("dom"),
        P("dom", None, None, None),
        P("dom", None),
        P("dom", None),
        P("dom", None, None, None, None),
        P("dom", None, None),
        P("dom", None, None),
        P("dom", "feat"),
    )
    return jax.shard_map(
        body,
        mesh=mesh,
        in_specs=placed,
        out_specs=(P("dom", "feat"), P("dom", "feat"), P("feat", None), P("feat", None)),
        check_vma=False,
    )
```

```python
import functools

import jax
import jax.numpy as jnp
from jax import lax
from jax.experimental import pallas as pl
from jax.experimental.pallas import tpu as pltpu
from jax.sharding import PartitionSpec as P

F32 = jnp.float32
BF16 = jnp.bfloat16
VMEM = pl.BlockSpec(memory_space=pltpu.VMEM)
SMEM = pl.BlockSpec(memory_space=pltpu.SMEM)


def shifted(x, axis, by):
    devices = lax.axis_size(axis)
    return lax.ppermute(x, axis, [(i, (i + by) % devices) for i in range(devices)])


def spread(parts, block_ids, count):
    table = (block_ids[:, None] == jnp.arange(count, dtype=jnp.int32)[None, :]).astype(F32)
    return jnp.einsum("kc,kif->cif", table, parts, precision=lax.Precision.HIGHEST)


def tile_apply(tiles, blocks):
    return jnp.einsum("kij,kjf->kif", tiles, blocks, preferred_element_type=F32)


def tile_apply_back(tiles, blocks):
    return jnp.einsum("kji,kjf->kif", tiles, blocks, preferred_element_type=F32)


def round_offsets(parts_total, rounds):
    return [(step + 1) * parts_total // (rounds + 1) for step in range(rounds)]


def sparse_body(
    features,
    w_self,
    w_neigh,
    degree,
    local_vals,
    local_dst,
    local_src,
    remote_vals,
    remote_dst,
    remote_src,
    cotangent,
):
    rows, width = features.shape
    block = local_vals.shape[-1]
    nblocks = rows // block
    rounds = remote_vals.shape[1]
    parts_total = lax.axis_size("dom")
    offsets = round_offsets(parts_total, rounds)
    blocks = features.reshape(nblocks, block, width)
    totals = spread(
        tile_apply(local_vals[0], jnp.take(blocks, local_src[0], axis=0)), local_dst[0], nblocks
    )
    arrived_ids = []
    for step in range(rounds):
        partial_blocks = tile_apply(
            remote_vals[0, step], jnp.take(blocks, remote_src[0, step], axis=0)
        ).astype(BF16)
        arrived, block_ids = shifted((partial_blocks, remote_dst[0, step]), "dom", offsets[step])
        arrived_ids.append(block_ids)
        totals = totals + spread(arrived.astype(F32), block_ids, nblocks)
    inverse = 1.0 / degree.astype(F32)
    agg = (totals.reshape(rows, width) * inverse[:, None]).astype(BF16)
    stacked = jnp.concatenate([features, agg], axis=1)
    weights = jnp.concatenate([w_self, w_neigh], axis=0)
    pre = lax.psum_scatter(
        lax.dot_general(weights, stacked, (((0,), (1,)), ((), ())), preferred_element_type=F32),
        "feat",
        scatter_dimension=0,
        tiled=True,
    ).T
    sigma = jax.nn.sigmoid(pre)
    out = (pre * sigma).astype(BF16)
    dpre = (cotangent.astype(F32) * sigma * (1.0 + pre * (1.0 - sigma))).astype(BF16)
    dpre_all = lax.all_gather(dpre, "feat", axis=1, tiled=True)
    dz_total = lax.dot_general(
        dpre_all, weights, (((1,), (1,)), ((), ())), preferred_element_type=F32
    )
    grad_local = lax.dot_general(
        stacked, dpre_all, (((0,), (0,)), ((), ())), preferred_element_type=F32
    )
    dx_self = dz_total[:, :width]
    dsum = (dz_total[:, width:] * inverse[:, None]).astype(BF16).reshape(nblocks, block, width)
    grad_all = lax.psum(grad_local, "dom")
    back = spread(
        tile_apply_back(local_vals[0], jnp.take(dsum, local_dst[0], axis=0)), local_src[0], nblocks
    )
    for step in range(rounds):
        picked = jnp.take(dsum, arrived_ids[step], axis=0)
        returned = shifted(picked, "dom", parts_total - offsets[step])
        back = back + spread(
            tile_apply_back(remote_vals[0, step], returned), remote_src[0, step], nblocks
        )
    grad_x = dx_self + back.reshape(rows, width)
    return (out, grad_x, grad_all[:width], grad_all[width:])


def tile_counts(rvals, lvals):
    return rvals.shape[0], rvals.shape[1], lvals.shape[0]


def round_of(offset, offsets):
    step, known = jnp.int32(0), offset < 0
    for at, this in enumerate(offsets):
        step = jnp.where(offset == this, at, step)
        known = known | (offset == this)
    return step, known


def crossed_block(block_id, mine, per_feat):
    return ((block_id // per_feat) ^ mine) * per_feat + block_id % per_feat


def tile_groups(masks, offsets, parts_total, me, groups, tiles, ids):
    ldst, lsrc, rdst, rsrc = ids
    jobs = []
    for at, mask in enumerate(masks):
        if mask == 0:
            for first in range(0, tiles, groups):
                count = min(groups, tiles - first)
                dst = [ldst[0, first + k] for k in range(count)]
                src = [lsrc[0, first + k] for k in range(count)]
                jobs.append((at, None, None, first, dst, src))
        else:
            offset = lax.rem((me ^ mask) - me + parts_total, parts_total)
            step, known = round_of(offset, offsets)
            dst = [rdst[step, 0, k] for k in range(groups)]
            src = [rsrc[step, 0, k] for k in range(groups)]
            jobs.append((at, step, known, None, dst, src))
    return jobs


def flat(masks):
    return [m for group in masks for m in (group if isinstance(group, list) else [group])]


def tiles_kernel(masks, offsets, parts_total, back, feats, extras, *refs):
    ids, (lvals, rvals), refs = refs[:4], refs[4:6], refs[6:]
    groups_of, masks = masks, flat(masks)
    me = lax.axis_index("dom")
    mine = lax.axis_index("feat")
    rounds, groups, tiles = tile_counts(rvals, lvals)
    jobs = tile_groups(masks, offsets, parts_total, me, groups, tiles, ids)
    held, prod, acc, sems = refs[-4:]
    copies = []
    for slot, (at, step, known, first, dst, src) in enumerate(jobs):
        source = lvals.at[pl.ds(first, len(dst))] if step is None else rvals.at[step]
        copy = pltpu.make_async_copy(source, held.at[slot, pl.ds(0, len(dst))], sems.at[slot])
        copy.start()
        copies.append(copy)
    if back:
        own_ref, grad_ref = refs[len(masks)], refs[len(masks) + 1]
        blocks = refs[: len(masks)]
        sinks = [grad_ref] * len(masks)
        acc[0] = own_ref[...]
    else:
        blocks = [refs[0]] * len(masks)
        sinks, used = [], 1 + extras
        for group in groups_of:
            if isinstance(group, list):
                sinks += [refs[used].at[n] for n in range(len(group))]
            else:
                sinks.append(refs[used])
            used += 1
    if extras:
        pieces, pair = refs[used : used + feats], refs[used + feats]
        pair[0] = refs[2][...]
        pair[1] = refs[3][...]
        for mask, piece in enumerate(pieces):
            rows = pl.ds((mine ^ mask) * piece.shape[1], piece.shape[1])
            piece[0] = refs[0][rows]
            piece[1] = refs[1][rows]
    total = 0
    for slot, (at, step, known, first, dst, src) in enumerate(jobs):
        copies[slot].wait()
        half = slot % 2
        for k in range(len(dst)):
            if back:
                per_feat = blocks[at].shape[0] // feats
                block = blocks[at][crossed_block(dst[k], mine, per_feat)]
                product = lax.dot_general(
                    held[slot, k], block, (((0,), (0,)), ((), ())), preferred_element_type=F32
                )
            else:
                product = jnp.dot(
                    held[slot, k], blocks[at][src[k]], preferred_element_type=F32
                )
            prod[half, k] = product if known is None else jnp.where(known, product, 0.0)
        fresh = not back and (slot == 0 or jobs[slot - 1][0] != at)
        if fresh:
            total = at % 2
            acc[total] = jnp.zeros(acc.shape[1:], F32)
        for k in range(len(dst)):
            into = src[k] if back else dst[k]
            acc[total, into] = acc[total, into] + prod[half, k]
        last = slot == len(jobs) - 1 or jobs[slot + 1][0] != at
        if last and (not back or slot == len(jobs) - 1):
            sinks[at][...] = acc[total].astype(sinks[at].dtype)


def tiles_call(masks, offsets, parts_total, back, feats, fixed, blocks, sinks, room):
    ids, lvals, rvals = fixed
    rounds, groups, tiles = tile_counts(rvals, lvals)
    nblocks, block, width = blocks[0].shape
    slots = sum(-(-tiles // groups) if mask == 0 else 1 for mask in flat(masks))
    flops = 2 * slots * groups * block * block * width
    extras = 0 if back else len(blocks) - 1
    return pl.pallas_call(
        functools.partial(tiles_kernel, masks, offsets, parts_total, back, feats, extras),
        out_shape=sinks,
        in_specs=[SMEM] * 4
        + [pl.BlockSpec(memory_space=pltpu.HBM)] * 2
        + [VMEM] * len(blocks),
        out_specs=jax.tree.map(lambda _: VMEM, sinks),
        scratch_shapes=[
            pltpu.VMEM((slots, groups, block, block), BF16),
            pltpu.VMEM((2, groups, block, width), F32),
            pltpu.VMEM((2, nblocks, block, width), F32),
            pltpu.SemaphoreType.DMA((slots,)),
        ],
        compiler_params=pltpu.CompilerParams(vmem_limit_bytes=room * 2**20),
        cost_estimate=pl.CostEstimate(
            flops=4 * flops,
            bytes_accessed=slots * groups * block * block * 2 + 4 * rounds * nblocks * block * width,
            transcendentals=0,
        ),
    )(*ids, lvals, rvals, *blocks)


def small_call(kernel, outs, arrays, scratch=(), flops=10**6):
    size = sum(t.size * t.dtype.itemsize for t in list(arrays) + list(outs))
    return pl.pallas_call(
        kernel,
        out_shape=outs,
        in_specs=[VMEM] * len(arrays),
        out_specs=[VMEM] * len(outs),
        scratch_shapes=scratch,
        compiler_params=pltpu.CompilerParams(vmem_limit_bytes=24 * 2**20),
        cost_estimate=pl.CostEstimate(flops=flops, bytes_accessed=size, transcendentals=0),
    )(*arrays)


def agg_kernel(feats, inv_ref, keep_ref, *refs):
    mine = lax.axis_index("feat")
    far_refs, agg_ref, piece_refs = refs[: -1 - feats], refs[-1 - feats], refs[-feats:]
    per_feat = piece_refs[0].shape[0]
    sums = keep_ref[...]
    for ref in far_refs:
        sums = sums + ref[...].astype(F32)
    agg_ref[...] = (sums * inv_ref[...]).astype(BF16)
    for mask, piece in enumerate(piece_refs):
        piece[...] = agg_ref[pl.ds((mine ^ mask) * per_feat, per_feat)]


def joined(parts):
    return jnp.concatenate(parts, axis=1)


def dense_kernel(feats, inv_ref, *refs):
    mine = lax.axis_index("feat")
    w_refs, early_refs, a_refs = refs[:feats], refs[feats : 2 * feats], refs[2 * feats : 3 * feats]
    core_ref, chip_ref, own_ref = refs[3 * feats : 3 * feats + 3]
    dsum_refs = refs[3 * feats + 3 : 4 * feats + 3]
    held = refs[-1]
    full = w_refs[0].shape[2]
    some, width = held.shape[1:]
    pre = jnp.zeros((some, full), F32)
    for mask in range(feats):
        early = early_refs[mask]
        pre = pre + jnp.dot(
            early[0].reshape(some, width), w_refs[mask][0], preferred_element_type=F32
        )
        pre = pre + jnp.dot(
            a_refs[mask][...].reshape(some, width), w_refs[mask][1], preferred_element_type=F32
        )
        held[mine ^ mask] = early[1].reshape(some, width)
    sigma = 1.0 / (1.0 + jnp.exp(-pre))
    out = (pre * sigma).astype(BF16)
    cot = joined([held[j] for j in range(feats)]).astype(F32)
    dpre = (cot * sigma * (1.0 + pre * (1.0 - sigma))).astype(BF16)
    for mask in range(feats):
        dagg = lax.dot_general(
            dpre, w_refs[mask][1], (((1,), (1,)), ((), ())), preferred_element_type=F32
        )
        dsum_refs[mask][...] = (dagg * inv_ref[...]).astype(BF16)
    for j in range(feats):
        cols = slice(j * width, (j + 1) * width)
        core_ref[j] = dpre[:, cols]
        chip_ref[j] = dpre[:, cols]
        held[j] = out[:, cols]
    own_ref[...] = held[mine]
    core_ref[feats] = held[mine ^ 1]
    chip_ref[feats] = held[mine ^ 2]
    chip_ref[feats + 1] = held[mine ^ 3]


def grad_kernel(feats, f_ref, a_ref, w_ref, *refs):
    me = lax.axis_index("dom")
    mine = lax.axis_index("feat")
    dpre_refs, (dx_ref, give_ref, keep_ref, held) = refs[:feats], refs[feats:]
    width = f_ref.shape[1]
    piece = held.shape[1]
    some = dpre_refs[0].shape[1]
    parts = [0.0, 0.0]
    for mask, dpre_ref in enumerate(dpre_refs):
        dpre = joined([dpre_ref[j] for j in range(feats)])
        rows = pl.ds(pl.multiple_of((mine ^ mask) * some, some), some)
        for at, ref in enumerate((f_ref, a_ref)):
            parts[at] = parts[at] + lax.dot_general(
                ref[rows], dpre, (((0,), (0,)), ((), ())), preferred_element_type=F32
            )
        dx_ref[rows] = lax.dot_general(
            dpre, w_ref[...], (((1,), (1,)), ((), ())), preferred_element_type=F32
        )
    for at, part in enumerate(parts):
        for j in range(width // piece):
            held[at * (width // piece) + j] = part[j * piece : (j + 1) * piece]
    side = me % 2
    for at in range(give_ref.shape[0]):
        give_ref[at] = held[2 * at + 1 - side].astype(BF16)
        keep_ref[at] = held[2 * at + side]


def finish_kernel(mine_ref, other_ref, self_ref, neigh_ref, held):
    side = lax.axis_index("dom") % 2
    for at in range(mine_ref.shape[0]):
        held[2 * at + side] = mine_ref[at].astype(F32)
        held[2 * at + 1 - side] = other_ref[at].astype(F32)
    some = held.shape[1]
    half = held.shape[0] // 2
    for j in range(half):
        self_ref[j * some : (j + 1) * some] = held[j]
        neigh_ref[j * some : (j + 1) * some] = held[half + j]


def place_kernel(*refs):
    mine = lax.axis_index("feat")
    own_ref, core_ref, chip_ref, both_ref, out_ref = refs
    feats = out_ref.shape[0]
    out_ref[mine] = own_ref[...]
    out_ref[mine ^ 1] = core_ref[feats]
    out_ref[mine ^ 2] = chip_ref[feats]
    out_ref[mine ^ 3] = both_ref[feats + 1]


def swap_feat(x):
    return lax.all_to_all(x, "feat", split_axis=0, concat_axis=0, tiled=True)


def crossed(x, mask, axis="dom"):
    return lax.ppermute(x, axis, [(i, i ^ mask) for i in range(lax.axis_size(axis))])


def like(shape, dtype):
    return jax.ShapeDtypeStruct(shape, dtype)


def dense_body(
    features,
    w_self,
    w_neigh,
    degree,
    local_vals,
    local_dst,
    local_src,
    remote_vals,
    remote_dst,
    remote_src,
    cotangent,
):
    rows, width = features.shape
    block = local_vals.shape[-1]
    nblocks = rows // block
    rounds = remote_vals.shape[1]
    parts_total = lax.axis_size("dom")
    feats = lax.axis_size("feat")
    some = rows // feats
    per_feat = nblocks // feats
    full = feats * width
    offsets = round_offsets(parts_total, rounds)
    near, far = 1, list(range(parts_total - 2, 0, -2))
    bits = [1, 2, 4]
    mine = lax.axis_index("feat").astype(jnp.int32)
    inverse = 1.0 / degree.astype(F32)
    inv_rows = lax.dynamic_slice(inverse, (mine * some,), (some,))[:, None]
    ids = (
        local_dst,
        local_src,
        jnp.swapaxes(remote_dst, 0, 1),
        jnp.swapaxes(remote_src, 0, 1),
    )
    shape = (nblocks, block, width)
    blocks = features.reshape(shape)
    fixed = (ids, local_vals[0], remote_vals[0])

    def forward(masks, arrays, sinks):
        return tiles_call(
            masks, offsets, parts_total, False, feats, fixed, arrays, sinks, 62
        )

    def relayed(x):
        over = crossed(x, 2, "feat")
        return [x, crossed(x, 1, "feat"), over, crossed(over, 1, "feat")]

    def tied(x, *others):
        return lax.optimization_barrier((x, others))[0]

    made = forward(
        [7, 5, 3, 1],
        [blocks, cotangent.reshape(shape), w_self, w_neigh],
        [like(shape, BF16)] * 4
        + [like((2, per_feat, block, width), BF16)] * feats
        + [like((2, width, full), BF16)],
    )
    sends, early_pieces, pair = made[:4], made[4:-1], made[-1]
    keep_6, keep_4 = forward([6, 4], [blocks], [like(shape, F32)] * 2)
    weights = relayed(pair)
    early = [early_pieces[0]] + [crossed(early_pieces[m], m, "feat") for m in range(1, feats)]
    near_6, near_4, near_2, near_0 = (crossed(send, near) for send in sends)
    sum_6 = (keep_6 + near_6.astype(F32)).astype(BF16)
    near_4 = tied(near_4, weights[2])
    sum_4 = (keep_4 + near_4.astype(F32) + crossed(sum_6, 2).astype(F32)).astype(BF16)
    far_0 = crossed(sum_4, 4)
    keep_2, keep = forward([2, 0], [tied(blocks, sum_4)], [like(shape, F32)] * 2)
    sum_2 = tied((keep_2 + near_2.astype(F32)).astype(BF16), far_0)
    mid_0 = crossed(sum_2, 2)
    arrived = [near_0, mid_0, far_0]
    early, weights, arrived = lax.optimization_barrier((early, weights, arrived))
    agg, *agg_pieces = small_call(
        functools.partial(agg_kernel, feats),
        [like(shape, BF16)] + [like((per_feat, block, width), BF16)] * feats,
        [inverse.reshape(nblocks, block, 1), keep, *arrived],
    )
    agg_rows = [agg_pieces[0]] + [crossed(agg_pieces[m], m, "feat") for m in range(1, feats)]
    for_core, for_chip, own_out, *dsum_pieces = small_call(
        functools.partial(dense_kernel, feats),
        [like((feats + 1, some, width), BF16), like((feats + 2, some, width), BF16)]
        + [like((some, width), BF16)] * (1 + feats),
        [inv_rows, *weights, *early, *agg_rows],
        [pltpu.VMEM((feats, some, width), BF16)],
        6 * some * full * full,
    )
    dsum = jnp.concatenate(
        [dsum_pieces[0]] + [crossed(dsum_pieces[m], m, "feat") for m in range(1, feats)], axis=0
    ).reshape(shape)
    found = {0: dsum}
    for bit in bits[::-1]:
        for mask in sorted(found):
            found[mask ^ bit] = crossed(found[mask], bit)
    for_core, for_chip = tied((for_core, for_chip), dsum)
    from_chip = crossed(for_chip, 2, "feat")
    from_core = crossed(for_core, 1, "feat")
    from_both = crossed(tied(from_chip, found[1], found[2], found[4]), 1, "feat")
    (out,) = small_call(
        place_kernel,
        [like((feats, some, width), BF16)],
        [own_out, from_core, from_chip, from_both],
    )
    dpre = [for_core, from_core, from_chip, from_both]
    piece = 2 * width // parts_total
    dx_self, give, keep = small_call(
        functools.partial(grad_kernel, feats),
        [
            like((rows, width), F32),
            like((len(far) + 1, piece, full), BF16),
            like((len(far) + 1, piece, full), F32),
        ],
        [features, agg.reshape(rows, width), w_self, *dpre],
        [pltpu.VMEM((parts_total, piece, full), F32)],
        6 * rows * width * full,
    )
    total = (keep + crossed(give, near).astype(F32)).astype(BF16)
    total = tied(total, found[3], found[6])
    total = (total.astype(F32) + crossed(total, 2).astype(F32)).astype(BF16)
    total = tied(total, found[5])
    total = (total.astype(F32) + crossed(total, 4).astype(F32)).astype(BF16)
    total, out = tied((total, out), found[5])
    grad_self, grad_neigh = small_call(
        finish_kernel,
        [like((width, full), F32)] * 2,
        [total, crossed(total, near)],
        [pltpu.VMEM((parts_total, piece, full), F32)],
    )
    grad_x = dx_self.reshape(shape)
    half = parts_total // 2
    for order in (list(range(half)), list(range(half, parts_total))):
        grad_x = tiles_call(
            order,
            offsets,
            parts_total,
            True,
            feats,
            fixed,
            [found[mask] for mask in order] + [grad_x],
            like(shape, F32),
            24,
        )
    return (out.reshape(rows, width), grad_x.reshape(rows, width), grad_self, grad_neigh)


def solution(mesh):
    def body(*args):
        rounds = args[7].shape[1]
        small = mesh.shape["dom"] == 8 and mesh.shape["feat"] == 4
        nearly_all = mesh.shape["dom"] <= rounds + 2
        return (dense_body if small and nearly_all else sparse_body)(*args)

    placed = (
        P("dom", "feat"),
        P("feat", None),
        P("feat", None),
        P("dom"),
        P("dom", None, None, None),
        P("dom", None),
        P("dom", None),
        P("dom", None, None, None, None),
        P("dom", None, None),
        P("dom", None, None),
        P("dom", "feat"),
    )
    return jax.shard_map(
        body,
        mesh=mesh,
        in_specs=placed,
        out_specs=(P("dom", "feat"), P("dom", "feat"), P("feat", None), P("feat", None)),
        check_vma=False,
    )
```

```python
import functools

import jax
import jax.numpy as jnp
from jax import lax
from jax.experimental import pallas as pl
from jax.experimental.pallas import tpu as pltpu
from jax.sharding import PartitionSpec as P

F32 = jnp.float32
BF16 = jnp.bfloat16
VMEM = pl.BlockSpec(memory_space=pltpu.VMEM)
SMEM = pl.BlockSpec(memory_space=pltpu.SMEM)


def shifted(x, axis, by):
    devices = lax.axis_size(axis)
    return lax.ppermute(x, axis, [(i, (i + by) % devices) for i in range(devices)])


def spread(parts, block_ids, count):
    table = (block_ids[:, None] == jnp.arange(count, dtype=jnp.int32)[None, :]).astype(F32)
    return jnp.einsum("kc,kif->cif", table, parts, precision=lax.Precision.HIGHEST)


def tile_apply(tiles, blocks):
    return jnp.einsum("kij,kjf->kif", tiles, blocks, preferred_element_type=F32)


def tile_apply_back(tiles, blocks):
    return jnp.einsum("kji,kjf->kif", tiles, blocks, preferred_element_type=F32)


def round_offsets(parts_total, rounds):
    return [(step + 1) * parts_total // (rounds + 1) for step in range(rounds)]


def sparse_body(
    features,
    w_self,
    w_neigh,
    degree,
    local_vals,
    local_dst,
    local_src,
    remote_vals,
    remote_dst,
    remote_src,
    cotangent,
):
    rows, width = features.shape
    block = local_vals.shape[-1]
    nblocks = rows // block
    rounds = remote_vals.shape[1]
    parts_total = lax.axis_size("dom")
    offsets = round_offsets(parts_total, rounds)
    blocks = features.reshape(nblocks, block, width)
    totals = spread(
        tile_apply(local_vals[0], jnp.take(blocks, local_src[0], axis=0)), local_dst[0], nblocks
    )
    arrived_ids = []
    for step in range(rounds):
        partial_blocks = tile_apply(
            remote_vals[0, step], jnp.take(blocks, remote_src[0, step], axis=0)
        ).astype(BF16)
        arrived, block_ids = shifted((partial_blocks, remote_dst[0, step]), "dom", offsets[step])
        arrived_ids.append(block_ids)
        totals = totals + spread(arrived.astype(F32), block_ids, nblocks)
    inverse = 1.0 / degree.astype(F32)
    agg = (totals.reshape(rows, width) * inverse[:, None]).astype(BF16)
    stacked = jnp.concatenate([features, agg], axis=1)
    weights = jnp.concatenate([w_self, w_neigh], axis=0)
    pre = lax.psum_scatter(
        lax.dot_general(weights, stacked, (((0,), (1,)), ((), ())), preferred_element_type=F32),
        "feat",
        scatter_dimension=0,
        tiled=True,
    ).T
    sigma = jax.nn.sigmoid(pre)
    out = (pre * sigma).astype(BF16)
    dpre = (cotangent.astype(F32) * sigma * (1.0 + pre * (1.0 - sigma))).astype(BF16)
    dpre_all = lax.all_gather(dpre, "feat", axis=1, tiled=True)
    dz_total = lax.dot_general(
        dpre_all, weights, (((1,), (1,)), ((), ())), preferred_element_type=F32
    )
    grad_local = lax.dot_general(
        stacked, dpre_all, (((0,), (0,)), ((), ())), preferred_element_type=F32
    )
    dx_self = dz_total[:, :width]
    dsum = (dz_total[:, width:] * inverse[:, None]).astype(BF16).reshape(nblocks, block, width)
    grad_all = lax.psum(grad_local, "dom")
    back = spread(
        tile_apply_back(local_vals[0], jnp.take(dsum, local_dst[0], axis=0)), local_src[0], nblocks
    )
    for step in range(rounds):
        picked = jnp.take(dsum, arrived_ids[step], axis=0)
        returned = shifted(picked, "dom", parts_total - offsets[step])
        back = back + spread(
            tile_apply_back(remote_vals[0, step], returned), remote_src[0, step], nblocks
        )
    grad_x = dx_self + back.reshape(rows, width)
    return (out, grad_x, grad_all[:width], grad_all[width:])


def tile_counts(rvals, lvals):
    return rvals.shape[0], rvals.shape[1], lvals.shape[0]


def round_of(offset, offsets):
    step, known = jnp.int32(0), offset < 0
    for at, this in enumerate(offsets):
        step = jnp.where(offset == this, at, step)
        known = known | (offset == this)
    return step, known


def crossed_block(block_id, mine, per_feat):
    return ((block_id // per_feat) ^ mine) * per_feat + block_id % per_feat


def tile_groups(masks, offsets, parts_total, me, groups, tiles, ids):
    ldst, lsrc, rdst, rsrc = ids
    jobs = []
    for at, mask in enumerate(masks):
        if mask == 0:
            for first in range(0, tiles, groups):
                count = min(groups, tiles - first)
                dst = [ldst[0, first + k] for k in range(count)]
                src = [lsrc[0, first + k] for k in range(count)]
                jobs.append((at, None, None, first, dst, src))
        else:
            offset = lax.rem((me ^ mask) - me + parts_total, parts_total)
            step, known = round_of(offset, offsets)
            dst = [rdst[step, 0, k] for k in range(groups)]
            src = [rsrc[step, 0, k] for k in range(groups)]
            jobs.append((at, step, known, None, dst, src))
    return jobs


def flat(masks):
    return [m for group in masks for m in (group if isinstance(group, list) else [group])]


def tiles_kernel(masks, offsets, parts_total, back, feats, extras, *refs):
    ids, (lvals, rvals), refs = refs[:4], refs[4:6], refs[6:]
    groups_of, masks = masks, flat(masks)
    me = lax.axis_index("dom")
    mine = lax.axis_index("feat")
    rounds, groups, tiles = tile_counts(rvals, lvals)
    jobs = tile_groups(masks, offsets, parts_total, me, groups, tiles, ids)
    held, prod, acc, sems = refs[-4:]
    copies = []
    for slot, (at, step, known, first, dst, src) in enumerate(jobs):
        source = lvals.at[pl.ds(first, len(dst))] if step is None else rvals.at[step]
        copy = pltpu.make_async_copy(source, held.at[slot, pl.ds(0, len(dst))], sems.at[slot])
        copy.start()
        copies.append(copy)
    if back:
        own_ref, grad_ref = refs[len(masks)], refs[len(masks) + 1]
        blocks = refs[: len(masks)]
        sinks = [grad_ref] * len(masks)
        acc[0] = own_ref[...]
    else:
        blocks = [refs[0]] * len(masks)
        sinks, used = [], 1 + extras
        for group in groups_of:
            if isinstance(group, list):
                sinks += [refs[used].at[n] for n in range(len(group))]
            else:
                sinks.append(refs[used])
            used += 1
    if extras:
        pieces, pair = refs[used : used + feats], refs[used + feats]
        pair[0] = refs[2][...]
        pair[1] = refs[3][...]
        for mask, piece in enumerate(pieces):
            rows = pl.ds((mine ^ mask) * piece.shape[1], piece.shape[1])
            piece[0] = refs[0][rows]
            piece[1] = refs[1][rows]
    total = 0
    for slot, (at, step, known, first, dst, src) in enumerate(jobs):
        copies[slot].wait()
        half = slot % 2
        for k in range(len(dst)):
            if back:
                per_feat = blocks[at].shape[0] // feats
                block = blocks[at][crossed_block(dst[k], mine, per_feat)]
                product = lax.dot_general(
                    held[slot, k], block, (((0,), (0,)), ((), ())), preferred_element_type=F32
                )
            else:
                product = jnp.dot(
                    held[slot, k], blocks[at][src[k]], preferred_element_type=F32
                )
            prod[half, k] = product if known is None else jnp.where(known, product, 0.0)
        fresh = not back and (slot == 0 or jobs[slot - 1][0] != at)
        if fresh:
            total = at % 2
            acc[total] = jnp.zeros(acc.shape[1:], F32)
        for k in range(len(dst)):
            into = src[k] if back else dst[k]
            acc[total, into] = acc[total, into] + prod[half, k]
        last = slot == len(jobs) - 1 or jobs[slot + 1][0] != at
        if last and (not back or slot == len(jobs) - 1):
            sinks[at][...] = acc[total].astype(sinks[at].dtype)


def tiles_call(masks, offsets, parts_total, back, feats, fixed, blocks, sinks, room):
    ids, lvals, rvals = fixed
    rounds, groups, tiles = tile_counts(rvals, lvals)
    nblocks, block, width = blocks[0].shape
    slots = sum(-(-tiles // groups) if mask == 0 else 1 for mask in flat(masks))
    extras = 0 if back else len(blocks) - 1
    return pl.pallas_call(
        functools.partial(tiles_kernel, masks, offsets, parts_total, back, feats, extras),
        out_shape=sinks,
        in_specs=[SMEM] * 4
        + [pl.BlockSpec(memory_space=pltpu.HBM)] * 2
        + [VMEM] * len(blocks),
        out_specs=jax.tree.map(lambda _: VMEM, sinks),
        scratch_shapes=[
            pltpu.VMEM((slots, groups, block, block), BF16),
            pltpu.VMEM((2, groups, block, width), F32),
            pltpu.VMEM((2, nblocks, block, width), F32),
            pltpu.SemaphoreType.DMA((slots,)),
        ],
        compiler_params=pltpu.CompilerParams(vmem_limit_bytes=room * 2**20),
        cost_estimate=pl.CostEstimate(flops=1, bytes_accessed=1, transcendentals=0),
    )(*ids, lvals, rvals, *blocks)


def small_call(kernel, outs, arrays, scratch=(), room=24):
    return pl.pallas_call(
        kernel,
        out_shape=outs,
        in_specs=[VMEM] * len(arrays),
        out_specs=[VMEM] * len(outs),
        scratch_shapes=scratch,
        compiler_params=pltpu.CompilerParams(vmem_limit_bytes=room * 2**20),
        cost_estimate=pl.CostEstimate(flops=1, bytes_accessed=1, transcendentals=0),
    )(*arrays)


def agg_kernel(feats, inv_ref, keep_ref, *refs):
    mine = lax.axis_index("feat")
    far_refs, agg_ref, piece_refs = refs[: -1 - feats], refs[-1 - feats], refs[-feats:]
    per_feat = piece_refs[0].shape[0]
    sums = keep_ref[...]
    for ref in far_refs:
        sums = sums + ref[...].astype(F32)
    agg_ref[...] = (sums * inv_ref[...]).astype(BF16)
    for mask, piece in enumerate(piece_refs):
        piece[...] = agg_ref[pl.ds((mine ^ mask) * per_feat, per_feat)]


def joined(parts):
    return jnp.concatenate(parts, axis=1)


def dense_kernel(feats, inv_ref, *refs):
    mine = lax.axis_index("feat")
    w_refs, early_refs, a_refs = refs[:feats], refs[feats : 2 * feats], refs[2 * feats : 3 * feats]
    sent_refs, own_ref = refs[3 * feats : 4 * feats - 1], refs[4 * feats - 1]
    dsum_refs = refs[4 * feats : 5 * feats]
    held = refs[-1]
    full = w_refs[0].shape[2]
    some, width = held.shape[1:]
    pre = jnp.zeros((some, full), F32)
    for mask in range(feats):
        early = early_refs[mask]
        pre = pre + jnp.dot(
            early[0].reshape(some, width), w_refs[mask][0], preferred_element_type=F32
        )
        pre = pre + jnp.dot(
            a_refs[mask][...].reshape(some, width), w_refs[mask][1], preferred_element_type=F32
        )
        held[mine ^ mask] = early[1].reshape(some, width)
    sigma = 1.0 / (1.0 + jnp.exp(-pre))
    out = (pre * sigma).astype(BF16)
    cot = joined([held[j] for j in range(feats)]).astype(F32)
    dpre = (cot * sigma * (1.0 + pre * (1.0 - sigma))).astype(BF16)
    for mask in range(feats):
        dagg = lax.dot_general(
            dpre, w_refs[mask][1], (((1,), (1,)), ((), ())), preferred_element_type=F32
        )
        dsum_refs[mask][...] = (dagg * inv_ref[...]).astype(BF16)
    for j in range(feats):
        cols = slice(j * width, (j + 1) * width)
        for sent in sent_refs:
            sent[j] = dpre[:, cols]
        held[j] = out[:, cols]
    own_ref[...] = held[mine]
    for mask, sent in enumerate(sent_refs, 1):
        sent[feats] = held[mine ^ mask]


def grad_kernel(feats, f_ref, a_ref, w_ref, *refs):
    me = lax.axis_index("dom")
    mine = lax.axis_index("feat")
    dpre_refs, (dx_ref, give_ref, keep_ref, held) = refs[:feats], refs[feats:]
    width = f_ref.shape[1]
    piece = held.shape[1]
    some = dpre_refs[0].shape[1]
    parts = [0.0, 0.0]
    for mask, dpre_ref in enumerate(dpre_refs):
        dpre = joined([dpre_ref[j] for j in range(feats)])
        rows = pl.ds(pl.multiple_of((mine ^ mask) * some, some), some)
        for at, ref in enumerate((f_ref, a_ref)):
            parts[at] = parts[at] + lax.dot_general(
                ref[rows], dpre, (((0,), (0,)), ((), ())), preferred_element_type=F32
            )
        dx_ref[rows] = lax.dot_general(
            dpre, w_ref[...], (((1,), (1,)), ((), ())), preferred_element_type=F32
        )
    for at, part in enumerate(parts):
        for j in range(width // piece):
            held[at * (width // piece) + j] = part[j * piece : (j + 1) * piece]
    side = me % 2
    for at in range(give_ref.shape[0]):
        give_ref[at] = held[2 * at + 1 - side].astype(BF16)
        keep_ref[at] = held[2 * at + side]


def finish_kernel(mine_ref, other_ref, self_ref, neigh_ref, held):
    side = lax.axis_index("dom") % 2
    for at in range(mine_ref.shape[0]):
        held[2 * at + side] = mine_ref[at].astype(F32)
        held[2 * at + 1 - side] = other_ref[at].astype(F32)
    some = held.shape[1]
    half = held.shape[0] // 2
    for j in range(half):
        self_ref[j * some : (j + 1) * some] = held[j]
        neigh_ref[j * some : (j + 1) * some] = held[half + j]


def place_kernel(*refs):
    mine = lax.axis_index("feat")
    own_ref, *come_refs, out_ref = refs
    out_ref[mine] = own_ref[...]
    for mask, come in enumerate(come_refs, 1):
        out_ref[mine ^ mask] = come[out_ref.shape[0]]


def swap_feat(x):
    return lax.all_to_all(x, "feat", split_axis=0, concat_axis=0, tiled=True)


def crossed(x, mask, axis="dom"):
    return lax.ppermute(x, axis, [(i, i ^ mask) for i in range(lax.axis_size(axis))])


def like(shape, dtype):
    return jax.ShapeDtypeStruct(shape, dtype)


def dense_body(
    features,
    w_self,
    w_neigh,
    degree,
    local_vals,
    local_dst,
    local_src,
    remote_vals,
    remote_dst,
    remote_src,
    cotangent,
):
    rows, width = features.shape
    block = local_vals.shape[-1]
    nblocks = rows // block
    rounds = remote_vals.shape[1]
    parts_total = lax.axis_size("dom")
    feats = lax.axis_size("feat")
    some = rows // feats
    per_feat = nblocks // feats
    full = feats * width
    offsets = round_offsets(parts_total, rounds)
    near, far = 1, list(range(parts_total - 2, 0, -2))
    bits = [1, 2, 4]
    mine = lax.axis_index("feat").astype(jnp.int32)
    inverse = 1.0 / degree.astype(F32)
    inv_rows = lax.dynamic_slice(inverse, (mine * some,), (some,))[:, None]
    ids = (
        local_dst,
        local_src,
        jnp.swapaxes(remote_dst, 0, 1),
        jnp.swapaxes(remote_src, 0, 1),
    )
    shape = (nblocks, block, width)
    blocks = features.reshape(shape)
    fixed = (ids, local_vals[0], remote_vals[0])

    def forward(masks, arrays, sinks):
        return tiles_call(
            masks, offsets, parts_total, False, feats, fixed, arrays, sinks, 62
        )

    def relayed(x):
        over = crossed(x, 2, "feat")
        return [x, crossed(x, 1, "feat"), over, crossed(over, 1, "feat")]

    def tied(x, *others):
        return lax.optimization_barrier((x, others))[0]

    made = forward(
        [7, 5, 3, 1],
        [blocks, cotangent.reshape(shape), w_self, w_neigh],
        [like(shape, BF16)] * 4
        + [like((2, per_feat, block, width), BF16)] * feats
        + [like((2, width, full), BF16)],
    )
    sends, early_pieces, pair = made[:4], made[4:-1], made[-1]
    keep_6, keep_4, keep_2 = forward([6, 4, 2], [blocks], [like(shape, F32)] * 3)
    weights = relayed(pair)
    early = [early_pieces[0]] + [crossed(early_pieces[m], m, "feat") for m in range(1, feats)]
    near_6, near_4, near_2, near_0 = (crossed(send, near) for send in sends)
    sum_6 = (keep_6 + near_6.astype(F32)).astype(BF16)
    near_4 = tied(near_4, weights[2])
    sum_4 = (keep_4 + near_4.astype(F32) + crossed(sum_6, 2).astype(F32)).astype(BF16)
    far_0 = crossed(sum_4, 4)
    sum_2 = (keep_2 + near_2.astype(F32)).astype(BF16)
    (keep,) = forward([0], [tied(blocks, sum_2)], [like(shape, F32)])
    mid_0 = crossed(sum_2, 2)
    weights[3] = crossed(tied(weights[2], far_0), 1, "feat")
    arrived = [near_0, mid_0, far_0]
    early, weights, arrived = lax.optimization_barrier((early, weights, arrived))
    agg, *agg_pieces = small_call(
        functools.partial(agg_kernel, feats),
        [like(shape, BF16)] + [like((per_feat, block, width), BF16)] * feats,
        [inverse.reshape(nblocks, block, 1), keep, *arrived],
    )
    agg_rows = [agg_pieces[0]] + [crossed(agg_pieces[m], m, "feat") for m in range(1, feats)]
    *sent, own_out, p0, p1, p2, p3 = small_call(
        functools.partial(dense_kernel, feats),
        [like((feats + 1, some, width), BF16)] * (feats - 1)
        + [like((some, width), BF16)] * (1 + feats),
        [inv_rows, *weights, *early, *agg_rows],
        [pltpu.VMEM((feats, some, width), BF16)],
    )
    dsum_pieces = [p0, p1, p2, p3]
    dsum = jnp.concatenate(
        [dsum_pieces[0]] + [crossed(dsum_pieces[m], m, "feat") for m in range(1, feats)], axis=0
    ).reshape(shape)
    found = {0: dsum}
    for mask in (4, 2, 1):
        found[mask] = crossed(dsum, mask)
    sent = tied(sent, dsum)
    sent[0] = tied(sent[0], found[4], found[2], found[1])
    come = [crossed(sent[m - 1], m, "feat") for m in range(1, feats)]
    (out,) = small_call(place_kernel, [like((feats, some, width), BF16)], [own_out, *come])
    come, found[4], found[2], found[1] = lax.optimization_barrier(
        (come, found[4], found[2], found[1])
    )
    dpre = [sent[0], *come]
    found[6] = crossed(found[4], 2)
    found[3] = crossed(found[2], near)
    found[5] = crossed(tied(found[4], found[3]), near)
    found[7] = crossed(tied(found[6], found[5]), near)
    piece = 2 * width // parts_total
    dx_self, give, keep = small_call(
        functools.partial(grad_kernel, feats),
        [
            like((rows, width), F32),
            like((len(far) + 1, piece, full), BF16),
            like((len(far) + 1, piece, full), F32),
        ],
        [features, agg.reshape(rows, width), w_self, *dpre],
        [pltpu.VMEM((parts_total, piece, full), F32)],
    )
    total = (keep + crossed(give, near).astype(F32)).astype(BF16)
    total = tied(total, found[3], found[6])
    total = (total.astype(F32) + crossed(total, 2).astype(F32)).astype(BF16)
    total = tied(total, found[5])
    total = (total.astype(F32) + crossed(total, 4).astype(F32)).astype(BF16)
    total, out = tied((total, out), found[7])
    grad_self, grad_neigh = small_call(
        finish_kernel,
        [like((width, full), F32)] * 2,
        [total, crossed(total, near)],
        [pltpu.VMEM((parts_total, piece, full), F32)],
    )
    grad_x = dx_self.reshape(shape)
    half = parts_total // 2
    for order in (list(range(half)), list(range(half, parts_total))):
        grad_x = tiles_call(
            order,
            offsets,
            parts_total,
            True,
            feats,
            fixed,
            [found[mask] for mask in order] + [grad_x],
            like(shape, F32),
            24,
        )
    return (out.reshape(rows, width), grad_x.reshape(rows, width), grad_self, grad_neigh)


def solution(mesh):
    def body(*args):
        rounds = args[7].shape[1]
        small = mesh.shape["dom"] == 8 and mesh.shape["feat"] == 4
        nearly_all = mesh.shape["dom"] <= rounds + 2
        return (dense_body if small and nearly_all else sparse_body)(*args)

    placed = (
        P("dom", "feat"),
        P("feat", None),
        P("feat", None),
        P("dom"),
        P("dom", None, None, None),
        P("dom", None),
        P("dom", None),
        P("dom", None, None, None, None),
        P("dom", None, None),
        P("dom", None, None),
        P("dom", "feat"),
    )
    return jax.shard_map(
        body,
        mesh=mesh,
        in_specs=placed,
        out_specs=(P("dom", "feat"), P("dom", "feat"), P("feat", None), P("feat", None)),
        check_vma=False,
    )
```

```python
import functools

import jax
import jax.numpy as jnp
from jax import lax
from jax.experimental import pallas as pl
from jax.experimental.pallas import tpu as pltpu
from jax.sharding import PartitionSpec as P

F32 = jnp.float32
BF16 = jnp.bfloat16
VMEM = pl.BlockSpec(memory_space=pltpu.VMEM)
SMEM = pl.BlockSpec(memory_space=pltpu.SMEM)


def shifted(x, axis, by):
    devices = lax.axis_size(axis)
    return lax.ppermute(x, axis, [(i, (i + by) % devices) for i in range(devices)])


def spread(parts, block_ids, count):
    table = (block_ids[:, None] == jnp.arange(count, dtype=jnp.int32)[None, :]).astype(F32)
    return jnp.einsum("kc,kif->cif", table, parts, precision=lax.Precision.HIGHEST)


def tile_apply(tiles, blocks):
    return jnp.einsum("kij,kjf->kif", tiles, blocks, preferred_element_type=F32)


def tile_apply_back(tiles, blocks):
    return jnp.einsum("kji,kjf->kif", tiles, blocks, preferred_element_type=F32)


def round_offsets(parts_total, rounds):
    return [(step + 1) * parts_total // (rounds + 1) for step in range(rounds)]


def sparse_body(
    features,
    w_self,
    w_neigh,
    degree,
    local_vals,
    local_dst,
    local_src,
    remote_vals,
    remote_dst,
    remote_src,
    cotangent,
):
    rows, width = features.shape
    block = local_vals.shape[-1]
    nblocks = rows // block
    rounds = remote_vals.shape[1]
    parts_total = lax.axis_size("dom")
    offsets = round_offsets(parts_total, rounds)
    blocks = features.reshape(nblocks, block, width)
    totals = spread(
        tile_apply(local_vals[0], jnp.take(blocks, local_src[0], axis=0)), local_dst[0], nblocks
    )
    arrived_ids = []
    for step in range(rounds):
        partial_blocks = tile_apply(
            remote_vals[0, step], jnp.take(blocks, remote_src[0, step], axis=0)
        ).astype(BF16)
        arrived, block_ids = shifted((partial_blocks, remote_dst[0, step]), "dom", offsets[step])
        arrived_ids.append(block_ids)
        totals = totals + spread(arrived.astype(F32), block_ids, nblocks)
    inverse = 1.0 / degree.astype(F32)
    agg = (totals.reshape(rows, width) * inverse[:, None]).astype(BF16)
    stacked = jnp.concatenate([features, agg], axis=1)
    weights = jnp.concatenate([w_self, w_neigh], axis=0)
    pre = lax.psum_scatter(
        lax.dot_general(weights, stacked, (((0,), (1,)), ((), ())), preferred_element_type=F32),
        "feat",
        scatter_dimension=0,
        tiled=True,
    ).T
    sigma = jax.nn.sigmoid(pre)
    out = (pre * sigma).astype(BF16)
    dpre = (cotangent.astype(F32) * sigma * (1.0 + pre * (1.0 - sigma))).astype(BF16)
    dpre_all = lax.all_gather(dpre, "feat", axis=1, tiled=True)
    dz_total = lax.dot_general(
        dpre_all, weights, (((1,), (1,)), ((), ())), preferred_element_type=F32
    )
    grad_local = lax.dot_general(
        stacked, dpre_all, (((0,), (0,)), ((), ())), preferred_element_type=F32
    )
    dx_self = dz_total[:, :width]
    dsum = (dz_total[:, width:] * inverse[:, None]).astype(BF16).reshape(nblocks, block, width)
    grad_all = lax.psum(grad_local, "dom")
    back = spread(
        tile_apply_back(local_vals[0], jnp.take(dsum, local_dst[0], axis=0)), local_src[0], nblocks
    )
    for step in range(rounds):
        picked = jnp.take(dsum, arrived_ids[step], axis=0)
        returned = shifted(picked, "dom", parts_total - offsets[step])
        back = back + spread(
            tile_apply_back(remote_vals[0, step], returned), remote_src[0, step], nblocks
        )
    grad_x = dx_self + back.reshape(rows, width)
    return (out, grad_x, grad_all[:width], grad_all[width:])


def tile_counts(rvals, lvals):
    return rvals.shape[0], rvals.shape[1], lvals.shape[0]


def round_of(offset, offsets):
    step, known = jnp.int32(0), offset < 0
    for at, this in enumerate(offsets):
        step = jnp.where(offset == this, at, step)
        known = known | (offset == this)
    return step, known


def crossed_block(block_id, mine, per_feat):
    return ((block_id // per_feat) ^ mine) * per_feat + block_id % per_feat


def tile_groups(masks, offsets, parts_total, me, groups, tiles, ids):
    ldst, lsrc, rdst, rsrc = ids
    jobs = []
    for at, mask in enumerate(masks):
        if mask == 0:
            for first in range(0, tiles, groups):
                count = min(groups, tiles - first)
                dst = [ldst[0, first + k] for k in range(count)]
                src = [lsrc[0, first + k] for k in range(count)]
                jobs.append((at, None, None, first, dst, src))
        else:
            offset = lax.rem((me ^ mask) - me + parts_total, parts_total)
            step, known = round_of(offset, offsets)
            dst = [rdst[step, 0, k] for k in range(groups)]
            src = [rsrc[step, 0, k] for k in range(groups)]
            jobs.append((at, step, known, None, dst, src))
    return jobs


def flat(masks):
    return [m for group in masks for m in (group if isinstance(group, list) else [group])]


def tiles_kernel(masks, offsets, parts_total, back, feats, extras, *refs):
    ids, (lvals, rvals), refs = refs[:4], refs[4:6], refs[6:]
    groups_of, masks = masks, flat(masks)
    me = lax.axis_index("dom")
    mine = lax.axis_index("feat")
    rounds, groups, tiles = tile_counts(rvals, lvals)
    jobs = tile_groups(masks, offsets, parts_total, me, groups, tiles, ids)
    held, prod, acc, sems = refs[-4:]
    copies = []
    for slot, (at, step, known, first, dst, src) in enumerate(jobs):
        source = lvals.at[pl.ds(first, len(dst))] if step is None else rvals.at[step]
        copy = pltpu.make_async_copy(source, held.at[slot, pl.ds(0, len(dst))], sems.at[slot])
        copy.start()
        copies.append(copy)
    if back:
        own_ref, grad_ref = refs[len(masks)], refs[len(masks) + 1]
        blocks = refs[: len(masks)]
        sinks = [grad_ref] * len(masks)
        acc[0] = own_ref[...]
    else:
        blocks = [refs[0]] * len(masks)
        sinks, used = [], 1 + extras
        for group in groups_of:
            if isinstance(group, list):
                sinks += [refs[used].at[n] for n in range(len(group))]
            else:
                sinks.append(refs[used])
            used += 1
    if extras:
        pieces, pair = refs[used : used + feats], refs[used + feats]
        pair[0] = refs[2][...]
        pair[1] = refs[3][...]
        for mask, piece in enumerate(pieces):
            rows = pl.ds((mine ^ mask) * piece.shape[1], piece.shape[1])
            piece[0] = refs[0][rows]
            piece[1] = refs[1][rows]
    total = 0
    for slot, (at, step, known, first, dst, src) in enumerate(jobs):
        copies[slot].wait()
        half = slot % 2
        for k in range(len(dst)):
            if back:
                per_feat = blocks[at].shape[0] // feats
                block = blocks[at][crossed_block(dst[k], mine, per_feat)]
                product = lax.dot_general(
                    held[slot, k], block, (((0,), (0,)), ((), ())), preferred_element_type=F32
                )
            else:
                product = jnp.dot(
                    held[slot, k], blocks[at][src[k]], preferred_element_type=F32
                )
            prod[half, k] = product if known is None else jnp.where(known, product, 0.0)
        fresh = not back and (slot == 0 or jobs[slot - 1][0] != at)
        if fresh:
            total = at % 2
            acc[total] = jnp.zeros(acc.shape[1:], F32)
        for k in range(len(dst)):
            into = src[k] if back else dst[k]
            acc[total, into] = acc[total, into] + prod[half, k]
        last = slot == len(jobs) - 1 or jobs[slot + 1][0] != at
        if last and (not back or slot == len(jobs) - 1):
            sinks[at][...] = acc[total].astype(sinks[at].dtype)


def tiles_call(masks, offsets, parts_total, back, feats, fixed, blocks, sinks, room):
    ids, lvals, rvals = fixed
    rounds, groups, tiles = tile_counts(rvals, lvals)
    nblocks, block, width = blocks[0].shape
    slots = sum(-(-tiles // groups) if mask == 0 else 1 for mask in flat(masks))
    extras = 0 if back else len(blocks) - 1
    return pl.pallas_call(
        functools.partial(tiles_kernel, masks, offsets, parts_total, back, feats, extras),
        out_shape=sinks,
        in_specs=[SMEM] * 4
        + [pl.BlockSpec(memory_space=pltpu.HBM)] * 2
        + [VMEM] * len(blocks),
        out_specs=jax.tree.map(lambda _: VMEM, sinks),
        scratch_shapes=[
            pltpu.VMEM((slots, groups, block, block), BF16),
            pltpu.VMEM((2, groups, block, width), F32),
            pltpu.VMEM((2, nblocks, block, width), F32),
            pltpu.SemaphoreType.DMA((slots,)),
        ],
        compiler_params=pltpu.CompilerParams(vmem_limit_bytes=room * 2**20),
        cost_estimate=pl.CostEstimate(flops=1, bytes_accessed=1, transcendentals=0),
    )(*ids, lvals, rvals, *blocks)


def small_call(kernel, outs, arrays, scratch=(), room=24):
    return pl.pallas_call(
        kernel,
        out_shape=outs,
        in_specs=[VMEM] * len(arrays),
        out_specs=[VMEM] * len(outs),
        scratch_shapes=scratch,
        compiler_params=pltpu.CompilerParams(vmem_limit_bytes=room * 2**20),
        cost_estimate=pl.CostEstimate(flops=1, bytes_accessed=1, transcendentals=0),
    )(*arrays)


def agg_kernel(feats, inv_ref, keep_ref, *refs):
    mine = lax.axis_index("feat")
    far_refs, agg_ref, piece_refs = refs[: -1 - feats], refs[-1 - feats], refs[-feats:]
    per_feat = piece_refs[0].shape[0]
    sums = keep_ref[...]
    for ref in far_refs:
        sums = sums + ref[...].astype(F32)
    agg_ref[...] = (sums * inv_ref[...]).astype(BF16)
    for mask, piece in enumerate(piece_refs):
        piece[...] = agg_ref[pl.ds((mine ^ mask) * per_feat, per_feat)]


def joined(parts):
    return jnp.concatenate(parts, axis=1)


def dense_kernel(feats, inv_ref, *refs):
    mine = lax.axis_index("feat")
    w_refs, early_refs, a_refs = refs[:feats], refs[feats : 2 * feats], refs[2 * feats : 3 * feats]
    sent_refs, own_ref = refs[3 * feats : 4 * feats - 1], refs[4 * feats - 1]
    dsum_refs = refs[4 * feats : 5 * feats]
    held = refs[-1]
    full = w_refs[0].shape[2]
    some, width = held.shape[1:]
    pre = jnp.zeros((some, full), F32)
    for mask in range(feats):
        early = early_refs[mask]
        pre = pre + jnp.dot(
            early[0].reshape(some, width), w_refs[mask][0], preferred_element_type=F32
        )
        pre = pre + jnp.dot(
            a_refs[mask][...].reshape(some, width), w_refs[mask][1], preferred_element_type=F32
        )
        held[mine ^ mask] = early[1].reshape(some, width)
    sigma = 1.0 / (1.0 + jnp.exp(-pre))
    out = (pre * sigma).astype(BF16)
    cot = joined([held[j] for j in range(feats)]).astype(F32)
    dpre = (cot * sigma * (1.0 + pre * (1.0 - sigma))).astype(BF16)
    for mask in range(feats):
        dagg = lax.dot_general(
            dpre, w_refs[mask][1], (((1,), (1,)), ((), ())), preferred_element_type=F32
        )
        dsum_refs[mask][...] = (dagg * inv_ref[...]).astype(BF16)
    for j in range(feats):
        cols = slice(j * width, (j + 1) * width)
        for sent in sent_refs:
            sent[j] = dpre[:, cols]
        held[j] = out[:, cols]
    own_ref[...] = held[mine]
    for mask, sent in enumerate(sent_refs, 1):
        sent[feats] = held[mine ^ mask]


def grad_kernel(feats, f_ref, a_ref, w_ref, *refs):
    me = lax.axis_index("dom")
    mine = lax.axis_index("feat")
    dpre_refs, (dx_ref, give_ref, keep_ref, held) = refs[:feats], refs[feats:]
    width = f_ref.shape[1]
    piece = held.shape[1]
    some = dpre_refs[0].shape[1]
    parts = [0.0, 0.0]
    for mask, dpre_ref in enumerate(dpre_refs):
        dpre = joined([dpre_ref[j] for j in range(feats)])
        rows = pl.ds(pl.multiple_of((mine ^ mask) * some, some), some)
        for at, ref in enumerate((f_ref, a_ref)):
            parts[at] = parts[at] + lax.dot_general(
                ref[rows], dpre, (((0,), (0,)), ((), ())), preferred_element_type=F32
            )
        dx_ref[rows] = lax.dot_general(
            dpre, w_ref[...], (((1,), (1,)), ((), ())), preferred_element_type=F32
        )
    for at, part in enumerate(parts):
        for j in range(width // piece):
            held[at * (width // piece) + j] = part[j * piece : (j + 1) * piece]
    side = me % 2
    for at in range(give_ref.shape[0]):
        give_ref[at] = held[2 * at + 1 - side].astype(BF16)
        keep_ref[at] = held[2 * at + side]


def finish_kernel(mine_ref, other_ref, self_ref, neigh_ref, held):
    side = lax.axis_index("dom") % 2
    for at in range(mine_ref.shape[0]):
        held[2 * at + side] = mine_ref[at].astype(F32)
        held[2 * at + 1 - side] = other_ref[at].astype(F32)
    some = held.shape[1]
    half = held.shape[0] // 2
    for j in range(half):
        self_ref[j * some : (j + 1) * some] = held[j]
        neigh_ref[j * some : (j + 1) * some] = held[half + j]


def place_kernel(*refs):
    mine = lax.axis_index("feat")
    own_ref, *come_refs, out_ref = refs
    out_ref[mine] = own_ref[...]
    for mask, come in enumerate(come_refs, 1):
        out_ref[mine ^ mask] = come[out_ref.shape[0]]


def swap_feat(x):
    return lax.all_to_all(x, "feat", split_axis=0, concat_axis=0, tiled=True)


def crossed(x, mask, axis="dom"):
    return lax.ppermute(x, axis, [(i, i ^ mask) for i in range(lax.axis_size(axis))])


def like(shape, dtype):
    return jax.ShapeDtypeStruct(shape, dtype)


def dense_body(
    features,
    w_self,
    w_neigh,
    degree,
    local_vals,
    local_dst,
    local_src,
    remote_vals,
    remote_dst,
    remote_src,
    cotangent,
):
    rows, width = features.shape
    block = local_vals.shape[-1]
    nblocks = rows // block
    rounds = remote_vals.shape[1]
    parts_total = lax.axis_size("dom")
    feats = lax.axis_size("feat")
    some = rows // feats
    per_feat = nblocks // feats
    full = feats * width
    offsets = round_offsets(parts_total, rounds)
    near, far = 1, list(range(parts_total - 2, 0, -2))
    bits = [1, 2, 4]
    mine = lax.axis_index("feat").astype(jnp.int32)
    inverse = 1.0 / degree.astype(F32)
    inv_rows = lax.dynamic_slice(inverse, (mine * some,), (some,))[:, None]
    ids = (
        local_dst,
        local_src,
        jnp.swapaxes(remote_dst, 0, 1),
        jnp.swapaxes(remote_src, 0, 1),
    )
    shape = (nblocks, block, width)
    blocks = features.reshape(shape)
    fixed = (ids, local_vals[0], remote_vals[0])

    def forward(masks, arrays, sinks):
        return tiles_call(
            masks, offsets, parts_total, False, feats, fixed, arrays, sinks, 62
        )

    def relayed(x):
        over = crossed(x, 2, "feat")
        return [x, crossed(x, 1, "feat"), over, crossed(over, 1, "feat")]

    def tied(x, *others):
        return lax.optimization_barrier((x, others))[0]

    made = forward(
        [7, 3, 5, 1],
        [blocks, cotangent.reshape(shape), w_self, w_neigh],
        [like(shape, BF16)] * 4
        + [like((2, per_feat, block, width), BF16)] * feats
        + [like((2, width, full), BF16)],
    )
    sends, early_pieces, pair = made[:4], made[4:-1], made[-1]
    keep_6, keep_2, keep_4, keep = forward([6, 2, 4, 0], [blocks], [like(shape, F32)] * 4)
    weights = relayed(pair)
    early = [early_pieces[0]] + [crossed(early_pieces[m], m, "feat") for m in range(1, feats)]
    near_6, near_2, near_4, near_0 = (crossed(send, near) for send in sends)
    sum_6 = (keep_6 + near_6.astype(F32)).astype(BF16)
    sum_2 = (keep_2 + near_2.astype(F32)).astype(BF16)
    mid_0 = crossed(sum_2, 2)
    near_4, mid_0, weights[2] = lax.optimization_barrier((near_4, mid_0, weights[2]))
    sum_4 = (keep_4 + near_4.astype(F32) + crossed(sum_6, 2).astype(F32)).astype(BF16)
    far_0 = crossed(sum_4, 4)
    part = keep + mid_0.astype(F32)
    arrived = [far_0, near_0]
    early, weights, arrived = lax.optimization_barrier((early, weights, arrived))
    agg, *agg_pieces = small_call(
        functools.partial(agg_kernel, feats),
        [like(shape, BF16)] + [like((per_feat, block, width), BF16)] * feats,
        [inverse.reshape(nblocks, block, 1), part, *arrived],
    )
    agg_rows = [agg_pieces[0]] + [crossed(agg_pieces[m], m, "feat") for m in range(1, feats)]
    *sent, own_out, p0, p1, p2, p3 = small_call(
        functools.partial(dense_kernel, feats),
        [like((feats + 1, some, width), BF16)] * (feats - 1)
        + [like((some, width), BF16)] * (1 + feats),
        [inv_rows, *weights, *early, *agg_rows],
        [pltpu.VMEM((feats, some, width), BF16)],
    )
    dsum_pieces = [p0, p1, p2, p3]
    dsum = jnp.concatenate(
        [dsum_pieces[0]] + [crossed(dsum_pieces[m], m, "feat") for m in range(1, feats)], axis=0
    ).reshape(shape)
    found = {0: dsum}
    for mask in (4, 2, 1):
        found[mask] = crossed(dsum, mask)
    sent = tied(sent, dsum)
    sent[0] = tied(sent[0], found[4], found[2], found[1])
    come = [crossed(sent[m - 1], m, "feat") for m in range(1, feats)]
    (out,) = small_call(place_kernel, [like((feats, some, width), BF16)], [own_out, *come])
    come, found[4], found[2], found[1] = lax.optimization_barrier(
        (come, found[4], found[2], found[1])
    )
    dpre = [sent[0], *come]
    found[6] = crossed(found[4], 2)
    found[3] = crossed(found[2], near)
    found[5] = crossed(found[1], 4)
    found[7] = crossed(found[6], near)
    piece = 2 * width // parts_total
    dx_self, give, keep = small_call(
        functools.partial(grad_kernel, feats),
        [
            like((rows, width), F32),
            like((len(far) + 1, piece, full), BF16),
            like((len(far) + 1, piece, full), F32),
        ],
        [features, agg.reshape(rows, width), w_self, *dpre],
        [pltpu.VMEM((parts_total, piece, full), F32)],
    )
    total = (keep + crossed(give, near).astype(F32)).astype(BF16)
    total = tied(total, found[3], found[5], found[6])
    total = (total.astype(F32) + crossed(total, 2).astype(F32)).astype(BF16)
    total = (total.astype(F32) + crossed(total, 4).astype(F32)).astype(BF16)
    total, out = tied((total, out), found[7])
    grad_self, grad_neigh = small_call(
        finish_kernel,
        [like((width, full), F32)] * 2,
        [total, crossed(total, near)],
        [pltpu.VMEM((parts_total, piece, full), F32)],
    )
    grad_x = dx_self.reshape(shape)
    half = parts_total // 2
    for order in (list(range(half)), list(range(half, parts_total))):
        grad_x = tiles_call(
            order,
            offsets,
            parts_total,
            True,
            feats,
            fixed,
            [found[mask] for mask in order] + [grad_x],
            like(shape, F32),
            24,
        )
    return (out.reshape(rows, width), grad_x.reshape(rows, width), grad_self, grad_neigh)


def solution(mesh):
    def body(*args):
        rounds = args[7].shape[1]
        small = mesh.shape["dom"] == 8 and mesh.shape["feat"] == 4
        nearly_all = mesh.shape["dom"] <= rounds + 2
        return (dense_body if small and nearly_all else sparse_body)(*args)

    placed = (
        P("dom", "feat"),
        P("feat", None),
        P("feat", None),
        P("dom"),
        P("dom", None, None, None),
        P("dom", None),
        P("dom", None),
        P("dom", None, None, None, None),
        P("dom", None, None),
        P("dom", None, None),
        P("dom", "feat"),
    )
    return jax.shard_map(
        body,
        mesh=mesh,
        in_specs=placed,
        out_specs=(P("dom", "feat"), P("dom", "feat"), P("feat", None), P("feat", None)),
        check_vma=False,
    )
```

```python
import functools

import jax
import jax.numpy as jnp
from jax import lax
from jax.experimental import pallas as pl
from jax.experimental.pallas import tpu as pltpu
from jax.sharding import PartitionSpec as P

F32 = jnp.float32
BF16 = jnp.bfloat16
VMEM = pl.BlockSpec(memory_space=pltpu.VMEM)
SMEM = pl.BlockSpec(memory_space=pltpu.SMEM)


def shifted(x, axis, by):
    devices = lax.axis_size(axis)
    return lax.ppermute(x, axis, [(i, (i + by) % devices) for i in range(devices)])


def spread(parts, block_ids, count):
    table = (block_ids[:, None] == jnp.arange(count, dtype=jnp.int32)[None, :]).astype(F32)
    return jnp.einsum("kc,kif->cif", table, parts, precision=lax.Precision.HIGHEST)


def tile_apply(tiles, blocks):
    return jnp.einsum("kij,kjf->kif", tiles, blocks, preferred_element_type=F32)


def tile_apply_back(tiles, blocks):
    return jnp.einsum("kji,kjf->kif", tiles, blocks, preferred_element_type=F32)


def round_offsets(parts_total, rounds):
    return [(step + 1) * parts_total // (rounds + 1) for step in range(rounds)]


def sparse_body(
    features,
    w_self,
    w_neigh,
    degree,
    local_vals,
    local_dst,
    local_src,
    remote_vals,
    remote_dst,
    remote_src,
    cotangent,
):
    rows, width = features.shape
    block = local_vals.shape[-1]
    nblocks = rows // block
    rounds = remote_vals.shape[1]
    parts_total = lax.axis_size("dom")
    offsets = round_offsets(parts_total, rounds)
    blocks = features.reshape(nblocks, block, width)
    totals = spread(
        tile_apply(local_vals[0], jnp.take(blocks, local_src[0], axis=0)), local_dst[0], nblocks
    )
    arrived_ids = []
    for step in range(rounds):
        partial_blocks = tile_apply(
            remote_vals[0, step], jnp.take(blocks, remote_src[0, step], axis=0)
        ).astype(BF16)
        arrived, block_ids = shifted((partial_blocks, remote_dst[0, step]), "dom", offsets[step])
        arrived_ids.append(block_ids)
        totals = totals + spread(arrived.astype(F32), block_ids, nblocks)
    inverse = 1.0 / degree.astype(F32)
    agg = (totals.reshape(rows, width) * inverse[:, None]).astype(BF16)
    stacked = jnp.concatenate([features, agg], axis=1)
    weights = jnp.concatenate([w_self, w_neigh], axis=0)
    pre = lax.psum_scatter(
        lax.dot_general(weights, stacked, (((0,), (1,)), ((), ())), preferred_element_type=F32),
        "feat",
        scatter_dimension=0,
        tiled=True,
    ).T
    sigma = jax.nn.sigmoid(pre)
    out = (pre * sigma).astype(BF16)
    dpre = (cotangent.astype(F32) * sigma * (1.0 + pre * (1.0 - sigma))).astype(BF16)
    dpre_all = lax.all_gather(dpre, "feat", axis=1, tiled=True)
    dz_total = lax.dot_general(
        dpre_all, weights, (((1,), (1,)), ((), ())), preferred_element_type=F32
    )
    grad_local = lax.dot_general(
        stacked, dpre_all, (((0,), (0,)), ((), ())), preferred_element_type=F32
    )
    dx_self = dz_total[:, :width]
    dsum = (dz_total[:, width:] * inverse[:, None]).astype(BF16).reshape(nblocks, block, width)
    grad_all = lax.psum(grad_local, "dom")
    back = spread(
        tile_apply_back(local_vals[0], jnp.take(dsum, local_dst[0], axis=0)), local_src[0], nblocks
    )
    for step in range(rounds):
        picked = jnp.take(dsum, arrived_ids[step], axis=0)
        returned = shifted(picked, "dom", parts_total - offsets[step])
        back = back + spread(
            tile_apply_back(remote_vals[0, step], returned), remote_src[0, step], nblocks
        )
    grad_x = dx_self + back.reshape(rows, width)
    return (out, grad_x, grad_all[:width], grad_all[width:])


def tile_counts(rvals, lvals):
    return rvals.shape[0], rvals.shape[1], lvals.shape[0]


def round_of(offset, offsets):
    step, known = jnp.int32(0), offset < 0
    for at, this in enumerate(offsets):
        step = jnp.where(offset == this, at, step)
        known = known | (offset == this)
    return step, known


def crossed_block(block_id, mine, per_feat):
    return ((block_id // per_feat) ^ mine) * per_feat + block_id % per_feat


def tile_groups(masks, offsets, parts_total, me, groups, tiles, ids):
    ldst, lsrc, rdst, rsrc = ids
    jobs = []
    for at, mask in enumerate(masks):
        if mask == 0:
            for first in range(0, tiles, groups):
                count = min(groups, tiles - first)
                dst = [ldst[0, first + k] for k in range(count)]
                src = [lsrc[0, first + k] for k in range(count)]
                jobs.append((at, None, None, first, dst, src))
        else:
            offset = lax.rem((me ^ mask) - me + parts_total, parts_total)
            step, known = round_of(offset, offsets)
            dst = [rdst[step, 0, k] for k in range(groups)]
            src = [rsrc[step, 0, k] for k in range(groups)]
            jobs.append((at, step, known, None, dst, src))
    return jobs


def flat(masks):
    return [m for group in masks for m in (group if isinstance(group, list) else [group])]


def tiles_kernel(masks, offsets, parts_total, back, feats, extras, *refs):
    ids, (lvals, rvals), refs = refs[:4], refs[4:6], refs[6:]
    groups_of, masks = masks, flat(masks)
    me = lax.axis_index("dom")
    mine = lax.axis_index("feat")
    rounds, groups, tiles = tile_counts(rvals, lvals)
    jobs = tile_groups(masks, offsets, parts_total, me, groups, tiles, ids)
    held, prod, acc, sems = refs[-4:]
    copies = []
    for slot, (at, step, known, first, dst, src) in enumerate(jobs):
        source = lvals.at[pl.ds(first, len(dst))] if step is None else rvals.at[step]
        copy = pltpu.make_async_copy(source, held.at[slot, pl.ds(0, len(dst))], sems.at[slot])
        copy.start()
        copies.append(copy)
    if back:
        own_ref, grad_ref = refs[len(masks)], refs[len(masks) + 1]
        blocks = refs[: len(masks)]
        sinks = [grad_ref] * len(masks)
        acc[0] = own_ref[...]
    else:
        blocks = [refs[0]] * len(masks)
        sinks, used = [], 1 + extras
        for group in groups_of:
            if isinstance(group, list):
                sinks += [refs[used].at[n] for n in range(len(group))]
            else:
                sinks.append(refs[used])
            used += 1
    if extras:
        pieces, pair = refs[used : used + feats], refs[used + feats]
        pair[0] = refs[2][...]
        pair[1] = refs[3][...]
        for mask, piece in enumerate(pieces):
            rows = pl.ds((mine ^ mask) * piece.shape[1], piece.shape[1])
            piece[0] = refs[0][rows]
            piece[1] = refs[1][rows]
    total = 0
    for slot, (at, step, known, first, dst, src) in enumerate(jobs):
        copies[slot].wait()
        half = slot % 2
        for k in range(len(dst)):
            if back:
                per_feat = blocks[at].shape[0] // feats
                block = blocks[at][crossed_block(dst[k], mine, per_feat)]
                product = lax.dot_general(
                    held[slot, k], block, (((0,), (0,)), ((), ())), preferred_element_type=F32
                )
            else:
                product = jnp.dot(
                    held[slot, k], blocks[at][src[k]], preferred_element_type=F32
                )
            prod[half, k] = product if known is None else jnp.where(known, product, 0.0)
        fresh = not back and (slot == 0 or jobs[slot - 1][0] != at)
        if fresh:
            total = at % 2
            acc[total] = jnp.zeros(acc.shape[1:], F32)
        for k in range(len(dst)):
            into = src[k] if back else dst[k]
            acc[total, into] = acc[total, into] + prod[half, k]
        last = slot == len(jobs) - 1 or jobs[slot + 1][0] != at
        if last and (not back or slot == len(jobs) - 1):
            sinks[at][...] = acc[total].astype(sinks[at].dtype)


def tiles_call(masks, offsets, parts_total, back, feats, fixed, blocks, sinks, room):
    ids, lvals, rvals = fixed
    rounds, groups, tiles = tile_counts(rvals, lvals)
    nblocks, block, width = blocks[0].shape
    slots = sum(-(-tiles // groups) if mask == 0 else 1 for mask in flat(masks))
    extras = 0 if back else len(blocks) - 1
    return pl.pallas_call(
        functools.partial(tiles_kernel, masks, offsets, parts_total, back, feats, extras),
        out_shape=sinks,
        in_specs=[SMEM] * 4
        + [pl.BlockSpec(memory_space=pltpu.HBM)] * 2
        + [VMEM] * len(blocks),
        out_specs=jax.tree.map(lambda _: VMEM, sinks),
        scratch_shapes=[
            pltpu.VMEM((slots, groups, block, block), BF16),
            pltpu.VMEM((2, groups, block, width), F32),
            pltpu.VMEM((2, nblocks, block, width), F32),
            pltpu.SemaphoreType.DMA((slots,)),
        ],
        compiler_params=pltpu.CompilerParams(vmem_limit_bytes=room * 2**20),
        cost_estimate=pl.CostEstimate(flops=1, bytes_accessed=1, transcendentals=0),
    )(*ids, lvals, rvals, *blocks)


def small_call(kernel, outs, arrays, scratch=(), room=24):
    return pl.pallas_call(
        kernel,
        out_shape=outs,
        in_specs=[VMEM] * len(arrays),
        out_specs=[VMEM] * len(outs),
        scratch_shapes=scratch,
        compiler_params=pltpu.CompilerParams(vmem_limit_bytes=room * 2**20),
        cost_estimate=pl.CostEstimate(flops=1, bytes_accessed=1, transcendentals=0),
    )(*arrays)


def agg_kernel(feats, inv_ref, keep_ref, *refs):
    mine = lax.axis_index("feat")
    far_refs, agg_ref, piece_refs = refs[: -1 - feats], refs[-1 - feats], refs[-feats:]
    per_feat = piece_refs[0].shape[0]
    sums = keep_ref[...]
    for ref in far_refs:
        sums = sums + ref[...].astype(F32)
    agg_ref[...] = (sums * inv_ref[...]).astype(BF16)
    for mask, piece in enumerate(piece_refs):
        piece[...] = agg_ref[pl.ds((mine ^ mask) * per_feat, per_feat)]


def joined(parts):
    return jnp.concatenate(parts, axis=1)


def dense_kernel(feats, inv_ref, *refs):
    mine = lax.axis_index("feat")
    w_refs, early_refs, a_refs = refs[:feats], refs[feats : 2 * feats], refs[2 * feats : 3 * feats]
    sent_refs, own_ref = refs[3 * feats : 4 * feats - 1], refs[4 * feats - 1]
    dsum_refs = refs[4 * feats : 5 * feats]
    held = refs[-1]
    full = w_refs[0].shape[2]
    some, width = held.shape[1:]
    pre = jnp.zeros((some, full), F32)
    for mask in range(feats):
        early = early_refs[mask]
        pre = pre + jnp.dot(
            early[0].reshape(some, width), w_refs[mask][0], preferred_element_type=F32
        )
        pre = pre + jnp.dot(
            a_refs[mask][...].reshape(some, width), w_refs[mask][1], preferred_element_type=F32
        )
        held[mine ^ mask] = early[1].reshape(some, width)
    sigma = 1.0 / (1.0 + jnp.exp(-pre))
    out = (pre * sigma).astype(BF16)
    cot = joined([held[j] for j in range(feats)]).astype(F32)
    dpre = (cot * sigma * (1.0 + pre * (1.0 - sigma))).astype(BF16)
    for mask in range(feats):
        dagg = lax.dot_general(
            dpre, w_refs[mask][1], (((1,), (1,)), ((), ())), preferred_element_type=F32
        )
        dsum_refs[mask][...] = (dagg * inv_ref[...]).astype(BF16)
    for j in range(feats):
        cols = slice(j * width, (j + 1) * width)
        for sent in sent_refs:
            sent[j] = dpre[:, cols]
        held[j] = out[:, cols]
    own_ref[...] = held[mine]
    for mask, sent in enumerate(sent_refs, 1):
        sent[feats] = held[mine ^ mask]


def grad_kernel(feats, f_ref, a_ref, w_ref, *refs):
    me = lax.axis_index("dom")
    mine = lax.axis_index("feat")
    dpre_refs, (dx_ref, give_ref, keep_ref, held) = refs[:feats], refs[feats:]
    width = f_ref.shape[1]
    piece = held.shape[1]
    some = dpre_refs[0].shape[1]
    parts = [0.0, 0.0]
    for mask, dpre_ref in enumerate(dpre_refs):
        dpre = joined([dpre_ref[j] for j in range(feats)])
        rows = pl.ds(pl.multiple_of((mine ^ mask) * some, some), some)
        for at, ref in enumerate((f_ref, a_ref)):
            parts[at] = parts[at] + lax.dot_general(
                ref[rows], dpre, (((0,), (0,)), ((), ())), preferred_element_type=F32
            )
        dx_ref[rows] = lax.dot_general(
            dpre, w_ref[...], (((1,), (1,)), ((), ())), preferred_element_type=F32
        )
    for at, part in enumerate(parts):
        for j in range(width // piece):
            held[at * (width // piece) + j] = part[j * piece : (j + 1) * piece]
    side = me % 2
    for at in range(give_ref.shape[0]):
        give_ref[at] = held[2 * at + 1 - side].astype(BF16)
        keep_ref[at] = held[2 * at + side]


def finish_kernel(mine_ref, other_ref, self_ref, neigh_ref, held):
    side = lax.axis_index("dom") % 2
    for at in range(mine_ref.shape[0]):
        held[2 * at + side] = mine_ref[at].astype(F32)
        held[2 * at + 1 - side] = other_ref[at].astype(F32)
    some = held.shape[1]
    half = held.shape[0] // 2
    for j in range(half):
        self_ref[j * some : (j + 1) * some] = held[j]
        neigh_ref[j * some : (j + 1) * some] = held[half + j]


def place_kernel(*refs):
    mine = lax.axis_index("feat")
    own_ref, *come_refs, out_ref = refs
    out_ref[mine] = own_ref[...]
    for mask, come in enumerate(come_refs, 1):
        out_ref[mine ^ mask] = come[out_ref.shape[0]]


def swap_feat(x):
    return lax.all_to_all(x, "feat", split_axis=0, concat_axis=0, tiled=True)


def crossed(x, mask, axis="dom"):
    return lax.ppermute(x, axis, [(i, i ^ mask) for i in range(lax.axis_size(axis))])


def like(shape, dtype):
    return jax.ShapeDtypeStruct(shape, dtype)


def dense_body(
    features,
    w_self,
    w_neigh,
    degree,
    local_vals,
    local_dst,
    local_src,
    remote_vals,
    remote_dst,
    remote_src,
    cotangent,
):
    rows, width = features.shape
    block = local_vals.shape[-1]
    nblocks = rows // block
    rounds = remote_vals.shape[1]
    parts_total = lax.axis_size("dom")
    feats = lax.axis_size("feat")
    some = rows // feats
    per_feat = nblocks // feats
    full = feats * width
    offsets = round_offsets(parts_total, rounds)
    near, far = 1, list(range(parts_total - 2, 0, -2))
    bits = [1, 2, 4]
    mine = lax.axis_index("feat").astype(jnp.int32)
    inverse = 1.0 / degree.astype(F32)
    inv_rows = lax.dynamic_slice(inverse, (mine * some,), (some,))[:, None]
    ids = (
        local_dst,
        local_src,
        jnp.swapaxes(remote_dst, 0, 1),
        jnp.swapaxes(remote_src, 0, 1),
    )
    shape = (nblocks, block, width)
    blocks = features.reshape(shape)
    fixed = (ids, local_vals[0], remote_vals[0])

    def forward(masks, arrays, sinks):
        return tiles_call(
            masks, offsets, parts_total, False, feats, fixed, arrays, sinks, 62
        )

    def relayed(x):
        over = crossed(x, 2, "feat")
        return [x, crossed(x, 1, "feat"), over, crossed(over, 1, "feat")]

    def tied(x, *others):
        return lax.optimization_barrier((x, others))[0]

    (send_7,) = forward([7], [blocks], [like(shape, BF16)])
    made = forward(
        [5, 3, 1],
        [tied(blocks, send_7), cotangent.reshape(shape), w_self, w_neigh],
        [like(shape, BF16)] * 3
        + [like((2, per_feat, block, width), BF16)] * feats
        + [like((2, width, full), BF16)],
    )
    sends, early_pieces, pair = [send_7, *made[:3]], list(made[3:-1]), made[-1]
    keep_6, keep_4, keep_2, keep = forward([6, 4, 2, 0], [blocks], [like(shape, F32)] * 4)
    weights = relayed(pair)
    near_6, near_4, near_2, near_0 = (crossed(send, near) for send in sends)
    sum_6 = (keep_6 + near_6.astype(F32)).astype(BF16)
    near_4 = tied(near_4, weights[2])
    sum_4 = (keep_4 + near_4.astype(F32) + crossed(sum_6, 2).astype(F32)).astype(BF16)
    far_0 = crossed(sum_4, 4)
    sum_2 = tied((tied(keep_2, sum_4) + near_2.astype(F32)).astype(BF16), far_0)
    mid_0 = crossed(sum_2, 2)
    early = [early_pieces[0]] + [crossed(early_pieces[m], m, "feat") for m in range(1, feats)]
    part = keep + near_0.astype(F32)
    arrived = [far_0, mid_0]
    arrived, early, weights = lax.optimization_barrier((arrived, early, weights))
    agg, *agg_pieces = small_call(
        functools.partial(agg_kernel, feats),
        [like(shape, BF16)] + [like((per_feat, block, width), BF16)] * feats,
        [inverse.reshape(nblocks, block, 1), part, *arrived],
    )
    agg_rows = [agg_pieces[0]] + [crossed(agg_pieces[m], m, "feat") for m in range(1, feats)]
    *sent, own_out, p0, p1, p2, p3 = small_call(
        functools.partial(dense_kernel, feats),
        [like((feats + 1, some, width), BF16)] * (feats - 1)
        + [like((some, width), BF16)] * (1 + feats),
        [inv_rows, *weights, *early, *agg_rows],
        [pltpu.VMEM((feats, some, width), BF16)],
    )
    dsum_pieces = [p0, p1, p2, p3]
    dsum = jnp.concatenate(
        [dsum_pieces[0]] + [crossed(dsum_pieces[m], m, "feat") for m in range(1, feats)], axis=0
    ).reshape(shape)
    found = {0: dsum}
    for mask in (4, 2, 1):
        found[mask] = crossed(dsum, mask)
    sent = tied(sent, dsum)
    sent[0] = tied(sent[0], found[4], found[2], found[1])
    come = [crossed(sent[m - 1], m, "feat") for m in range(1, feats)]
    (out,) = small_call(place_kernel, [like((feats, some, width), BF16)], [own_out, *come])
    come, found[4], found[2], found[1] = lax.optimization_barrier(
        (come, found[4], found[2], found[1])
    )
    dpre = [sent[0], *come]
    found[6] = crossed(found[4], 2)
    found[3] = crossed(found[2], near)
    found[5] = crossed(found[4], near)
    found[7] = crossed(found[6], near)
    piece = 2 * width // parts_total
    dx_self, give, keep = small_call(
        functools.partial(grad_kernel, feats),
        [
            like((rows, width), F32),
            like((len(far) + 1, piece, full), BF16),
            like((len(far) + 1, piece, full), F32),
        ],
        [features, agg.reshape(rows, width), w_self, *dpre],
        [pltpu.VMEM((parts_total, piece, full), F32)],
    )
    total = (keep + crossed(give, near).astype(F32)).astype(BF16)
    total = (total.astype(F32) + crossed(total, 2).astype(F32)).astype(BF16)
    total = tied(total, found[3], found[6])
    total = (total.astype(F32) + crossed(total, 4).astype(F32)).astype(BF16)
    total, out = tied((total, out), found[5], found[7])
    grad_self, grad_neigh = small_call(
        finish_kernel,
        [like((width, full), F32)] * 2,
        [total, crossed(total, near)],
        [pltpu.VMEM((parts_total, piece, full), F32)],
    )
    grad_x = dx_self.reshape(shape)
    half = parts_total // 2
    for order in (list(range(half)), list(range(half, parts_total))):
        grad_x = tiles_call(
            order,
            offsets,
            parts_total,
            True,
            feats,
            fixed,
            [found[mask] for mask in order] + [grad_x],
            like(shape, F32),
            24,
        )
    return (out.reshape(rows, width), grad_x.reshape(rows, width), grad_self, grad_neigh)


def solution(mesh):
    def body(*args):
        rounds = args[7].shape[1]
        small = mesh.shape["dom"] == 8 and mesh.shape["feat"] == 4
        nearly_all = mesh.shape["dom"] <= rounds + 2
        return (dense_body if small and nearly_all else sparse_body)(*args)

    placed = (
        P("dom", "feat"),
        P("feat", None),
        P("feat", None),
        P("dom"),
        P("dom", None, None, None),
        P("dom", None),
        P("dom", None),
        P("dom", None, None, None, None),
        P("dom", None, None),
        P("dom", None, None),
        P("dom", "feat"),
    )
    return jax.shard_map(
        body,
        mesh=mesh,
        in_specs=placed,
        out_specs=(P("dom", "feat"), P("dom", "feat"), P("feat", None), P("feat", None)),
        check_vma=False,
    )
```

```python
import functools

import jax
import jax.numpy as jnp
from jax import lax
from jax.experimental import pallas as pl
from jax.experimental.pallas import tpu as pltpu
from jax.sharding import PartitionSpec as P

F32 = jnp.float32
BF16 = jnp.bfloat16
VMEM = pl.BlockSpec(memory_space=pltpu.VMEM)
SMEM = pl.BlockSpec(memory_space=pltpu.SMEM)


def shifted(x, axis, by):
    devices = lax.axis_size(axis)
    return lax.ppermute(x, axis, [(i, (i + by) % devices) for i in range(devices)])


def spread(parts, block_ids, count):
    table = (block_ids[:, None] == jnp.arange(count, dtype=jnp.int32)[None, :]).astype(F32)
    return jnp.einsum("kc,kif->cif", table, parts, precision=lax.Precision.HIGHEST)


def tile_apply(tiles, blocks):
    return jnp.einsum("kij,kjf->kif", tiles, blocks, preferred_element_type=F32)


def tile_apply_back(tiles, blocks):
    return jnp.einsum("kji,kjf->kif", tiles, blocks, preferred_element_type=F32)


def round_offsets(parts_total, rounds):
    return [(step + 1) * parts_total // (rounds + 1) for step in range(rounds)]


def sparse_body(
    features,
    w_self,
    w_neigh,
    degree,
    local_vals,
    local_dst,
    local_src,
    remote_vals,
    remote_dst,
    remote_src,
    cotangent,
):
    rows, width = features.shape
    block = local_vals.shape[-1]
    nblocks = rows // block
    rounds = remote_vals.shape[1]
    parts_total = lax.axis_size("dom")
    offsets = round_offsets(parts_total, rounds)
    blocks = features.reshape(nblocks, block, width)
    totals = spread(
        tile_apply(local_vals[0], jnp.take(blocks, local_src[0], axis=0)), local_dst[0], nblocks
    )
    arrived_ids = []
    for step in range(rounds):
        partial_blocks = tile_apply(
            remote_vals[0, step], jnp.take(blocks, remote_src[0, step], axis=0)
        ).astype(BF16)
        arrived, block_ids = shifted((partial_blocks, remote_dst[0, step]), "dom", offsets[step])
        arrived_ids.append(block_ids)
        totals = totals + spread(arrived.astype(F32), block_ids, nblocks)
    inverse = 1.0 / degree.astype(F32)
    agg = (totals.reshape(rows, width) * inverse[:, None]).astype(BF16)
    stacked = jnp.concatenate([features, agg], axis=1)
    weights = jnp.concatenate([w_self, w_neigh], axis=0)
    pre = lax.psum_scatter(
        lax.dot_general(weights, stacked, (((0,), (1,)), ((), ())), preferred_element_type=F32),
        "feat",
        scatter_dimension=0,
        tiled=True,
    ).T
    sigma = jax.nn.sigmoid(pre)
    out = (pre * sigma).astype(BF16)
    dpre = (cotangent.astype(F32) * sigma * (1.0 + pre * (1.0 - sigma))).astype(BF16)
    dpre_all = lax.all_gather(dpre, "feat", axis=1, tiled=True)
    dz_total = lax.dot_general(
        dpre_all, weights, (((1,), (1,)), ((), ())), preferred_element_type=F32
    )
    grad_local = lax.dot_general(
        stacked, dpre_all, (((0,), (0,)), ((), ())), preferred_element_type=F32
    )
    dx_self = dz_total[:, :width]
    dsum = (dz_total[:, width:] * inverse[:, None]).astype(BF16).reshape(nblocks, block, width)
    grad_all = lax.psum(grad_local, "dom")
    back = spread(
        tile_apply_back(local_vals[0], jnp.take(dsum, local_dst[0], axis=0)), local_src[0], nblocks
    )
    for step in range(rounds):
        picked = jnp.take(dsum, arrived_ids[step], axis=0)
        returned = shifted(picked, "dom", parts_total - offsets[step])
        back = back + spread(
            tile_apply_back(remote_vals[0, step], returned), remote_src[0, step], nblocks
        )
    grad_x = dx_self + back.reshape(rows, width)
    return (out, grad_x, grad_all[:width], grad_all[width:])


def tile_counts(rvals, lvals):
    return rvals.shape[0], rvals.shape[1], lvals.shape[0]


def round_of(offset, offsets):
    step, known = jnp.int32(0), offset < 0
    for at, this in enumerate(offsets):
        step = jnp.where(offset == this, at, step)
        known = known | (offset == this)
    return step, known


def crossed_block(block_id, mine, per_feat):
    return ((block_id // per_feat) ^ mine) * per_feat + block_id % per_feat


def tile_groups(masks, offsets, parts_total, me, groups, tiles):
    jobs = []
    for at, mask in enumerate(masks):
        if mask == 0:
            for first in range(0, tiles, groups):
                count = min(groups, tiles - first)
                jobs.append((at, None, None, first, count))
        else:
            offset = lax.rem((me ^ mask) - me + parts_total, parts_total)
            step, known = round_of(offset, offsets)
            jobs.append((at, step, known, None, groups))
    return jobs


def flat(masks):
    return [m for group in masks for m in (group if isinstance(group, list) else [group])]


def tiles_kernel(masks, offsets, parts_total, back, feats, extras, *refs):
    ids_in, (lvals, rvals), refs = refs[:4], refs[4:6], refs[6:]
    ids, id_sems, refs = refs[-5:-1], refs[-1], refs[:-5]
    id_copies = [
        pltpu.make_async_copy(ids_in[n], ids[n], id_sems.at[n]) for n in range(len(ids))
    ]
    for copy in id_copies:
        copy.start()
    groups_of, masks = masks, flat(masks)
    me = lax.axis_index("dom")
    mine = lax.axis_index("feat")
    rounds, groups, tiles = tile_counts(rvals, lvals)
    jobs = tile_groups(masks, offsets, parts_total, me, groups, tiles)
    held, prod, acc, sems = refs[-4:]
    copies = []
    for slot, (at, step, known, first, count) in enumerate(jobs):
        source = lvals.at[pl.ds(first, count)] if step is None else rvals.at[step]
        copy = pltpu.make_async_copy(source, held.at[slot, pl.ds(0, count)], sems.at[slot])
        copy.start()
        copies.append(copy)
    if back:
        own_ref, grad_ref = refs[len(masks)], refs[len(masks) + 1]
        blocks = refs[: len(masks)]
        sinks = [grad_ref] * len(masks)
        acc[0] = own_ref[...]
    else:
        blocks = [refs[0]] * len(masks)
        sinks, used = [], 1 + extras
        for group in groups_of:
            if isinstance(group, list):
                sinks += [refs[used].at[n] for n in range(len(group))]
            else:
                sinks.append(refs[used])
            used += 1
    if extras:
        pieces, pair = refs[used : used + feats], refs[used + feats]
        pair[0] = refs[2][...]
        pair[1] = refs[3][...]
        for mask, piece in enumerate(pieces):
            rows = pl.ds((mine ^ mask) * piece.shape[1], piece.shape[1])
            piece[0] = refs[0][rows]
            piece[1] = refs[1][rows]
    total = 0
    for copy in id_copies:
        copy.wait()
    ldst, lsrc, rdst, rsrc = ids
    for slot, (at, step, known, first, count) in enumerate(jobs):
        copies[slot].wait()
        if step is None:
            dst = [ldst[0, first + k] for k in range(count)]
            src = [lsrc[0, first + k] for k in range(count)]
        else:
            dst = [rdst[step, 0, k] for k in range(count)]
            src = [rsrc[step, 0, k] for k in range(count)]
        half = slot % 2
        for k in range(len(dst)):
            if back:
                per_feat = blocks[at].shape[0] // feats
                block = blocks[at][crossed_block(dst[k], mine, per_feat)]
                product = lax.dot_general(
                    held[slot, k], block, (((0,), (0,)), ((), ())), preferred_element_type=F32
                )
            else:
                product = jnp.dot(
                    held[slot, k], blocks[at][src[k]], preferred_element_type=F32
                )
            prod[half, k] = product if known is None else jnp.where(known, product, 0.0)
        fresh = not back and (slot == 0 or jobs[slot - 1][0] != at)
        if fresh:
            total = at % 2
            acc[total] = jnp.zeros(acc.shape[1:], F32)
        for k in range(len(dst)):
            into = src[k] if back else dst[k]
            acc[total, into] = acc[total, into] + prod[half, k]
        last = slot == len(jobs) - 1 or jobs[slot + 1][0] != at
        if last and (not back or slot == len(jobs) - 1):
            sinks[at][...] = acc[total].astype(sinks[at].dtype)


def tiles_call(masks, offsets, parts_total, back, feats, fixed, blocks, sinks, room):
    ids, lvals, rvals = fixed
    rounds, groups, tiles = tile_counts(rvals, lvals)
    nblocks, block, width = blocks[0].shape
    slots = sum(-(-tiles // groups) if mask == 0 else 1 for mask in flat(masks))
    extras = 0 if back else len(blocks) - 1
    return pl.pallas_call(
        functools.partial(tiles_kernel, masks, offsets, parts_total, back, feats, extras),
        out_shape=sinks,
        in_specs=[pl.BlockSpec(memory_space=pltpu.HBM)] * 6
        + [VMEM] * len(blocks),
        out_specs=jax.tree.map(lambda _: VMEM, sinks),
        scratch_shapes=[
            pltpu.VMEM((slots, groups, block, block), BF16),
            pltpu.VMEM((2, groups, block, width), F32),
            pltpu.VMEM((2, nblocks, block, width), F32),
            pltpu.SemaphoreType.DMA((slots,)),
            *[pltpu.SMEM(t.shape, jnp.int32) for t in ids],
            pltpu.SemaphoreType.DMA((len(ids),)),
        ],
        compiler_params=pltpu.CompilerParams(vmem_limit_bytes=room * 2**20),
        cost_estimate=pl.CostEstimate(flops=1, bytes_accessed=1, transcendentals=0),
    )(*ids, lvals, rvals, *blocks)


def small_call(kernel, outs, arrays, scratch=(), room=24):
    return pl.pallas_call(
        kernel,
        out_shape=outs,
        in_specs=[VMEM] * len(arrays),
        out_specs=[VMEM] * len(outs),
        scratch_shapes=scratch,
        compiler_params=pltpu.CompilerParams(vmem_limit_bytes=room * 2**20),
        cost_estimate=pl.CostEstimate(flops=1, bytes_accessed=1, transcendentals=0),
    )(*arrays)


def agg_kernel(feats, inv_ref, keep_ref, *refs):
    mine = lax.axis_index("feat")
    far_refs, agg_ref, piece_refs = refs[: -1 - feats], refs[-1 - feats], refs[-feats:]
    per_feat = piece_refs[0].shape[0]
    sums = keep_ref[...]
    for ref in far_refs:
        sums = sums + ref[...].astype(F32)
    agg_ref[...] = (sums * inv_ref[...]).astype(BF16)
    for mask, piece in enumerate(piece_refs):
        piece[...] = agg_ref[pl.ds((mine ^ mask) * per_feat, per_feat)]


def joined(parts):
    return jnp.concatenate(parts, axis=1)


def dense_kernel(feats, inv_ref, *refs):
    mine = lax.axis_index("feat")
    w_refs, early_refs, a_refs = refs[:feats], refs[feats : 2 * feats], refs[2 * feats : 3 * feats]
    sent_refs, own_ref = refs[3 * feats : 4 * feats - 1], refs[4 * feats - 1]
    dsum_refs = refs[4 * feats : 5 * feats]
    held = refs[-1]
    full = w_refs[0].shape[2]
    some, width = held.shape[1:]
    pre = jnp.zeros((some, full), F32)
    for mask in range(feats):
        early = early_refs[mask]
        pre = pre + jnp.dot(
            early[0].reshape(some, width), w_refs[mask][0], preferred_element_type=F32
        )
        pre = pre + jnp.dot(
            a_refs[mask][...].reshape(some, width), w_refs[mask][1], preferred_element_type=F32
        )
        held[mine ^ mask] = early[1].reshape(some, width)
    sigma = 1.0 / (1.0 + jnp.exp(-pre))
    out = (pre * sigma).astype(BF16)
    cot = joined([held[j] for j in range(feats)]).astype(F32)
    dpre = (cot * sigma * (1.0 + pre * (1.0 - sigma))).astype(BF16)
    for mask in range(feats):
        dagg = lax.dot_general(
            dpre, w_refs[mask][1], (((1,), (1,)), ((), ())), preferred_element_type=F32
        )
        dsum_refs[mask][...] = (dagg * inv_ref[...]).astype(BF16)
    for j in range(feats):
        cols = slice(j * width, (j + 1) * width)
        for sent in sent_refs:
            sent[j] = dpre[:, cols]
        held[j] = out[:, cols]
    own_ref[...] = held[mine]
    for mask, sent in enumerate(sent_refs, 1):
        sent[feats] = held[mine ^ mask]


def grad_kernel(feats, f_ref, a_ref, w_ref, *refs):
    me = lax.axis_index("dom")
    mine = lax.axis_index("feat")
    dpre_refs, (dx_ref, give_ref, keep_ref, held) = refs[:feats], refs[feats:]
    width = f_ref.shape[1]
    piece = held.shape[1]
    some = dpre_refs[0].shape[1]
    parts = [0.0, 0.0]
    for mask, dpre_ref in enumerate(dpre_refs):
        dpre = joined([dpre_ref[j] for j in range(feats)])
        rows = pl.ds(pl.multiple_of((mine ^ mask) * some, some), some)
        for at, ref in enumerate((f_ref, a_ref)):
            parts[at] = parts[at] + lax.dot_general(
                ref[rows], dpre, (((0,), (0,)), ((), ())), preferred_element_type=F32
            )
        dx_ref[rows] = lax.dot_general(
            dpre, w_ref[...], (((1,), (1,)), ((), ())), preferred_element_type=F32
        )
    for at, part in enumerate(parts):
        for j in range(width // piece):
            held[at * (width // piece) + j] = part[j * piece : (j + 1) * piece]
    side = me % 2
    for at in range(give_ref.shape[0]):
        give_ref[at] = held[2 * at + 1 - side].astype(BF16)
        keep_ref[at] = held[2 * at + side]


def finish_kernel(mine_ref, other_ref, self_ref, neigh_ref, held):
    side = lax.axis_index("dom") % 2
    for at in range(mine_ref.shape[0]):
        held[2 * at + side] = mine_ref[at].astype(F32)
        held[2 * at + 1 - side] = other_ref[at].astype(F32)
    some = held.shape[1]
    half = held.shape[0] // 2
    for j in range(half):
        self_ref[j * some : (j + 1) * some] = held[j]
        neigh_ref[j * some : (j + 1) * some] = held[half + j]


def place_kernel(*refs):
    mine = lax.axis_index("feat")
    own_ref, *come_refs, out_ref = refs
    out_ref[mine] = own_ref[...]
    for mask, come in enumerate(come_refs, 1):
        out_ref[mine ^ mask] = come[out_ref.shape[0]]


def swap_feat(x):
    return lax.all_to_all(x, "feat", split_axis=0, concat_axis=0, tiled=True)


def crossed(x, mask, axis="dom"):
    return lax.ppermute(x, axis, [(i, i ^ mask) for i in range(lax.axis_size(axis))])


def like(shape, dtype):
    return jax.ShapeDtypeStruct(shape, dtype)


def dense_body(
    features,
    w_self,
    w_neigh,
    degree,
    local_vals,
    local_dst,
    local_src,
    remote_vals,
    remote_dst,
    remote_src,
    cotangent,
):
    rows, width = features.shape
    block = local_vals.shape[-1]
    nblocks = rows // block
    rounds = remote_vals.shape[1]
    parts_total = lax.axis_size("dom")
    feats = lax.axis_size("feat")
    some = rows // feats
    per_feat = nblocks // feats
    full = feats * width
    offsets = round_offsets(parts_total, rounds)
    near, far = 1, list(range(parts_total - 2, 0, -2))
    bits = [1, 2, 4]
    mine = lax.axis_index("feat").astype(jnp.int32)
    inverse = 1.0 / degree.astype(F32)
    inv_rows = lax.dynamic_slice(inverse, (mine * some,), (some,))[:, None]
    ids = (
        local_dst,
        local_src,
        jnp.swapaxes(remote_dst, 0, 1),
        jnp.swapaxes(remote_src, 0, 1),
    )
    shape = (nblocks, block, width)
    blocks = features.reshape(shape)
    fixed = (ids, local_vals[0], remote_vals[0])

    def forward(masks, arrays, sinks):
        return tiles_call(
            masks, offsets, parts_total, False, feats, fixed, arrays, sinks, 62
        )

    def relayed(x):
        over = crossed(x, 2, "feat")
        return [x, crossed(x, 1, "feat"), over, crossed(over, 1, "feat")]

    def tied(x, *others):
        return lax.optimization_barrier((x, others))[0]

    sends = forward([7, 3, 5, 1], [blocks], [like(shape, BF16)] * 4)
    made = forward(
        [6, 2, 4, 0],
        [blocks, cotangent.reshape(shape), w_self, w_neigh],
        [like(shape, F32)] * 4
        + [like((2, per_feat, block, width), BF16)] * feats
        + [like((2, width, full), BF16)],
    )
    keep_6, keep_2, keep_4, keep = made[:4]
    early_pieces, pair = made[4:-1], made[-1]
    weights = relayed(pair)
    early = [early_pieces[0]] + [crossed(early_pieces[m], m, "feat") for m in range(1, feats)]
    near_6, near_2, near_4, near_0 = (crossed(send, near) for send in sends)
    sum_6 = (keep_6 + near_6.astype(F32)).astype(BF16)
    sum_2 = (keep_2 + near_2.astype(F32)).astype(BF16)
    mid_0 = crossed(sum_2, 2)
    near_4, mid_0, weights[2] = lax.optimization_barrier((near_4, mid_0, weights[2]))
    sum_4 = (keep_4 + near_4.astype(F32) + crossed(sum_6, 2).astype(F32)).astype(BF16)
    far_0 = crossed(sum_4, 4)
    part = keep + mid_0.astype(F32)
    arrived = [far_0, near_0]
    early, weights, arrived = lax.optimization_barrier((early, weights, arrived))
    agg, *agg_pieces = small_call(
        functools.partial(agg_kernel, feats),
        [like(shape, BF16)] + [like((per_feat, block, width), BF16)] * feats,
        [inverse.reshape(nblocks, block, 1), part, *arrived],
    )
    agg_rows = [agg_pieces[0]] + [crossed(agg_pieces[m], m, "feat") for m in range(1, feats)]
    *sent, own_out, p0, p1, p2, p3 = small_call(
        functools.partial(dense_kernel, feats),
        [like((feats + 1, some, width), BF16)] * (feats - 1)
        + [like((some, width), BF16)] * (1 + feats),
        [inv_rows, *weights, *early, *agg_rows],
        [pltpu.VMEM((feats, some, width), BF16)],
    )
    dsum_pieces = [p0, p1, p2, p3]
    dsum = jnp.concatenate(
        [dsum_pieces[0]] + [crossed(dsum_pieces[m], m, "feat") for m in range(1, feats)], axis=0
    ).reshape(shape)
    found = {0: dsum}
    for mask in (4, 2, 1):
        found[mask] = crossed(dsum, mask)
    sent = tied(sent, dsum)
    sent[0] = tied(sent[0], found[4], found[2], found[1])
    come = [crossed(sent[m - 1], m, "feat") for m in range(1, feats)]
    (out,) = small_call(place_kernel, [like((feats, some, width), BF16)], [own_out, *come])
    come, found[4], found[2], found[1] = lax.optimization_barrier(
        (come, found[4], found[2], found[1])
    )
    dpre = [sent[0], *come]
    found[6] = crossed(found[4], 2)
    found[3] = crossed(found[2], near)
    found[5] = crossed(found[4], near)
    found[7] = crossed(found[5], 2)
    piece = 2 * width // parts_total
    dx_self, give, keep = small_call(
        functools.partial(grad_kernel, feats),
        [
            like((rows, width), F32),
            like((len(far) + 1, piece, full), BF16),
            like((len(far) + 1, piece, full), F32),
        ],
        [features, agg.reshape(rows, width), w_self, *dpre],
        [pltpu.VMEM((parts_total, piece, full), F32)],
    )
    total = (keep + crossed(give, near).astype(F32)).astype(BF16)
    total = tied(total, found[5], found[6])
    total = (total.astype(F32) + crossed(total, 2).astype(F32)).astype(BF16)
    total = tied(total, found[3], found[7])
    total = (total.astype(F32) + crossed(total, 4).astype(F32)).astype(BF16)
    grad_x = dx_self.reshape(shape)
    half = parts_total // 2
    for order in (list(range(half)), list(range(half, parts_total))):
        grad_x = tiles_call(
            order,
            offsets,
            parts_total,
            True,
            feats,
            fixed,
            [found[mask] for mask in order] + [grad_x],
            like(shape, F32),
            24,
        )
    total, out, grad_x = lax.optimization_barrier((total, out, grad_x))
    grad_self, grad_neigh = small_call(
        finish_kernel,
        [like((width, full), F32)] * 2,
        [total, crossed(total, near)],
        [pltpu.VMEM((parts_total, piece, full), F32)],
    )
    return (out.reshape(rows, width), grad_x.reshape(rows, width), grad_self, grad_neigh)


def solution(mesh):
    def body(*args):
        rounds = args[7].shape[1]
        small = mesh.shape["dom"] == 8 and mesh.shape["feat"] == 4
        nearly_all = mesh.shape["dom"] <= rounds + 2
        return (dense_body if small and nearly_all else sparse_body)(*args)

    placed = (
        P("dom", "feat"),
        P("feat", None),
        P("feat", None),
        P("dom"),
        P("dom", None, None, None),
        P("dom", None),
        P("dom", None),
        P("dom", None, None, None, None),
        P("dom", None, None),
        P("dom", None, None),
        P("dom", "feat"),
    )
    return jax.shard_map(
        body,
        mesh=mesh,
        in_specs=placed,
        out_specs=(P("dom", "feat"), P("dom", "feat"), P("feat", None), P("feat", None)),
        check_vma=False,
    )
```

```python
import functools

import jax
import jax.numpy as jnp
from jax import lax
from jax.experimental import pallas as pl
from jax.experimental.pallas import tpu as pltpu
from jax.sharding import PartitionSpec as P

F32 = jnp.float32
BF16 = jnp.bfloat16
VMEM = pl.BlockSpec(memory_space=pltpu.VMEM)
SMEM = pl.BlockSpec(memory_space=pltpu.SMEM)


def shifted(x, axis, by):
    devices = lax.axis_size(axis)
    return lax.ppermute(x, axis, [(i, (i + by) % devices) for i in range(devices)])


def spread(parts, block_ids, count):
    table = (block_ids[:, None] == jnp.arange(count, dtype=jnp.int32)[None, :]).astype(F32)
    return jnp.einsum("kc,kif->cif", table, parts, precision=lax.Precision.HIGHEST)


def tile_apply(tiles, blocks):
    return jnp.einsum("kij,kjf->kif", tiles, blocks, preferred_element_type=F32)


def tile_apply_back(tiles, blocks):
    return jnp.einsum("kji,kjf->kif", tiles, blocks, preferred_element_type=F32)


def round_offsets(parts_total, rounds):
    return [(step + 1) * parts_total // (rounds + 1) for step in range(rounds)]


def sparse_body(
    features,
    w_self,
    w_neigh,
    degree,
    local_vals,
    local_dst,
    local_src,
    remote_vals,
    remote_dst,
    remote_src,
    cotangent,
):
    rows, width = features.shape
    block = local_vals.shape[-1]
    nblocks = rows // block
    rounds = remote_vals.shape[1]
    parts_total = lax.axis_size("dom")
    offsets = round_offsets(parts_total, rounds)
    blocks = features.reshape(nblocks, block, width)
    totals = spread(
        tile_apply(local_vals[0], jnp.take(blocks, local_src[0], axis=0)), local_dst[0], nblocks
    )
    arrived_ids = []
    for step in range(rounds):
        partial_blocks = tile_apply(
            remote_vals[0, step], jnp.take(blocks, remote_src[0, step], axis=0)
        ).astype(BF16)
        arrived, block_ids = shifted((partial_blocks, remote_dst[0, step]), "dom", offsets[step])
        arrived_ids.append(block_ids)
        totals = totals + spread(arrived.astype(F32), block_ids, nblocks)
    inverse = 1.0 / degree.astype(F32)
    agg = (totals.reshape(rows, width) * inverse[:, None]).astype(BF16)
    stacked = jnp.concatenate([features, agg], axis=1)
    weights = jnp.concatenate([w_self, w_neigh], axis=0)
    pre = lax.psum_scatter(
        lax.dot_general(weights, stacked, (((0,), (1,)), ((), ())), preferred_element_type=F32),
        "feat",
        scatter_dimension=0,
        tiled=True,
    ).T
    sigma = jax.nn.sigmoid(pre)
    out = (pre * sigma).astype(BF16)
    dpre = (cotangent.astype(F32) * sigma * (1.0 + pre * (1.0 - sigma))).astype(BF16)
    dpre_all = lax.all_gather(dpre, "feat", axis=1, tiled=True)
    dz_total = lax.dot_general(
        dpre_all, weights, (((1,), (1,)), ((), ())), preferred_element_type=F32
    )
    grad_local = lax.dot_general(
        stacked, dpre_all, (((0,), (0,)), ((), ())), preferred_element_type=F32
    )
    dx_self = dz_total[:, :width]
    dsum = (dz_total[:, width:] * inverse[:, None]).astype(BF16).reshape(nblocks, block, width)
    grad_all = lax.psum(grad_local, "dom")
    back = spread(
        tile_apply_back(local_vals[0], jnp.take(dsum, local_dst[0], axis=0)), local_src[0], nblocks
    )
    for step in range(rounds):
        picked = jnp.take(dsum, arrived_ids[step], axis=0)
        returned = shifted(picked, "dom", parts_total - offsets[step])
        back = back + spread(
            tile_apply_back(remote_vals[0, step], returned), remote_src[0, step], nblocks
        )
    grad_x = dx_self + back.reshape(rows, width)
    return (out, grad_x, grad_all[:width], grad_all[width:])


def tile_counts(rvals, lvals):
    return rvals.shape[0], rvals.shape[1], lvals.shape[0]


def round_of(offset, offsets):
    step, known = jnp.int32(0), offset < 0
    for at, this in enumerate(offsets):
        step = jnp.where(offset == this, at, step)
        known = known | (offset == this)
    return step, known


def crossed_block(block_id, mine, per_feat):
    return ((block_id // per_feat) ^ mine) * per_feat + block_id % per_feat


def tile_groups(masks, offsets, parts_total, me, groups, tiles):
    jobs = []
    for at, mask in enumerate(masks):
        if mask == 0:
            for first in range(0, tiles, groups):
                count = min(groups, tiles - first)
                jobs.append((at, None, None, first, count))
        else:
            offset = lax.rem((me ^ mask) - me + parts_total, parts_total)
            step, known = round_of(offset, offsets)
            jobs.append((at, step, known, None, groups))
    return jobs


def flat(masks):
    return [m for group in masks for m in (group if isinstance(group, list) else [group])]


def tiles_kernel(masks, offsets, parts_total, back, feats, extras, *refs):
    ids_in, (lvals, rvals), refs = refs[:4], refs[4:6], refs[6:]
    ids, id_sems, refs = refs[-5:-1], refs[-1], refs[:-5]
    id_copies = [
        pltpu.make_async_copy(ids_in[n], ids[n], id_sems.at[n]) for n in range(len(ids))
    ]
    for copy in id_copies:
        copy.start()
    groups_of, masks = masks, flat(masks)
    me = lax.axis_index("dom")
    mine = lax.axis_index("feat")
    rounds, groups, tiles = tile_counts(rvals, lvals)
    jobs = tile_groups(masks, offsets, parts_total, me, groups, tiles)
    held, prod, acc, sems = refs[-4:]
    copies = []
    for slot, (at, step, known, first, count) in enumerate(jobs):
        source = lvals.at[pl.ds(first, count)] if step is None else rvals.at[step]
        copy = pltpu.make_async_copy(source, held.at[slot, pl.ds(0, count)], sems.at[slot])
        copy.start()
        copies.append(copy)
    if back:
        own_ref, grad_ref = refs[len(masks)], refs[len(masks) + 1]
        blocks = refs[: len(masks)]
        sinks = [grad_ref] * len(masks)
        acc[0] = own_ref[...]
    else:
        blocks = [refs[0]] * len(masks)
        sinks, used = [], 1 + extras
        for group in groups_of:
            if isinstance(group, list):
                sinks += [refs[used].at[n] for n in range(len(group))]
            else:
                sinks.append(refs[used])
            used += 1
    if extras:
        pieces, pair = refs[used : used + feats], refs[used + feats]
        pair[0] = refs[2][...]
        pair[1] = refs[3][...]
        for mask, piece in enumerate(pieces):
            rows = pl.ds((mine ^ mask) * piece.shape[1], piece.shape[1])
            piece[0] = refs[0][rows]
            piece[1] = refs[1][rows]
    total = 0
    for copy in id_copies:
        copy.wait()
    ldst, lsrc, rdst, rsrc = ids
    for slot, (at, step, known, first, count) in enumerate(jobs):
        copies[slot].wait()
        if step is None:
            dst = [ldst[0, first + k] for k in range(count)]
            src = [lsrc[0, first + k] for k in range(count)]
        else:
            dst = [rdst[step, 0, k] for k in range(count)]
            src = [rsrc[step, 0, k] for k in range(count)]
        half = slot % 2
        for k in range(len(dst)):
            if back:
                per_feat = blocks[at].shape[0] // feats
                block = blocks[at][crossed_block(dst[k], mine, per_feat)]
                product = lax.dot_general(
                    held[slot, k], block, (((0,), (0,)), ((), ())), preferred_element_type=F32
                )
            else:
                product = jnp.dot(
                    held[slot, k], blocks[at][src[k]], preferred_element_type=F32
                )
            prod[half, k] = product if known is None else jnp.where(known, product, 0.0)
        fresh = not back and (slot == 0 or jobs[slot - 1][0] != at)
        if fresh:
            total = at % 2
            acc[total] = jnp.zeros(acc.shape[1:], F32)
        for k in range(len(dst)):
            into = src[k] if back else dst[k]
            acc[total, into] = acc[total, into] + prod[half, k]
        last = slot == len(jobs) - 1 or jobs[slot + 1][0] != at
        if last and (not back or slot == len(jobs) - 1):
            sinks[at][...] = acc[total].astype(sinks[at].dtype)


def tiles_call(masks, offsets, parts_total, back, feats, fixed, blocks, sinks, room):
    ids, lvals, rvals = fixed
    rounds, groups, tiles = tile_counts(rvals, lvals)
    nblocks, block, width = blocks[0].shape
    slots = sum(-(-tiles // groups) if mask == 0 else 1 for mask in flat(masks))
    extras = 0 if back else len(blocks) - 1
    return pl.pallas_call(
        functools.partial(tiles_kernel, masks, offsets, parts_total, back, feats, extras),
        out_shape=sinks,
        in_specs=[pl.BlockSpec(memory_space=pltpu.HBM)] * 6
        + [VMEM] * len(blocks),
        out_specs=jax.tree.map(lambda _: VMEM, sinks),
        scratch_shapes=[
            pltpu.VMEM((slots, groups, block, block), BF16),
            pltpu.VMEM((2, groups, block, width), F32),
            pltpu.VMEM((2, nblocks, block, width), F32),
            pltpu.SemaphoreType.DMA((slots,)),
            *[pltpu.SMEM(t.shape, jnp.int32) for t in ids],
            pltpu.SemaphoreType.DMA((len(ids),)),
        ],
        compiler_params=pltpu.CompilerParams(vmem_limit_bytes=room * 2**20),
        cost_estimate=pl.CostEstimate(flops=1, bytes_accessed=1, transcendentals=0),
    )(*ids, lvals, rvals, *blocks)


def small_call(kernel, outs, arrays, scratch=(), room=24):
    return pl.pallas_call(
        kernel,
        out_shape=outs,
        in_specs=[VMEM] * len(arrays),
        out_specs=[VMEM] * len(outs),
        scratch_shapes=scratch,
        compiler_params=pltpu.CompilerParams(vmem_limit_bytes=room * 2**20),
        cost_estimate=pl.CostEstimate(flops=1, bytes_accessed=1, transcendentals=0),
    )(*arrays)


def agg_kernel(feats, inv_ref, keep_ref, *refs):
    mine = lax.axis_index("feat")
    far_refs, agg_ref, piece_refs = refs[: -1 - feats], refs[-1 - feats], refs[-feats:]
    per_feat = piece_refs[0].shape[0]
    sums = keep_ref[...]
    for ref in far_refs:
        sums = sums + ref[...].astype(F32)
    agg_ref[...] = (sums * inv_ref[...]).astype(BF16)
    for mask, piece in enumerate(piece_refs):
        piece[...] = agg_ref[pl.ds((mine ^ mask) * per_feat, per_feat)]


def joined(parts):
    return jnp.concatenate(parts, axis=1)


def dense_kernel(feats, inv_ref, *refs):
    mine = lax.axis_index("feat")
    w_refs, early_refs, a_refs = refs[:feats], refs[feats : 2 * feats], refs[2 * feats : 3 * feats]
    sent_refs, own_ref = refs[3 * feats : 4 * feats - 1], refs[4 * feats - 1]
    dsum_refs = refs[4 * feats : 5 * feats]
    held = refs[-1]
    full = w_refs[0].shape[2]
    some, width = held.shape[1:]
    pre = jnp.zeros((some, full), F32)
    for mask in range(feats):
        early = early_refs[mask]
        pre = pre + jnp.dot(
            early[0].reshape(some, width), w_refs[mask][0], preferred_element_type=F32
        )
        pre = pre + jnp.dot(
            a_refs[mask][...].reshape(some, width), w_refs[mask][1], preferred_element_type=F32
        )
        held[mine ^ mask] = early[1].reshape(some, width)
    sigma = 1.0 / (1.0 + jnp.exp(-pre))
    out = (pre * sigma).astype(BF16)
    cot = joined([held[j] for j in range(feats)]).astype(F32)
    dpre = (cot * sigma * (1.0 + pre * (1.0 - sigma))).astype(BF16)
    for mask in range(feats):
        dagg = lax.dot_general(
            dpre, w_refs[mask][1], (((1,), (1,)), ((), ())), preferred_element_type=F32
        )
        dsum_refs[mask][...] = (dagg * inv_ref[...]).astype(BF16)
    for j in range(feats):
        cols = slice(j * width, (j + 1) * width)
        for sent in sent_refs:
            sent[j] = dpre[:, cols]
        held[j] = out[:, cols]
    own_ref[...] = held[mine]
    for mask, sent in enumerate(sent_refs, 1):
        sent[feats] = held[mine ^ mask]


def grad_kernel(feats, f_ref, a_ref, w_ref, *refs):
    me = lax.axis_index("dom")
    mine = lax.axis_index("feat")
    dpre_refs, (dx_ref, give_ref, keep_ref, held) = refs[:feats], refs[feats:]
    width = f_ref.shape[1]
    piece = held.shape[1]
    some = dpre_refs[0].shape[1]
    parts = [0.0, 0.0]
    for mask, dpre_ref in enumerate(dpre_refs):
        dpre = joined([dpre_ref[j] for j in range(feats)])
        rows = pl.ds(pl.multiple_of((mine ^ mask) * some, some), some)
        for at, ref in enumerate((f_ref, a_ref)):
            parts[at] = parts[at] + lax.dot_general(
                ref[rows], dpre, (((0,), (0,)), ((), ())), preferred_element_type=F32
            )
        dx_ref[rows] = lax.dot_general(
            dpre, w_ref[...], (((1,), (1,)), ((), ())), preferred_element_type=F32
        )
    for at, part in enumerate(parts):
        for j in range(width // piece):
            held[at * (width // piece) + j] = part[j * piece : (j + 1) * piece]
    side = me % 2
    for at in range(give_ref.shape[0]):
        give_ref[at] = held[2 * at + 1 - side].astype(BF16)
        keep_ref[at] = held[2 * at + side]


def finish_kernel(mine_ref, other_ref, self_ref, neigh_ref, held):
    side = lax.axis_index("dom") % 2
    for at in range(mine_ref.shape[0]):
        held[2 * at + side] = mine_ref[at].astype(F32)
        held[2 * at + 1 - side] = other_ref[at].astype(F32)
    some = held.shape[1]
    half = held.shape[0] // 2
    for j in range(half):
        self_ref[j * some : (j + 1) * some] = held[j]
        neigh_ref[j * some : (j + 1) * some] = held[half + j]


def place_kernel(*refs):
    mine = lax.axis_index("feat")
    own_ref, *come_refs, out_ref = refs
    out_ref[mine] = own_ref[...]
    for mask, come in enumerate(come_refs, 1):
        out_ref[mine ^ mask] = come[out_ref.shape[0]]


def swap_feat(x):
    return lax.all_to_all(x, "feat", split_axis=0, concat_axis=0, tiled=True)


def crossed(x, mask, axis="dom"):
    return lax.ppermute(x, axis, [(i, i ^ mask) for i in range(lax.axis_size(axis))])


def like(shape, dtype):
    return jax.ShapeDtypeStruct(shape, dtype)


def dense_body(
    features,
    w_self,
    w_neigh,
    degree,
    local_vals,
    local_dst,
    local_src,
    remote_vals,
    remote_dst,
    remote_src,
    cotangent,
):
    rows, width = features.shape
    block = local_vals.shape[-1]
    nblocks = rows // block
    rounds = remote_vals.shape[1]
    parts_total = lax.axis_size("dom")
    feats = lax.axis_size("feat")
    some = rows // feats
    per_feat = nblocks // feats
    full = feats * width
    offsets = round_offsets(parts_total, rounds)
    near, far = 1, list(range(parts_total - 2, 0, -2))
    bits = [1, 2, 4]
    mine = lax.axis_index("feat").astype(jnp.int32)
    inverse = 1.0 / degree.astype(F32)
    inv_rows = lax.dynamic_slice(inverse, (mine * some,), (some,))[:, None]
    ids = (
        local_dst,
        local_src,
        jnp.swapaxes(remote_dst, 0, 1),
        jnp.swapaxes(remote_src, 0, 1),
    )
    shape = (nblocks, block, width)
    blocks = features.reshape(shape)
    fixed = (ids, local_vals[0], remote_vals[0])

    def forward(masks, arrays, sinks):
        return tiles_call(
            masks, offsets, parts_total, False, feats, fixed, arrays, sinks, 62
        )

    def relayed(x):
        over = crossed(x, 2, "feat")
        return [x, crossed(x, 1, "feat"), over, crossed(over, 1, "feat")]

    def tied(x, *others):
        return lax.optimization_barrier((x, others))[0]

    sends = forward([7, 3, 5, 1], [blocks], [like(shape, BF16)] * 4)
    made = forward(
        [6, 2, 4, 0],
        [blocks, cotangent.reshape(shape), w_self, w_neigh],
        [like(shape, F32)] * 4
        + [like((2, per_feat, block, width), BF16)] * feats
        + [like((2, width, full), BF16)],
    )
    keep_6, keep_2, keep_4, keep = made[:4]
    early_pieces, pair = made[4:-1], made[-1]
    weights = relayed(pair)
    early = [early_pieces[0]] + [crossed(early_pieces[m], m, "feat") for m in range(1, feats)]
    near_6, near_2, near_4, near_0 = (crossed(send, near) for send in sends)
    sum_6 = (keep_6 + near_6.astype(F32)).astype(BF16)
    sum_2 = (keep_2 + near_2.astype(F32)).astype(BF16)
    mid_0 = crossed(sum_2, 2)
    near_4, weights[2] = lax.optimization_barrier((tied(near_4, sum_2), weights[2]))
    sum_4 = (keep_4 + near_4.astype(F32) + crossed(sum_6, 2).astype(F32)).astype(BF16)
    far_0 = crossed(sum_4, 4)
    part = keep + near_0.astype(F32)
    arrived = [far_0, mid_0]
    early, weights, arrived = lax.optimization_barrier((early, weights, arrived))
    agg, *agg_pieces = small_call(
        functools.partial(agg_kernel, feats),
        [like(shape, BF16)] + [like((per_feat, block, width), BF16)] * feats,
        [inverse.reshape(nblocks, block, 1), part, *arrived],
    )
    agg_rows = [agg_pieces[0]] + [crossed(agg_pieces[m], m, "feat") for m in range(1, feats)]
    *sent, own_out, p0, p1, p2, p3 = small_call(
        functools.partial(dense_kernel, feats),
        [like((feats + 1, some, width), BF16)] * (feats - 1)
        + [like((some, width), BF16)] * (1 + feats),
        [inv_rows, *weights, *early, *agg_rows],
        [pltpu.VMEM((feats, some, width), BF16)],
    )
    dsum_pieces = [p0, p1, p2, p3]
    dsum = jnp.concatenate(
        [dsum_pieces[0]] + [crossed(dsum_pieces[m], m, "feat") for m in range(1, feats)], axis=0
    ).reshape(shape)
    found = {0: dsum}
    for mask in (4, 2, 1):
        found[mask] = crossed(dsum, mask)
    sent = tied(sent, dsum)
    come_2, come_3 = crossed(sent[1], 2, "feat"), crossed(sent[2], 3, "feat")
    come_2, come_3, found[4], found[2], found[1], sent[0] = lax.optimization_barrier(
        (come_2, come_3, found[4], found[2], found[1], sent[0])
    )
    come = [crossed(sent[0], 1, "feat"), come_2, come_3]
    (out,) = small_call(place_kernel, [like((feats, some, width), BF16)], [own_out, *come])
    dpre = [sent[0], *come]
    found[6] = crossed(found[4], 2)
    found[3] = crossed(found[2], near)
    found[5] = crossed(found[4], near)
    found[7] = crossed(found[5], 2)
    piece = 2 * width // parts_total
    dx_self, give, keep = small_call(
        functools.partial(grad_kernel, feats),
        [
            like((rows, width), F32),
            like((len(far) + 1, piece, full), BF16),
            like((len(far) + 1, piece, full), F32),
        ],
        [features, agg.reshape(rows, width), w_self, *dpre],
        [pltpu.VMEM((parts_total, piece, full), F32)],
    )
    total = (keep + crossed(give, near).astype(F32)).astype(BF16)
    total = (total.astype(F32) + crossed(total, 2).astype(F32)).astype(BF16)
    total = tied(total, found[5], found[6])
    total = (total.astype(F32) + crossed(total, 4).astype(F32)).astype(BF16)
    grad_x = dx_self.reshape(shape)
    half = parts_total // 2
    for order in (list(range(half)), list(range(half, parts_total))):
        grad_x = tiles_call(
            order,
            offsets,
            parts_total,
            True,
            feats,
            fixed,
            [found[mask] for mask in order] + [grad_x],
            like(shape, F32),
            24,
        )
    total, out = tied((total, out), found[3], found[7])
    grad_self, grad_neigh = small_call(
        finish_kernel,
        [like((width, full), F32)] * 2,
        [total, crossed(total, near)],
        [pltpu.VMEM((parts_total, piece, full), F32)],
    )
    return (out.reshape(rows, width), grad_x.reshape(rows, width), grad_self, grad_neigh)


def solution(mesh):
    def body(*args):
        rounds = args[7].shape[1]
        small = mesh.shape["dom"] == 8 and mesh.shape["feat"] == 4
        nearly_all = mesh.shape["dom"] <= rounds + 2
        return (dense_body if small and nearly_all else sparse_body)(*args)

    placed = (
        P("dom", "feat"),
        P("feat", None),
        P("feat", None),
        P("dom"),
        P("dom", None, None, None),
        P("dom", None),
        P("dom", None),
        P("dom", None, None, None, None),
        P("dom", None, None),
        P("dom", None, None),
        P("dom", "feat"),
    )
    return jax.shard_map(
        body,
        mesh=mesh,
        in_specs=placed,
        out_specs=(P("dom", "feat"), P("dom", "feat"), P("feat", None), P("feat", None)),
        check_vma=False,
    )
```

```python
import functools

import jax
import jax.numpy as jnp
from jax import lax
from jax.experimental import pallas as pl
from jax.experimental.pallas import tpu as pltpu
from jax.sharding import PartitionSpec as P

F32 = jnp.float32
BF16 = jnp.bfloat16
VMEM = pl.BlockSpec(memory_space=pltpu.VMEM)
SMEM = pl.BlockSpec(memory_space=pltpu.SMEM)


def shifted(x, axis, by):
    devices = lax.axis_size(axis)
    return lax.ppermute(x, axis, [(i, (i + by) % devices) for i in range(devices)])


def spread(parts, block_ids, count):
    table = (block_ids[:, None] == jnp.arange(count, dtype=jnp.int32)[None, :]).astype(F32)
    return jnp.einsum("kc,kif->cif", table, parts, precision=lax.Precision.HIGHEST)


def tile_apply(tiles, blocks):
    return jnp.einsum("kij,kjf->kif", tiles, blocks, preferred_element_type=F32)


def tile_apply_back(tiles, blocks):
    return jnp.einsum("kji,kjf->kif", tiles, blocks, preferred_element_type=F32)


def round_offsets(parts_total, rounds):
    return [(step + 1) * parts_total // (rounds + 1) for step in range(rounds)]


def sparse_body(
    features,
    w_self,
    w_neigh,
    degree,
    local_vals,
    local_dst,
    local_src,
    remote_vals,
    remote_dst,
    remote_src,
    cotangent,
):
    rows, width = features.shape
    block = local_vals.shape[-1]
    nblocks = rows // block
    rounds = remote_vals.shape[1]
    parts_total = lax.axis_size("dom")
    offsets = round_offsets(parts_total, rounds)
    blocks = features.reshape(nblocks, block, width)
    totals = spread(
        tile_apply(local_vals[0], jnp.take(blocks, local_src[0], axis=0)), local_dst[0], nblocks
    )
    arrived_ids = []
    for step in range(rounds):
        partial_blocks = tile_apply(
            remote_vals[0, step], jnp.take(blocks, remote_src[0, step], axis=0)
        ).astype(BF16)
        arrived, block_ids = shifted((partial_blocks, remote_dst[0, step]), "dom", offsets[step])
        arrived_ids.append(block_ids)
        totals = totals + spread(arrived.astype(F32), block_ids, nblocks)
    inverse = 1.0 / degree.astype(F32)
    agg = (totals.reshape(rows, width) * inverse[:, None]).astype(BF16)
    stacked = jnp.concatenate([features, agg], axis=1)
    weights = jnp.concatenate([w_self, w_neigh], axis=0)
    pre = lax.psum_scatter(
        lax.dot_general(weights, stacked, (((0,), (1,)), ((), ())), preferred_element_type=F32),
        "feat",
        scatter_dimension=0,
        tiled=True,
    ).T
    sigma = jax.nn.sigmoid(pre)
    out = (pre * sigma).astype(BF16)
    dpre = (cotangent.astype(F32) * sigma * (1.0 + pre * (1.0 - sigma))).astype(BF16)
    dpre_all = lax.all_gather(dpre, "feat", axis=1, tiled=True)
    dz_total = lax.dot_general(
        dpre_all, weights, (((1,), (1,)), ((), ())), preferred_element_type=F32
    )
    grad_local = lax.dot_general(
        stacked, dpre_all, (((0,), (0,)), ((), ())), preferred_element_type=F32
    )
    dx_self = dz_total[:, :width]
    dsum = (dz_total[:, width:] * inverse[:, None]).astype(BF16).reshape(nblocks, block, width)
    grad_all = lax.psum(grad_local, "dom")
    back = spread(
        tile_apply_back(local_vals[0], jnp.take(dsum, local_dst[0], axis=0)), local_src[0], nblocks
    )
    for step in range(rounds):
        picked = jnp.take(dsum, arrived_ids[step], axis=0)
        returned = shifted(picked, "dom", parts_total - offsets[step])
        back = back + spread(
            tile_apply_back(remote_vals[0, step], returned), remote_src[0, step], nblocks
        )
    grad_x = dx_self + back.reshape(rows, width)
    return (out, grad_x, grad_all[:width], grad_all[width:])


def tile_counts(rvals, lvals):
    return rvals.shape[0], rvals.shape[1], lvals.shape[0]


def round_of(offset, offsets):
    step, known = jnp.int32(0), offset < 0
    for at, this in enumerate(offsets):
        step = jnp.where(offset == this, at, step)
        known = known | (offset == this)
    return step, known


def crossed_block(block_id, mine, per_feat):
    return ((block_id // per_feat) ^ mine) * per_feat + block_id % per_feat


def tile_groups(masks, offsets, parts_total, me, groups, tiles):
    jobs = []
    for at, mask in enumerate(masks):
        if mask == 0:
            for first in range(0, tiles, groups):
                count = min(groups, tiles - first)
                jobs.append((at, None, None, first, count))
        else:
            offset = lax.rem((me ^ mask) - me + parts_total, parts_total)
            step, known = round_of(offset, offsets)
            jobs.append((at, step, known, None, groups))
    return jobs


def flat(masks):
    return [m for group in masks for m in (group if isinstance(group, list) else [group])]


def tiles_kernel(masks, offsets, parts_total, back, feats, extras, *refs):
    ids_in, (lvals, rvals), refs = refs[:4], refs[4:6], refs[6:]
    ids, id_sems, refs = refs[-5:-1], refs[-1], refs[:-5]
    id_copies = [
        pltpu.make_async_copy(ids_in[n], ids[n], id_sems.at[n]) for n in range(len(ids))
    ]
    for copy in id_copies:
        copy.start()
    groups_of, masks = masks, flat(masks)
    me = lax.axis_index("dom")
    mine = lax.axis_index("feat")
    rounds, groups, tiles = tile_counts(rvals, lvals)
    jobs = tile_groups(masks, offsets, parts_total, me, groups, tiles)
    held, prod, acc, sems = refs[-4:]
    copies = []
    for slot, (at, step, known, first, count) in enumerate(jobs):
        source = lvals.at[pl.ds(first, count)] if step is None else rvals.at[step]
        copy = pltpu.make_async_copy(source, held.at[slot, pl.ds(0, count)], sems.at[slot])
        copy.start()
        copies.append(copy)
    if back:
        own_ref, grad_ref = refs[len(masks)], refs[len(masks) + 1]
        blocks = refs[: len(masks)]
        sinks = [grad_ref] * len(masks)
        acc[0] = own_ref[...]
    else:
        blocks = [refs[0]] * len(masks)
        sinks, used = [], 1 + extras
        for group in groups_of:
            if isinstance(group, list):
                sinks += [refs[used].at[n] for n in range(len(group))]
            else:
                sinks.append(refs[used])
            used += 1
    if extras:
        pieces, pair = refs[used : used + feats], refs[used + feats]
        pair[0] = refs[2][...]
        pair[1] = refs[3][...]
        for mask, piece in enumerate(pieces):
            rows = pl.ds((mine ^ mask) * piece.shape[1], piece.shape[1])
            piece[0] = refs[0][rows]
            piece[1] = refs[1][rows]
    total = 0
    for copy in id_copies:
        copy.wait()
    ldst, lsrc, rdst, rsrc = ids
    for slot, (at, step, known, first, count) in enumerate(jobs):
        copies[slot].wait()
        if step is None:
            dst = [ldst[0, first + k] for k in range(count)]
            src = [lsrc[0, first + k] for k in range(count)]
        else:
            dst = [rdst[step, 0, k] for k in range(count)]
            src = [rsrc[step, 0, k] for k in range(count)]
        half = slot % 2
        for k in range(len(dst)):
            if back:
                per_feat = blocks[at].shape[0] // feats
                block = blocks[at][crossed_block(dst[k], mine, per_feat)]
                product = lax.dot_general(
                    held[slot, k], block, (((0,), (0,)), ((), ())), preferred_element_type=F32
                )
            else:
                product = jnp.dot(
                    held[slot, k], blocks[at][src[k]], preferred_element_type=F32
                )
            prod[half, k] = product if known is None else jnp.where(known, product, 0.0)
        fresh = not back and (slot == 0 or jobs[slot - 1][0] != at)
        if fresh:
            total = at % 2
            acc[total] = jnp.zeros(acc.shape[1:], F32)
        for k in range(len(dst)):
            into = src[k] if back else dst[k]
            acc[total, into] = acc[total, into] + prod[half, k]
        last = slot == len(jobs) - 1 or jobs[slot + 1][0] != at
        if last and (not back or slot == len(jobs) - 1):
            sinks[at][...] = acc[total].astype(sinks[at].dtype)


def tiles_call(masks, offsets, parts_total, back, feats, fixed, blocks, sinks, room):
    ids, lvals, rvals = fixed
    rounds, groups, tiles = tile_counts(rvals, lvals)
    nblocks, block, width = blocks[0].shape
    slots = sum(-(-tiles // groups) if mask == 0 else 1 for mask in flat(masks))
    extras = 0 if back else len(blocks) - 1
    return pl.pallas_call(
        functools.partial(tiles_kernel, masks, offsets, parts_total, back, feats, extras),
        out_shape=sinks,
        in_specs=[pl.BlockSpec(memory_space=pltpu.HBM)] * 6
        + [VMEM] * len(blocks),
        out_specs=jax.tree.map(lambda _: VMEM, sinks),
        scratch_shapes=[
            pltpu.VMEM((slots, groups, block, block), BF16),
            pltpu.VMEM((2, groups, block, width), F32),
            pltpu.VMEM((2, nblocks, block, width), F32),
            pltpu.SemaphoreType.DMA((slots,)),
            *[pltpu.SMEM(t.shape, jnp.int32) for t in ids],
            pltpu.SemaphoreType.DMA((len(ids),)),
        ],
        compiler_params=pltpu.CompilerParams(vmem_limit_bytes=room * 2**20),
        cost_estimate=pl.CostEstimate(flops=1, bytes_accessed=1, transcendentals=0),
    )(*ids, lvals, rvals, *blocks)


def small_call(kernel, outs, arrays, scratch=(), room=24):
    return pl.pallas_call(
        kernel,
        out_shape=outs,
        in_specs=[VMEM] * len(arrays),
        out_specs=[VMEM] * len(outs),
        scratch_shapes=scratch,
        compiler_params=pltpu.CompilerParams(vmem_limit_bytes=room * 2**20),
        cost_estimate=pl.CostEstimate(flops=1, bytes_accessed=1, transcendentals=0),
    )(*arrays)


def agg_kernel(feats, inv_ref, keep_ref, *refs):
    mine = lax.axis_index("feat")
    far_refs, agg_ref, piece_refs = refs[: -1 - feats], refs[-1 - feats], refs[-feats:]
    per_feat = piece_refs[0].shape[0]
    sums = keep_ref[...]
    for ref in far_refs:
        sums = sums + ref[...].astype(F32)
    agg_ref[...] = (sums * inv_ref[...]).astype(BF16)
    for mask, piece in enumerate(piece_refs):
        piece[...] = agg_ref[pl.ds((mine ^ mask) * per_feat, per_feat)]


def joined(parts):
    return jnp.concatenate(parts, axis=1)


def dense_kernel(feats, inv_ref, *refs):
    mine = lax.axis_index("feat")
    w_refs, early_refs, a_refs = refs[:feats], refs[feats : 2 * feats], refs[2 * feats : 3 * feats]
    sent_refs, own_ref = refs[3 * feats : 4 * feats - 1], refs[4 * feats - 1]
    dsum_refs = refs[4 * feats : 5 * feats]
    held = refs[-1]
    full = w_refs[0].shape[2]
    some, width = held.shape[1:]
    pre = jnp.zeros((some, full), F32)
    for mask in range(feats):
        early = early_refs[mask]
        pre = pre + jnp.dot(
            early[0].reshape(some, width), w_refs[mask][0], preferred_element_type=F32
        )
        pre = pre + jnp.dot(
            a_refs[mask][...].reshape(some, width), w_refs[mask][1], preferred_element_type=F32
        )
        held[mine ^ mask] = early[1].reshape(some, width)
    sigma = 1.0 / (1.0 + jnp.exp(-pre))
    out = (pre * sigma).astype(BF16)
    cot = joined([held[j] for j in range(feats)]).astype(F32)
    dpre = (cot * sigma * (1.0 + pre * (1.0 - sigma))).astype(BF16)
    for mask in range(feats):
        dagg = lax.dot_general(
            dpre, w_refs[mask][1], (((1,), (1,)), ((), ())), preferred_element_type=F32
        )
        dsum_refs[mask][...] = (dagg * inv_ref[...]).astype(BF16)
    for j in range(feats):
        cols = slice(j * width, (j + 1) * width)
        for sent in sent_refs:
            sent[j] = dpre[:, cols]
        held[j] = out[:, cols]
    own_ref[...] = held[mine]
    for mask, sent in enumerate(sent_refs, 1):
        sent[feats] = held[mine ^ mask]


def grad_kernel(feats, f_ref, a_ref, w_ref, *refs):
    me = lax.axis_index("dom")
    mine = lax.axis_index("feat")
    dpre_refs, (dx_ref, give_ref, keep_ref, held) = refs[:feats], refs[feats:]
    width = f_ref.shape[1]
    piece = held.shape[1]
    some = dpre_refs[0].shape[1]
    parts = [0.0, 0.0]
    for mask, dpre_ref in enumerate(dpre_refs):
        dpre = joined([dpre_ref[j] for j in range(feats)])
        rows = pl.ds(pl.multiple_of((mine ^ mask) * some, some), some)
        for at, ref in enumerate((f_ref, a_ref)):
            parts[at] = parts[at] + lax.dot_general(
                ref[rows], dpre, (((0,), (0,)), ((), ())), preferred_element_type=F32
            )
        dx_ref[rows] = lax.dot_general(
            dpre, w_ref[...], (((1,), (1,)), ((), ())), preferred_element_type=F32
        )
    for at, part in enumerate(parts):
        for j in range(width // piece):
            held[at * (width // piece) + j] = part[j * piece : (j + 1) * piece]
    side = me % 2
    for at in range(give_ref.shape[0]):
        give_ref[at] = held[2 * at + 1 - side].astype(BF16)
        keep_ref[at] = held[2 * at + side]


def finish_kernel(mine_ref, other_ref, self_ref, neigh_ref, held):
    side = lax.axis_index("dom") % 2
    for at in range(mine_ref.shape[0]):
        held[2 * at + side] = mine_ref[at].astype(F32)
        held[2 * at + 1 - side] = other_ref[at].astype(F32)
    some = held.shape[1]
    half = held.shape[0] // 2
    for j in range(half):
        self_ref[j * some : (j + 1) * some] = held[j]
        neigh_ref[j * some : (j + 1) * some] = held[half + j]


def place_kernel(*refs):
    mine = lax.axis_index("feat")
    own_ref, *come_refs, out_ref = refs
    out_ref[mine] = own_ref[...]
    for mask, come in enumerate(come_refs, 1):
        out_ref[mine ^ mask] = come[out_ref.shape[0]]


def swap_feat(x):
    return lax.all_to_all(x, "feat", split_axis=0, concat_axis=0, tiled=True)


def crossed(x, mask, axis="dom"):
    return lax.ppermute(x, axis, [(i, i ^ mask) for i in range(lax.axis_size(axis))])


def like(shape, dtype):
    return jax.ShapeDtypeStruct(shape, dtype)


def dense_body(
    features,
    w_self,
    w_neigh,
    degree,
    local_vals,
    local_dst,
    local_src,
    remote_vals,
    remote_dst,
    remote_src,
    cotangent,
):
    rows, width = features.shape
    block = local_vals.shape[-1]
    nblocks = rows // block
    rounds = remote_vals.shape[1]
    parts_total = lax.axis_size("dom")
    feats = lax.axis_size("feat")
    some = rows // feats
    per_feat = nblocks // feats
    full = feats * width
    offsets = round_offsets(parts_total, rounds)
    near, far = 1, list(range(parts_total - 2, 0, -2))
    bits = [1, 2, 4]
    mine = lax.axis_index("feat").astype(jnp.int32)
    inverse = 1.0 / degree.astype(F32)
    inv_rows = lax.dynamic_slice(inverse, (mine * some,), (some,))[:, None]
    ids = (
        local_dst,
        local_src,
        jnp.swapaxes(remote_dst, 0, 1),
        jnp.swapaxes(remote_src, 0, 1),
    )
    shape = (nblocks, block, width)
    blocks = features.reshape(shape)
    fixed = (ids, local_vals[0], remote_vals[0])

    def forward(masks, arrays, sinks):
        return tiles_call(
            masks, offsets, parts_total, False, feats, fixed, arrays, sinks, 62
        )

    def relayed(x):
        over = crossed(x, 2, "feat")
        return [x, crossed(x, 1, "feat"), over, crossed(over, 1, "feat")]

    def tied(x, *others):
        return lax.optimization_barrier((x, others))[0]

    sends = forward([7, 5, 3, 1], [blocks], [like(shape, BF16)] * 4)
    made = forward(
        [6, 4, 2, 0],
        [blocks, cotangent.reshape(shape), w_self, w_neigh],
        [like(shape, F32)] * 4
        + [like((2, per_feat, block, width), BF16)] * feats
        + [like((2, width, full), BF16)],
    )
    keep_6, keep_4, keep_2, keep = made[:4]
    early_pieces, pair = made[4:-1], made[-1]
    weights = relayed(pair)
    near_6, near_4, near_2 = (crossed(send, near) for send in sends[:3])
    sum_6 = (keep_6 + near_6.astype(F32)).astype(BF16)
    near_4, weights[2] = lax.optimization_barrier((near_4, weights[2]))
    sum_4 = (keep_4 + near_4.astype(F32) + crossed(sum_6, 2).astype(F32)).astype(BF16)
    far_0 = crossed(sum_4, 4)
    keep_2, send_1, early_pieces = tied((keep_2, sends[3], early_pieces), sum_4)
    near_0 = crossed(send_1, near)
    sum_2 = (keep_2 + near_2.astype(F32)).astype(BF16)
    mid_0 = crossed(sum_2, 2)
    early_2, early_3 = crossed(early_pieces[2], 2, "feat"), crossed(early_pieces[3], 3, "feat")
    far_0, early_2, early_3, early_1 = lax.optimization_barrier(
        (far_0, early_2, early_3, early_pieces[1])
    )
    early = [early_pieces[0], crossed(early_1, 1, "feat"), early_2, early_3]
    part = keep + mid_0.astype(F32) + near_0.astype(F32)
    arrived = [far_0]
    early, weights, arrived = lax.optimization_barrier((early, weights, arrived))
    agg, *agg_pieces = small_call(
        functools.partial(agg_kernel, feats),
        [like(shape, BF16)] + [like((per_feat, block, width), BF16)] * feats,
        [inverse.reshape(nblocks, block, 1), part, *arrived],
    )
    agg_rows = [agg_pieces[0]] + [crossed(agg_pieces[m], m, "feat") for m in range(1, feats)]
    *sent, own_out, p0, p1, p2, p3 = small_call(
        functools.partial(dense_kernel, feats),
        [like((feats + 1, some, width), BF16)] * (feats - 1)
        + [like((some, width), BF16)] * (1 + feats),
        [inv_rows, *weights, *early, *agg_rows],
        [pltpu.VMEM((feats, some, width), BF16)],
    )
    dsum_pieces = [p0, p1, p2, p3]
    dsum = jnp.concatenate(
        [dsum_pieces[0]] + [crossed(dsum_pieces[m], m, "feat") for m in range(1, feats)], axis=0
    ).reshape(shape)
    found = {0: dsum}
    for mask in (4, 2, 1):
        found[mask] = crossed(dsum, mask)
    sent = tied(sent, dsum)
    come_2, come_3 = crossed(sent[1], 2, "feat"), crossed(sent[2], 3, "feat")
    found[4], come_2, come_3, found[2], found[1], sent[0] = lax.optimization_barrier(
        (found[4], come_2, come_3, found[2], found[1], sent[0])
    )
    come = [crossed(sent[0], 1, "feat"), come_2, come_3]
    (out,) = small_call(place_kernel, [like((feats, some, width), BF16)], [own_out, *come])
    dpre = [sent[0], *come]
    found[6] = crossed(found[4], 2)
    found[3] = crossed(found[2], near)
    found[5] = crossed(found[4], near)
    found[7] = crossed(found[5], 2)
    piece = 2 * width // parts_total
    dx_self, give, keep = small_call(
        functools.partial(grad_kernel, feats),
        [
            like((rows, width), F32),
            like((len(far) + 1, piece, full), BF16),
            like((len(far) + 1, piece, full), F32),
        ],
        [features, agg.reshape(rows, width), w_self, *dpre],
        [pltpu.VMEM((parts_total, piece, full), F32)],
    )
    total = (keep + crossed(give, near).astype(F32)).astype(BF16)
    total = (total.astype(F32) + crossed(total, 2).astype(F32)).astype(BF16)
    total = tied(total, found[5], found[6])
    total = (total.astype(F32) + crossed(total, 4).astype(F32)).astype(BF16)
    grad_x = dx_self.reshape(shape)
    half = parts_total // 2
    for order in (list(range(half)), list(range(half, parts_total))):
        grad_x = tiles_call(
            order,
            offsets,
            parts_total,
            True,
            feats,
            fixed,
            [found[mask] for mask in order] + [grad_x],
            like(shape, F32),
            24,
        )
    total, out = tied((total, out), found[3], found[7])
    grad_self, grad_neigh = small_call(
        finish_kernel,
        [like((width, full), F32)] * 2,
        [total, crossed(total, near)],
        [pltpu.VMEM((parts_total, piece, full), F32)],
    )
    return (out.reshape(rows, width), grad_x.reshape(rows, width), grad_self, grad_neigh)


def solution(mesh):
    def body(*args):
        rounds = args[7].shape[1]
        small = mesh.shape["dom"] == 8 and mesh.shape["feat"] == 4
        nearly_all = mesh.shape["dom"] <= rounds + 2
        return (dense_body if small and nearly_all else sparse_body)(*args)

    placed = (
        P("dom", "feat"),
        P("feat", None),
        P("feat", None),
        P("dom"),
        P("dom", None, None, None),
        P("dom", None),
        P("dom", None),
        P("dom", None, None, None, None),
        P("dom", None, None),
        P("dom", None, None),
        P("dom", "feat"),
    )
    return jax.shard_map(
        body,
        mesh=mesh,
        in_specs=placed,
        out_specs=(P("dom", "feat"), P("dom", "feat"), P("feat", None), P("feat", None)),
        check_vma=False,
    )
```

```python
import functools

import jax
import jax.numpy as jnp
from jax import lax
from jax.experimental import pallas as pl
from jax.experimental.pallas import tpu as pltpu
from jax.sharding import PartitionSpec as P

F32 = jnp.float32
BF16 = jnp.bfloat16
VMEM = pl.BlockSpec(memory_space=pltpu.VMEM)
SMEM = pl.BlockSpec(memory_space=pltpu.SMEM)


def shifted(x, axis, by):
    devices = lax.axis_size(axis)
    return lax.ppermute(x, axis, [(i, (i + by) % devices) for i in range(devices)])


def spread(parts, block_ids, count):
    table = (block_ids[:, None] == jnp.arange(count, dtype=jnp.int32)[None, :]).astype(F32)
    return jnp.einsum("kc,kif->cif", table, parts, precision=lax.Precision.HIGHEST)


def tile_apply(tiles, blocks):
    return jnp.einsum("kij,kjf->kif", tiles, blocks, preferred_element_type=F32)


def tile_apply_back(tiles, blocks):
    return jnp.einsum("kji,kjf->kif", tiles, blocks, preferred_element_type=F32)


def round_offsets(parts_total, rounds):
    return [(step + 1) * parts_total // (rounds + 1) for step in range(rounds)]


def sparse_body(
    features,
    w_self,
    w_neigh,
    degree,
    local_vals,
    local_dst,
    local_src,
    remote_vals,
    remote_dst,
    remote_src,
    cotangent,
):
    rows, width = features.shape
    block = local_vals.shape[-1]
    nblocks = rows // block
    rounds = remote_vals.shape[1]
    parts_total = lax.axis_size("dom")
    offsets = round_offsets(parts_total, rounds)
    blocks = features.reshape(nblocks, block, width)
    totals = spread(
        tile_apply(local_vals[0], jnp.take(blocks, local_src[0], axis=0)), local_dst[0], nblocks
    )
    arrived_ids = []
    for step in range(rounds):
        partial_blocks = tile_apply(
            remote_vals[0, step], jnp.take(blocks, remote_src[0, step], axis=0)
        ).astype(BF16)
        arrived, block_ids = shifted((partial_blocks, remote_dst[0, step]), "dom", offsets[step])
        arrived_ids.append(block_ids)
        totals = totals + spread(arrived.astype(F32), block_ids, nblocks)
    inverse = 1.0 / degree.astype(F32)
    agg = (totals.reshape(rows, width) * inverse[:, None]).astype(BF16)
    stacked = jnp.concatenate([features, agg], axis=1)
    weights = jnp.concatenate([w_self, w_neigh], axis=0)
    pre = lax.psum_scatter(
        lax.dot_general(weights, stacked, (((0,), (1,)), ((), ())), preferred_element_type=F32),
        "feat",
        scatter_dimension=0,
        tiled=True,
    ).T
    sigma = jax.nn.sigmoid(pre)
    out = (pre * sigma).astype(BF16)
    dpre = (cotangent.astype(F32) * sigma * (1.0 + pre * (1.0 - sigma))).astype(BF16)
    dpre_all = lax.all_gather(dpre, "feat", axis=1, tiled=True)
    dz_total = lax.dot_general(
        dpre_all, weights, (((1,), (1,)), ((), ())), preferred_element_type=F32
    )
    grad_local = lax.dot_general(
        stacked, dpre_all, (((0,), (0,)), ((), ())), preferred_element_type=F32
    )
    dx_self = dz_total[:, :width]
    dsum = (dz_total[:, width:] * inverse[:, None]).astype(BF16).reshape(nblocks, block, width)
    grad_all = lax.psum(grad_local, "dom")
    back = spread(
        tile_apply_back(local_vals[0], jnp.take(dsum, local_dst[0], axis=0)), local_src[0], nblocks
    )
    for step in range(rounds):
        picked = jnp.take(dsum, arrived_ids[step], axis=0)
        returned = shifted(picked, "dom", parts_total - offsets[step])
        back = back + spread(
            tile_apply_back(remote_vals[0, step], returned), remote_src[0, step], nblocks
        )
    grad_x = dx_self + back.reshape(rows, width)
    return (out, grad_x, grad_all[:width], grad_all[width:])


def tile_counts(rvals, lvals):
    return rvals.shape[0], rvals.shape[1], lvals.shape[0]


def round_of(offset, offsets):
    step, known = jnp.int32(0), offset < 0
    for at, this in enumerate(offsets):
        step = jnp.where(offset == this, at, step)
        known = known | (offset == this)
    return step, known


def crossed_block(block_id, mine, per_feat):
    return ((block_id // per_feat) ^ mine) * per_feat + block_id % per_feat


def tile_groups(masks, offsets, parts_total, me, groups, tiles):
    jobs = []
    for at, mask in enumerate(masks):
        if mask == 0:
            for first in range(0, tiles, groups):
                count = min(groups, tiles - first)
                jobs.append((at, None, None, first, count))
        else:
            offset = lax.rem((me ^ mask) - me + parts_total, parts_total)
            step, known = round_of(offset, offsets)
            jobs.append((at, step, known, None, groups))
    return jobs


def flat(masks):
    return [m for group in masks for m in (group if isinstance(group, list) else [group])]


def tiles_kernel(masks, offsets, parts_total, back, feats, extras, *refs):
    ids_in, (lvals, rvals), refs = refs[:4], refs[4:6], refs[6:]
    ids, id_sems, refs = refs[-5:-1], refs[-1], refs[:-5]
    id_copies = [
        pltpu.make_async_copy(ids_in[n], ids[n], id_sems.at[n]) for n in range(len(ids))
    ]
    for copy in id_copies:
        copy.start()
    groups_of, masks = masks, flat(masks)
    me = lax.axis_index("dom")
    mine = lax.axis_index("feat")
    rounds, groups, tiles = tile_counts(rvals, lvals)
    jobs = tile_groups(masks, offsets, parts_total, me, groups, tiles)
    held, prod, acc, sems = refs[-4:]
    copies = []
    for slot, (at, step, known, first, count) in enumerate(jobs):
        source = lvals.at[pl.ds(first, count)] if step is None else rvals.at[step]
        copy = pltpu.make_async_copy(source, held.at[slot, pl.ds(0, count)], sems.at[slot])
        copy.start()
        copies.append(copy)
    if back:
        own_ref, grad_ref = refs[len(masks)], refs[len(masks) + 1]
        blocks = refs[: len(masks)]
        sinks = [grad_ref] * len(masks)
        acc[0] = own_ref[...]
    else:
        blocks = [refs[0]] * len(masks)
        sinks, used = [], 1 + extras
        for group in groups_of:
            if isinstance(group, list):
                sinks += [refs[used].at[n] for n in range(len(group))]
            else:
                sinks.append(refs[used])
            used += 1
    if extras:
        pieces, pair = refs[used : used + feats], refs[used + feats]
        pair[0] = refs[2][...]
        pair[1] = refs[3][...]
        for mask, piece in enumerate(pieces):
            rows = pl.ds((mine ^ mask) * piece.shape[1], piece.shape[1])
            piece[0] = refs[0][rows]
            piece[1] = refs[1][rows]
    total = 0
    for copy in id_copies:
        copy.wait()
    ldst, lsrc, rdst, rsrc = ids
    for slot, (at, step, known, first, count) in enumerate(jobs):
        copies[slot].wait()
        if step is None:
            dst = [ldst[0, first + k] for k in range(count)]
            src = [lsrc[0, first + k] for k in range(count)]
        else:
            dst = [rdst[step, 0, k] for k in range(count)]
            src = [rsrc[step, 0, k] for k in range(count)]
        half = slot % 2
        for k in range(len(dst)):
            if back:
                per_feat = blocks[at].shape[0] // feats
                block = blocks[at][crossed_block(dst[k], mine, per_feat)]
                product = lax.dot_general(
                    held[slot, k], block, (((0,), (0,)), ((), ())), preferred_element_type=F32
                )
            else:
                product = jnp.dot(
                    held[slot, k], blocks[at][src[k]], preferred_element_type=F32
                )
            prod[half, k] = product if known is None else jnp.where(known, product, 0.0)
        fresh = not back and (slot == 0 or jobs[slot - 1][0] != at)
        if fresh:
            total = at % 2
            acc[total] = jnp.zeros(acc.shape[1:], F32)
        for k in range(len(dst)):
            into = src[k] if back else dst[k]
            acc[total, into] = acc[total, into] + prod[half, k]
        last = slot == len(jobs) - 1 or jobs[slot + 1][0] != at
        if last and (not back or slot == len(jobs) - 1):
            sinks[at][...] = acc[total].astype(sinks[at].dtype)


def tiles_call(masks, offsets, parts_total, back, feats, fixed, blocks, sinks, room):
    ids, lvals, rvals = fixed
    rounds, groups, tiles = tile_counts(rvals, lvals)
    nblocks, block, width = blocks[0].shape
    slots = sum(-(-tiles // groups) if mask == 0 else 1 for mask in flat(masks))
    extras = 0 if back else len(blocks) - 1
    return pl.pallas_call(
        functools.partial(tiles_kernel, masks, offsets, parts_total, back, feats, extras),
        out_shape=sinks,
        in_specs=[pl.BlockSpec(memory_space=pltpu.HBM)] * 6
        + [VMEM] * len(blocks),
        out_specs=jax.tree.map(lambda _: VMEM, sinks),
        scratch_shapes=[
            pltpu.VMEM((slots, groups, block, block), BF16),
            pltpu.VMEM((2, groups, block, width), F32),
            pltpu.VMEM((2, nblocks, block, width), F32),
            pltpu.SemaphoreType.DMA((slots,)),
            *[pltpu.SMEM(t.shape, jnp.int32) for t in ids],
            pltpu.SemaphoreType.DMA((len(ids),)),
        ],
        compiler_params=pltpu.CompilerParams(vmem_limit_bytes=room * 2**20),
        cost_estimate=pl.CostEstimate(flops=1, bytes_accessed=1, transcendentals=0),
    )(*ids, lvals, rvals, *blocks)


def small_call(kernel, outs, arrays, scratch=(), room=24):
    return pl.pallas_call(
        kernel,
        out_shape=outs,
        in_specs=[VMEM] * len(arrays),
        out_specs=[VMEM] * len(outs),
        scratch_shapes=scratch,
        compiler_params=pltpu.CompilerParams(vmem_limit_bytes=room * 2**20),
        cost_estimate=pl.CostEstimate(flops=1, bytes_accessed=1, transcendentals=0),
    )(*arrays)


def agg_kernel(feats, inv_ref, keep_ref, *refs):
    mine = lax.axis_index("feat")
    far_refs, agg_ref, piece_refs = refs[: -1 - feats], refs[-1 - feats], refs[-feats:]
    per_feat = piece_refs[0].shape[0]
    sums = keep_ref[...]
    for ref in far_refs:
        sums = sums + ref[...].astype(F32)
    agg_ref[...] = (sums * inv_ref[...]).astype(BF16)
    for mask, piece in enumerate(piece_refs):
        piece[...] = agg_ref[pl.ds((mine ^ mask) * per_feat, per_feat)]


def joined(parts):
    return jnp.concatenate(parts, axis=1)


def dense_kernel(feats, inv_ref, *refs):
    mine = lax.axis_index("feat")
    w_refs, early_refs, a_refs = refs[:feats], refs[feats : 2 * feats], refs[2 * feats : 3 * feats]
    sent_refs, own_ref = refs[3 * feats : 4 * feats - 1], refs[4 * feats - 1]
    dsum_refs = refs[4 * feats : 5 * feats]
    held = refs[-1]
    full = w_refs[0].shape[2]
    some, width = held.shape[1:]
    pre = jnp.zeros((some, full), F32)
    for mask in range(feats):
        early = early_refs[mask]
        pre = pre + jnp.dot(
            early[0].reshape(some, width), w_refs[mask][0], preferred_element_type=F32
        )
        pre = pre + jnp.dot(
            a_refs[mask][...].reshape(some, width), w_refs[mask][1], preferred_element_type=F32
        )
        held[mine ^ mask] = early[1].reshape(some, width)
    sigma = 1.0 / (1.0 + jnp.exp(-pre))
    out = (pre * sigma).astype(BF16)
    cot = joined([held[j] for j in range(feats)]).astype(F32)
    dpre = (cot * sigma * (1.0 + pre * (1.0 - sigma))).astype(BF16)
    for mask in range(feats):
        dagg = lax.dot_general(
            dpre, w_refs[mask][1], (((1,), (1,)), ((), ())), preferred_element_type=F32
        )
        dsum_refs[mask][...] = (dagg * inv_ref[...]).astype(BF16)
    for j in range(feats):
        cols = slice(j * width, (j + 1) * width)
        for sent in sent_refs:
            sent[j] = dpre[:, cols]
        held[j] = out[:, cols]
    own_ref[...] = held[mine]
    for mask, sent in enumerate(sent_refs, 1):
        sent[feats] = held[mine ^ mask]


def grad_kernel(feats, f_ref, a_ref, w_ref, *refs):
    me = lax.axis_index("dom")
    mine = lax.axis_index("feat")
    dpre_refs, (dx_ref, give_ref, keep_ref, held) = refs[:feats], refs[feats:]
    width = f_ref.shape[1]
    piece = held.shape[1]
    some = dpre_refs[0].shape[1]
    parts = [0.0, 0.0]
    for mask, dpre_ref in enumerate(dpre_refs):
        dpre = joined([dpre_ref[j] for j in range(feats)])
        rows = pl.ds(pl.multiple_of((mine ^ mask) * some, some), some)
        for at, ref in enumerate((f_ref, a_ref)):
            parts[at] = parts[at] + lax.dot_general(
                ref[rows], dpre, (((0,), (0,)), ((), ())), preferred_element_type=F32
            )
        dx_ref[rows] = lax.dot_general(
            dpre, w_ref[...], (((1,), (1,)), ((), ())), preferred_element_type=F32
        )
    for at, part in enumerate(parts):
        for j in range(width // piece):
            held[at * (width // piece) + j] = part[j * piece : (j + 1) * piece]
    side = me % 2
    for at in range(give_ref.shape[0]):
        give_ref[at] = held[2 * at + 1 - side].astype(BF16)
        keep_ref[at] = held[2 * at + side]


def finish_kernel(mine_ref, other_ref, self_ref, neigh_ref, held):
    side = lax.axis_index("dom") % 2
    for at in range(mine_ref.shape[0]):
        held[2 * at + side] = mine_ref[at].astype(F32)
        held[2 * at + 1 - side] = other_ref[at].astype(F32)
    some = held.shape[1]
    half = held.shape[0] // 2
    for j in range(half):
        self_ref[j * some : (j + 1) * some] = held[j]
        neigh_ref[j * some : (j + 1) * some] = held[half + j]


def place_kernel(*refs):
    mine = lax.axis_index("feat")
    own_ref, *come_refs, out_ref = refs
    out_ref[mine] = own_ref[...]
    for mask, come in enumerate(come_refs, 1):
        out_ref[mine ^ mask] = come[out_ref.shape[0]]


def swap_feat(x):
    return lax.all_to_all(x, "feat", split_axis=0, concat_axis=0, tiled=True)


def crossed(x, mask, axis="dom"):
    return lax.ppermute(x, axis, [(i, i ^ mask) for i in range(lax.axis_size(axis))])


def like(shape, dtype):
    return jax.ShapeDtypeStruct(shape, dtype)


def dense_body(
    features,
    w_self,
    w_neigh,
    degree,
    local_vals,
    local_dst,
    local_src,
    remote_vals,
    remote_dst,
    remote_src,
    cotangent,
):
    rows, width = features.shape
    block = local_vals.shape[-1]
    nblocks = rows // block
    rounds = remote_vals.shape[1]
    parts_total = lax.axis_size("dom")
    feats = lax.axis_size("feat")
    some = rows // feats
    per_feat = nblocks // feats
    full = feats * width
    offsets = round_offsets(parts_total, rounds)
    near, far = 1, list(range(parts_total - 2, 0, -2))
    bits = [1, 2, 4]
    mine = lax.axis_index("feat").astype(jnp.int32)
    inverse = 1.0 / degree.astype(F32)
    inv_rows = lax.dynamic_slice(inverse, (mine * some,), (some,))[:, None]
    ids = (
        local_dst,
        local_src,
        jnp.swapaxes(remote_dst, 0, 1),
        jnp.swapaxes(remote_src, 0, 1),
    )
    shape = (nblocks, block, width)
    blocks = features.reshape(shape)
    fixed = (ids, local_vals[0], remote_vals[0])

    def forward(masks, arrays, sinks):
        return tiles_call(
            masks, offsets, parts_total, False, feats, fixed, arrays, sinks, 62
        )

    def relayed(x):
        over = crossed(x, 2, "feat")
        return [x, crossed(x, 1, "feat"), over, crossed(over, 1, "feat")]

    def tied(x, *others):
        return lax.optimization_barrier((x, others))[0]

    sends = forward([7, 5, 3, 1], [blocks], [like(shape, BF16)] * 4)
    made = forward(
        [6, 4, 2, 0],
        [blocks, cotangent.reshape(shape), w_self, w_neigh],
        [like(shape, F32)] * 4
        + [like((2, per_feat, block, width), BF16)] * feats
        + [like((2, width, full), BF16)],
    )
    keep_6, keep_4, keep_2, keep = made[:4]
    early_pieces, pair = made[4:-1], made[-1]
    weights = relayed(pair)
    near_6, near_4, near_2 = (crossed(send, near) for send in sends[:3])
    sum_6 = (keep_6 + near_6.astype(F32)).astype(BF16)
    near_4, weights[2] = lax.optimization_barrier((near_4, weights[2]))
    sum_4 = (keep_4 + near_4.astype(F32) + crossed(sum_6, 2).astype(F32)).astype(BF16)
    far_0 = crossed(sum_4, 4)
    keep_2, send_1, early_pieces = tied((keep_2, sends[3], early_pieces), sum_4)
    near_0 = crossed(send_1, near)
    sum_2 = (keep_2 + near_2.astype(F32)).astype(BF16)
    mid_0 = crossed(sum_2, 2)
    early_2, early_3 = crossed(early_pieces[2], 2, "feat"), crossed(early_pieces[3], 3, "feat")
    far_0, early_2, early_3, early_1 = lax.optimization_barrier(
        (far_0, early_2, early_3, early_pieces[1])
    )
    early = [early_pieces[0], crossed(early_1, 1, "feat"), early_2, early_3]
    part = keep + mid_0.astype(F32) + near_0.astype(F32)
    arrived = [far_0]
    early, weights, arrived = lax.optimization_barrier((early, weights, arrived))
    agg, *agg_pieces = small_call(
        functools.partial(agg_kernel, feats),
        [like(shape, BF16)] + [like((per_feat, block, width), BF16)] * feats,
        [inverse.reshape(nblocks, block, 1), part, *arrived],
    )
    agg_rows = [agg_pieces[0]] + [crossed(agg_pieces[m], m, "feat") for m in range(1, feats)]
    *sent, own_out, p0, p1, p2, p3 = small_call(
        functools.partial(dense_kernel, feats),
        [like((feats + 1, some, width), BF16)] * (feats - 1)
        + [like((some, width), BF16)] * (1 + feats),
        [inv_rows, *weights, *early, *agg_rows],
        [pltpu.VMEM((feats, some, width), BF16)],
    )
    dsum_pieces = [p0, p1, p2, p3]
    dsum = jnp.concatenate(
        [dsum_pieces[0]] + [crossed(dsum_pieces[m], m, "feat") for m in range(1, feats)], axis=0
    ).reshape(shape)
    found = {0: dsum}
    for mask in (4, 2, 1):
        found[mask] = crossed(dsum, mask)
    sent = tied(sent, dsum)
    come_2, come_3 = crossed(sent[1], 2, "feat"), crossed(sent[2], 3, "feat")
    found[4], come_2, come_3, found[2], found[1], sent[0] = lax.optimization_barrier(
        (found[4], come_2, come_3, found[2], found[1], sent[0])
    )
    come = [crossed(sent[0], 1, "feat"), come_2, come_3]
    (out,) = small_call(place_kernel, [like((feats, some, width), BF16)], [own_out, *come])
    dpre = [sent[0], *come]
    found[6] = crossed(found[4], 2)
    found[3] = crossed(found[2], near)
    found[5] = crossed(found[4], near)
    found[7] = crossed(found[5], 2)
    piece = 2 * width // parts_total
    dx_self, give, keep = small_call(
        functools.partial(grad_kernel, feats),
        [
            like((rows, width), F32),
            like((len(far) + 1, piece, full), BF16),
            like((len(far) + 1, piece, full), F32),
        ],
        [features, agg.reshape(rows, width), w_self, *dpre],
        [pltpu.VMEM((parts_total, piece, full), F32)],
    )
    total = (keep + crossed(give, near).astype(F32)).astype(BF16)
    total = tied(total, found[6])
    total = (total.astype(F32) + crossed(total, 2).astype(F32)).astype(BF16)
    total = tied(total, found[5])
    total = (total.astype(F32) + crossed(total, 4).astype(F32)).astype(BF16)
    grad_x = dx_self.reshape(shape)
    half = parts_total // 2
    for order in (list(range(half)), list(range(half, parts_total))):
        grad_x = tiles_call(
            order,
            offsets,
            parts_total,
            True,
            feats,
            fixed,
            [found[mask] for mask in order] + [grad_x],
            like(shape, F32),
            24,
        )
    total, out = tied((total, out), found[3], found[7])
    grad_self, grad_neigh = small_call(
        finish_kernel,
        [like((width, full), F32)] * 2,
        [total, crossed(total, near)],
        [pltpu.VMEM((parts_total, piece, full), F32)],
    )
    return (out.reshape(rows, width), grad_x.reshape(rows, width), grad_self, grad_neigh)


def solution(mesh):
    def body(*args):
        rounds = args[7].shape[1]
        small = mesh.shape["dom"] == 8 and mesh.shape["feat"] == 4
        nearly_all = mesh.shape["dom"] <= rounds + 2
        return (dense_body if small and nearly_all else sparse_body)(*args)

    placed = (
        P("dom", "feat"),
        P("feat", None),
        P("feat", None),
        P("dom"),
        P("dom", None, None, None),
        P("dom", None),
        P("dom", None),
        P("dom", None, None, None, None),
        P("dom", None, None),
        P("dom", None, None),
        P("dom", "feat"),
    )
    return jax.shard_map(
        body,
        mesh=mesh,
        in_specs=placed,
        out_specs=(P("dom", "feat"), P("dom", "feat"), P("feat", None), P("feat", None)),
        check_vma=False,
    )
```

```python
import functools

import jax
import jax.numpy as jnp
from jax import lax
from jax.experimental import pallas as pl
from jax.experimental.pallas import tpu as pltpu
from jax.sharding import PartitionSpec as P

F32 = jnp.float32
BF16 = jnp.bfloat16
VMEM = pl.BlockSpec(memory_space=pltpu.VMEM)
SMEM = pl.BlockSpec(memory_space=pltpu.SMEM)


def shifted(x, axis, by):
    devices = lax.axis_size(axis)
    return lax.ppermute(x, axis, [(i, (i + by) % devices) for i in range(devices)])


def spread(parts, block_ids, count):
    table = (block_ids[:, None] == jnp.arange(count, dtype=jnp.int32)[None, :]).astype(F32)
    return jnp.einsum("kc,kif->cif", table, parts, precision=lax.Precision.HIGHEST)


def tile_apply(tiles, blocks):
    return jnp.einsum("kij,kjf->kif", tiles, blocks, preferred_element_type=F32)


def tile_apply_back(tiles, blocks):
    return jnp.einsum("kji,kjf->kif", tiles, blocks, preferred_element_type=F32)


def round_offsets(parts_total, rounds):
    return [(step + 1) * parts_total // (rounds + 1) for step in range(rounds)]


def sparse_body(
    features,
    w_self,
    w_neigh,
    degree,
    local_vals,
    local_dst,
    local_src,
    remote_vals,
    remote_dst,
    remote_src,
    cotangent,
):
    rows, width = features.shape
    block = local_vals.shape[-1]
    nblocks = rows // block
    rounds = remote_vals.shape[1]
    parts_total = lax.axis_size("dom")
    offsets = round_offsets(parts_total, rounds)
    blocks = features.reshape(nblocks, block, width)
    totals = spread(
        tile_apply(local_vals[0], jnp.take(blocks, local_src[0], axis=0)), local_dst[0], nblocks
    )
    arrived_ids = []
    for step in range(rounds):
        partial_blocks = tile_apply(
            remote_vals[0, step], jnp.take(blocks, remote_src[0, step], axis=0)
        ).astype(BF16)
        arrived, block_ids = shifted((partial_blocks, remote_dst[0, step]), "dom", offsets[step])
        arrived_ids.append(block_ids)
        totals = totals + spread(arrived.astype(F32), block_ids, nblocks)
    inverse = 1.0 / degree.astype(F32)
    agg = (totals.reshape(rows, width) * inverse[:, None]).astype(BF16)
    stacked = jnp.concatenate([features, agg], axis=1)
    weights = jnp.concatenate([w_self, w_neigh], axis=0)
    pre = lax.psum_scatter(
        lax.dot_general(weights, stacked, (((0,), (1,)), ((), ())), preferred_element_type=F32),
        "feat",
        scatter_dimension=0,
        tiled=True,
    ).T
    sigma = jax.nn.sigmoid(pre)
    out = (pre * sigma).astype(BF16)
    dpre = (cotangent.astype(F32) * sigma * (1.0 + pre * (1.0 - sigma))).astype(BF16)
    dpre_all = lax.all_gather(dpre, "feat", axis=1, tiled=True)
    dz_total = lax.dot_general(
        dpre_all, weights, (((1,), (1,)), ((), ())), preferred_element_type=F32
    )
    grad_local = lax.dot_general(
        stacked, dpre_all, (((0,), (0,)), ((), ())), preferred_element_type=F32
    )
    dx_self = dz_total[:, :width]
    dsum = (dz_total[:, width:] * inverse[:, None]).astype(BF16).reshape(nblocks, block, width)
    grad_all = lax.psum(grad_local, "dom")
    back = spread(
        tile_apply_back(local_vals[0], jnp.take(dsum, local_dst[0], axis=0)), local_src[0], nblocks
    )
    for step in range(rounds):
        picked = jnp.take(dsum, arrived_ids[step], axis=0)
        returned = shifted(picked, "dom", parts_total - offsets[step])
        back = back + spread(
            tile_apply_back(remote_vals[0, step], returned), remote_src[0, step], nblocks
        )
    grad_x = dx_self + back.reshape(rows, width)
    return (out, grad_x, grad_all[:width], grad_all[width:])


def tile_counts(rvals, lvals):
    return rvals.shape[0], rvals.shape[1], lvals.shape[0]


def round_of(offset, offsets):
    step, known = jnp.int32(0), offset < 0
    for at, this in enumerate(offsets):
        step = jnp.where(offset == this, at, step)
        known = known | (offset == this)
    return step, known


def crossed_block(block_id, mine, per_feat):
    return ((block_id // per_feat) ^ mine) * per_feat + block_id % per_feat


def tile_groups(masks, offsets, parts_total, me, groups, tiles):
    jobs = []
    for at, mask in enumerate(masks):
        if mask == 0:
            for first in range(0, tiles, groups):
                count = min(groups, tiles - first)
                jobs.append((at, None, None, first, count))
        else:
            offset = lax.rem((me ^ mask) - me + parts_total, parts_total)
            step, known = round_of(offset, offsets)
            jobs.append((at, step, known, None, groups))
    return jobs


def flat(masks):
    return [m for group in masks for m in (group if isinstance(group, list) else [group])]


def tiles_kernel(masks, offsets, parts_total, back, feats, extras, *refs):
    ids_in, (lvals, rvals), refs = refs[:4], refs[4:6], refs[6:]
    ids, id_sems, refs = refs[-5:-1], refs[-1], refs[:-5]
    id_copies = [
        pltpu.make_async_copy(ids_in[n], ids[n], id_sems.at[n]) for n in range(len(ids))
    ]
    for copy in id_copies:
        copy.start()
    groups_of, masks = masks, flat(masks)
    me = lax.axis_index("dom")
    mine = lax.axis_index("feat")
    rounds, groups, tiles = tile_counts(rvals, lvals)
    jobs = tile_groups(masks, offsets, parts_total, me, groups, tiles)
    held, prod, acc, sems = refs[-4:]
    copies = []
    for slot, (at, step, known, first, count) in enumerate(jobs):
        source = lvals.at[pl.ds(first, count)] if step is None else rvals.at[step]
        copy = pltpu.make_async_copy(source, held.at[slot, pl.ds(0, count)], sems.at[slot])
        copy.start()
        copies.append(copy)
    if back:
        own_ref, grad_ref = refs[len(masks)], refs[len(masks) + 1]
        blocks = refs[: len(masks)]
        sinks = [grad_ref] * len(masks)
        acc[0] = own_ref[...]
    else:
        blocks = [refs[0]] * len(masks)
        sinks, used = [], 1 + extras
        for group in groups_of:
            if isinstance(group, list):
                sinks += [refs[used].at[n] for n in range(len(group))]
            else:
                sinks.append(refs[used])
            used += 1
    if extras:
        pieces, pair = refs[used : used + feats], refs[used + feats]
        pair[0] = refs[2][...]
        pair[1] = refs[3][...]
        for mask, piece in enumerate(pieces):
            rows = pl.ds((mine ^ mask) * piece.shape[1], piece.shape[1])
            piece[0] = refs[0][rows]
            piece[1] = refs[1][rows]
    total = 0
    for copy in id_copies:
        copy.wait()
    ldst, lsrc, rdst, rsrc = ids
    for slot, (at, step, known, first, count) in enumerate(jobs):
        copies[slot].wait()
        if step is None:
            dst = [ldst[0, first + k] for k in range(count)]
            src = [lsrc[0, first + k] for k in range(count)]
        else:
            dst = [rdst[step, 0, k] for k in range(count)]
            src = [rsrc[step, 0, k] for k in range(count)]
        half = slot % 2
        for k in range(len(dst)):
            if back:
                per_feat = blocks[at].shape[0] // feats
                block = blocks[at][crossed_block(dst[k], mine, per_feat)]
                product = lax.dot_general(
                    held[slot, k], block, (((0,), (0,)), ((), ())), preferred_element_type=F32
                )
            else:
                product = jnp.dot(
                    held[slot, k], blocks[at][src[k]], preferred_element_type=F32
                )
            prod[half, k] = product if known is None else jnp.where(known, product, 0.0)
        fresh = not back and (slot == 0 or jobs[slot - 1][0] != at)
        if fresh:
            total = at % 2
            acc[total] = jnp.zeros(acc.shape[1:], F32)
        for k in range(len(dst)):
            into = src[k] if back else dst[k]
            acc[total, into] = acc[total, into] + prod[half, k]
        last = slot == len(jobs) - 1 or jobs[slot + 1][0] != at
        if last and (not back or slot == len(jobs) - 1):
            sinks[at][...] = acc[total].astype(sinks[at].dtype)


def tiles_call(masks, offsets, parts_total, back, feats, fixed, blocks, sinks, room):
    ids, lvals, rvals = fixed
    rounds, groups, tiles = tile_counts(rvals, lvals)
    nblocks, block, width = blocks[0].shape
    slots = sum(-(-tiles // groups) if mask == 0 else 1 for mask in flat(masks))
    extras = 0 if back else len(blocks) - 1
    return pl.pallas_call(
        functools.partial(tiles_kernel, masks, offsets, parts_total, back, feats, extras),
        out_shape=sinks,
        in_specs=[pl.BlockSpec(memory_space=pltpu.HBM)] * 6
        + [VMEM] * len(blocks),
        out_specs=jax.tree.map(lambda _: VMEM, sinks),
        scratch_shapes=[
            pltpu.VMEM((slots, groups, block, block), BF16),
            pltpu.VMEM((2, groups, block, width), F32),
            pltpu.VMEM((2, nblocks, block, width), F32),
            pltpu.SemaphoreType.DMA((slots,)),
            *[pltpu.SMEM(t.shape, jnp.int32) for t in ids],
            pltpu.SemaphoreType.DMA((len(ids),)),
        ],
        compiler_params=pltpu.CompilerParams(vmem_limit_bytes=room * 2**20),
        cost_estimate=pl.CostEstimate(flops=1, bytes_accessed=1, transcendentals=0),
    )(*ids, lvals, rvals, *blocks)


def small_call(kernel, outs, arrays, scratch=(), room=24):
    return pl.pallas_call(
        kernel,
        out_shape=outs,
        in_specs=[VMEM] * len(arrays),
        out_specs=[VMEM] * len(outs),
        scratch_shapes=scratch,
        compiler_params=pltpu.CompilerParams(vmem_limit_bytes=room * 2**20),
        cost_estimate=pl.CostEstimate(flops=1, bytes_accessed=1, transcendentals=0),
    )(*arrays)


def agg_kernel(feats, inv_ref, keep_ref, *refs):
    mine = lax.axis_index("feat")
    far_refs, agg_ref, piece_refs = refs[: -1 - feats], refs[-1 - feats], refs[-feats:]
    per_feat = piece_refs[0].shape[0]
    sums = keep_ref[...]
    for ref in far_refs:
        sums = sums + ref[...].astype(F32)
    agg_ref[...] = (sums * inv_ref[...]).astype(BF16)
    for mask, piece in enumerate(piece_refs):
        piece[...] = agg_ref[pl.ds((mine ^ mask) * per_feat, per_feat)]


def joined(parts):
    return jnp.concatenate(parts, axis=1)


def dense_kernel(feats, inv_ref, *refs):
    mine = lax.axis_index("feat")
    w_refs, early_refs, a_refs = refs[:feats], refs[feats : 2 * feats], refs[2 * feats : 3 * feats]
    sent_refs, own_ref = refs[3 * feats : 4 * feats - 1], refs[4 * feats - 1]
    dsum_refs = refs[4 * feats : 5 * feats]
    held = refs[-1]
    full = w_refs[0].shape[2]
    some, width = held.shape[1:]
    pre = jnp.zeros((some, full), F32)
    for mask in range(feats):
        early = early_refs[mask]
        pre = pre + jnp.dot(
            early[0].reshape(some, width), w_refs[mask][0], preferred_element_type=F32
        )
        pre = pre + jnp.dot(
            a_refs[mask][...].reshape(some, width), w_refs[mask][1], preferred_element_type=F32
        )
        held[mine ^ mask] = early[1].reshape(some, width)
    sigma = 1.0 / (1.0 + jnp.exp(-pre))
    out = (pre * sigma).astype(BF16)
    cot = joined([held[j] for j in range(feats)]).astype(F32)
    dpre = (cot * sigma * (1.0 + pre * (1.0 - sigma))).astype(BF16)
    for mask in range(feats):
        dagg = lax.dot_general(
            dpre, w_refs[mask][1], (((1,), (1,)), ((), ())), preferred_element_type=F32
        )
        dsum_refs[mask][...] = (dagg * inv_ref[...]).astype(BF16)
    for j in range(feats):
        cols = slice(j * width, (j + 1) * width)
        for sent in sent_refs:
            sent[j] = dpre[:, cols]
        held[j] = out[:, cols]
    own_ref[...] = held[mine]
    for mask, sent in enumerate(sent_refs, 1):
        sent[feats] = held[mine ^ mask]


def grad_kernel(feats, f_ref, a_ref, w_ref, *refs):
    me = lax.axis_index("dom")
    mine = lax.axis_index("feat")
    dpre_refs, (dx_ref, give_ref, keep_ref, held) = refs[:feats], refs[feats:]
    width = f_ref.shape[1]
    piece = held.shape[1]
    some = dpre_refs[0].shape[1]
    parts = [0.0, 0.0]
    for mask, dpre_ref in enumerate(dpre_refs):
        dpre = joined([dpre_ref[j] for j in range(feats)])
        rows = pl.ds(pl.multiple_of((mine ^ mask) * some, some), some)
        for at, ref in enumerate((f_ref, a_ref)):
            parts[at] = parts[at] + lax.dot_general(
                ref[rows], dpre, (((0,), (0,)), ((), ())), preferred_element_type=F32
            )
        dx_ref[rows] = lax.dot_general(
            dpre, w_ref[...], (((1,), (1,)), ((), ())), preferred_element_type=F32
        )
    for at, part in enumerate(parts):
        for j in range(width // piece):
            held[at * (width // piece) + j] = part[j * piece : (j + 1) * piece]
    side = me % 2
    for at in range(give_ref.shape[0]):
        give_ref[at] = held[2 * at + 1 - side].astype(BF16)
        keep_ref[at] = held[2 * at + side]


def finish_kernel(mine_ref, other_ref, self_ref, neigh_ref, held):
    side = lax.axis_index("dom") % 2
    for at in range(mine_ref.shape[0]):
        held[2 * at + side] = mine_ref[at].astype(F32)
        held[2 * at + 1 - side] = other_ref[at].astype(F32)
    some = held.shape[1]
    half = held.shape[0] // 2
    for j in range(half):
        self_ref[j * some : (j + 1) * some] = held[j]
        neigh_ref[j * some : (j + 1) * some] = held[half + j]


def place_kernel(*refs):
    mine = lax.axis_index("feat")
    own_ref, *come_refs, out_ref = refs
    out_ref[mine] = own_ref[...]
    for mask, come in enumerate(come_refs, 1):
        out_ref[mine ^ mask] = come[out_ref.shape[0]]


def swap_feat(x):
    return lax.all_to_all(x, "feat", split_axis=0, concat_axis=0, tiled=True)


def crossed(x, mask, axis="dom"):
    return lax.ppermute(x, axis, [(i, i ^ mask) for i in range(lax.axis_size(axis))])


def like(shape, dtype):
    return jax.ShapeDtypeStruct(shape, dtype)


def dense_body(
    features,
    w_self,
    w_neigh,
    degree,
    local_vals,
    local_dst,
    local_src,
    remote_vals,
    remote_dst,
    remote_src,
    cotangent,
):
    rows, width = features.shape
    block = local_vals.shape[-1]
    nblocks = rows // block
    rounds = remote_vals.shape[1]
    parts_total = lax.axis_size("dom")
    feats = lax.axis_size("feat")
    some = rows // feats
    per_feat = nblocks // feats
    full = feats * width
    offsets = round_offsets(parts_total, rounds)
    near, far = 1, list(range(parts_total - 2, 0, -2))
    bits = [1, 2, 4]
    mine = lax.axis_index("feat").astype(jnp.int32)
    inverse = 1.0 / degree.astype(F32)
    inv_rows = lax.dynamic_slice(inverse, (mine * some,), (some,))[:, None]
    ids = (
        local_dst,
        local_src,
        jnp.swapaxes(remote_dst, 0, 1),
        jnp.swapaxes(remote_src, 0, 1),
    )
    shape = (nblocks, block, width)
    blocks = features.reshape(shape)
    fixed = (ids, local_vals[0], remote_vals[0])

    def forward(masks, arrays, sinks):
        return tiles_call(
            masks, offsets, parts_total, False, feats, fixed, arrays, sinks, 62
        )

    def relayed(x):
        over = crossed(x, 2, "feat")
        return [x, crossed(x, 1, "feat"), over, crossed(over, 1, "feat")]

    def tied(x, *others):
        return lax.optimization_barrier((x, others))[0]

    sends = forward([7, 5, 3, 1], [blocks], [like(shape, BF16)] * 4)
    made = forward(
        [6, 4, 2, 0],
        [blocks, cotangent.reshape(shape), w_self, w_neigh],
        [like(shape, F32)] * 4
        + [like((2, per_feat, block, width), BF16)] * feats
        + [like((2, width, full), BF16)],
    )
    keep_6, keep_4, keep_2, keep = made[:4]
    early_pieces, pair = made[4:-1], made[-1]
    weights = relayed(pair)
    near_6, near_4, near_2 = (crossed(send, near) for send in sends[:3])
    sum_6 = (keep_6 + near_6.astype(F32)).astype(BF16)
    near_4, weights[2] = lax.optimization_barrier((near_4, weights[2]))
    sum_4 = (keep_4 + near_4.astype(F32) + crossed(sum_6, 2).astype(F32)).astype(BF16)
    far_0 = crossed(sum_4, 4)
    keep_2, send_1, early_pieces = tied((keep_2, sends[3], early_pieces), sum_4)
    near_0 = crossed(send_1, near)
    sum_2 = (keep_2 + near_2.astype(F32)).astype(BF16)
    mid_0 = crossed(sum_2, 2)
    early_2, early_3 = crossed(early_pieces[2], 2, "feat"), crossed(early_pieces[3], 3, "feat")
    far_0, early_2, early_3, early_1 = lax.optimization_barrier(
        (far_0, early_2, early_3, early_pieces[1])
    )
    early = [early_pieces[0], crossed(early_1, 1, "feat"), early_2, early_3]
    part = keep + mid_0.astype(F32) + near_0.astype(F32)
    arrived = [far_0]
    early, weights, arrived = lax.optimization_barrier((early, weights, arrived))
    agg, *agg_pieces = small_call(
        functools.partial(agg_kernel, feats),
        [like(shape, BF16)] + [like((per_feat, block, width), BF16)] * feats,
        [inverse.reshape(nblocks, block, 1), part, *arrived],
    )
    agg_rows = [agg_pieces[0]] + [crossed(agg_pieces[m], m, "feat") for m in range(1, feats)]
    *sent, own_out, p0, p1, p2, p3 = small_call(
        functools.partial(dense_kernel, feats),
        [like((feats + 1, some, width), BF16)] * (feats - 1)
        + [like((some, width), BF16)] * (1 + feats),
        [inv_rows, *weights, *early, *agg_rows],
        [pltpu.VMEM((feats, some, width), BF16)],
    )
    dsum_pieces = [p0, p1, p2, p3]
    dsum = jnp.concatenate(
        [dsum_pieces[0]] + [crossed(dsum_pieces[m], m, "feat") for m in range(1, feats)], axis=0
    ).reshape(shape)
    found = {0: dsum}
    for mask in (4, 2, 1):
        found[mask] = crossed(dsum, mask)
    sent = tied(sent, dsum)
    come_2, come_3 = crossed(sent[1], 2, "feat"), crossed(sent[2], 3, "feat")
    found[4], come_2, come_3, found[2], found[1], sent[0] = lax.optimization_barrier(
        (found[4], come_2, come_3, found[2], found[1], sent[0])
    )
    come = [crossed(sent[0], 1, "feat"), come_2, come_3]
    (out,) = small_call(place_kernel, [like((feats, some, width), BF16)], [own_out, *come])
    dpre = [sent[0], *come]
    found[6] = crossed(found[4], 2)
    found[3] = crossed(found[2], near)
    found[5] = crossed(found[4], near)
    found[7] = crossed(tied(found[5], found[6]), 2)
    piece = 2 * width // parts_total
    dx_self, give, keep = small_call(
        functools.partial(grad_kernel, feats),
        [
            like((rows, width), F32),
            like((len(far) + 1, piece, full), BF16),
            like((len(far) + 1, piece, full), F32),
        ],
        [features, agg.reshape(rows, width), w_self, *dpre],
        [pltpu.VMEM((parts_total, piece, full), F32)],
    )
    total = (keep + crossed(give, near).astype(F32)).astype(BF16)
    total = (total.astype(F32) + crossed(total, 2).astype(F32)).astype(BF16)
    total = (total.astype(F32) + crossed(total, 4).astype(F32)).astype(BF16)
    grad_x = dx_self.reshape(shape)
    half = parts_total // 2
    for order in (list(range(half)), list(range(half, parts_total))):
        grad_x = tiles_call(
            order,
            offsets,
            parts_total,
            True,
            feats,
            fixed,
            [found[mask] for mask in order] + [grad_x],
            like(shape, F32),
            24,
        )
    total, out = tied((total, out), found[3], found[7])
    grad_self, grad_neigh = small_call(
        finish_kernel,
        [like((width, full), F32)] * 2,
        [total, crossed(total, near)],
        [pltpu.VMEM((parts_total, piece, full), F32)],
    )
    return (out.reshape(rows, width), grad_x.reshape(rows, width), grad_self, grad_neigh)


def solution(mesh):
    def body(*args):
        rounds = args[7].shape[1]
        small = mesh.shape["dom"] == 8 and mesh.shape["feat"] == 4
        nearly_all = mesh.shape["dom"] <= rounds + 2
        return (dense_body if small and nearly_all else sparse_body)(*args)

    placed = (
        P("dom", "feat"),
        P("feat", None),
        P("feat", None),
        P("dom"),
        P("dom", None, None, None),
        P("dom", None),
        P("dom", None),
        P("dom", None, None, None, None),
        P("dom", None, None),
        P("dom", None, None),
        P("dom", "feat"),
    )
    return jax.shard_map(
        body,
        mesh=mesh,
        in_specs=placed,
        out_specs=(P("dom", "feat"), P("dom", "feat"), P("feat", None), P("feat", None)),
        check_vma=False,
    )
```

```python
import functools

import jax
import jax.numpy as jnp
from jax import lax
from jax.experimental import pallas as pl
from jax.experimental.pallas import tpu as pltpu
from jax.sharding import PartitionSpec as P

F32 = jnp.float32
BF16 = jnp.bfloat16
VMEM = pl.BlockSpec(memory_space=pltpu.VMEM)
SMEM = pl.BlockSpec(memory_space=pltpu.SMEM)


def shifted(x, axis, by):
    devices = lax.axis_size(axis)
    return lax.ppermute(x, axis, [(i, (i + by) % devices) for i in range(devices)])


def spread(parts, block_ids, count):
    table = (block_ids[:, None] == jnp.arange(count, dtype=jnp.int32)[None, :]).astype(F32)
    return jnp.einsum("kc,kif->cif", table, parts, precision=lax.Precision.HIGHEST)


def tile_apply(tiles, blocks):
    return jnp.einsum("kij,kjf->kif", tiles, blocks, preferred_element_type=F32)


def tile_apply_back(tiles, blocks):
    return jnp.einsum("kji,kjf->kif", tiles, blocks, preferred_element_type=F32)


def round_offsets(parts_total, rounds):
    return [(step + 1) * parts_total // (rounds + 1) for step in range(rounds)]


def sparse_body(
    features,
    w_self,
    w_neigh,
    degree,
    local_vals,
    local_dst,
    local_src,
    remote_vals,
    remote_dst,
    remote_src,
    cotangent,
):
    rows, width = features.shape
    block = local_vals.shape[-1]
    nblocks = rows // block
    rounds = remote_vals.shape[1]
    parts_total = lax.axis_size("dom")
    offsets = round_offsets(parts_total, rounds)
    blocks = features.reshape(nblocks, block, width)
    totals = spread(
        tile_apply(local_vals[0], jnp.take(blocks, local_src[0], axis=0)), local_dst[0], nblocks
    )
    arrived_ids = []
    for step in range(rounds):
        partial_blocks = tile_apply(
            remote_vals[0, step], jnp.take(blocks, remote_src[0, step], axis=0)
        ).astype(BF16)
        arrived, block_ids = shifted((partial_blocks, remote_dst[0, step]), "dom", offsets[step])
        arrived_ids.append(block_ids)
        totals = totals + spread(arrived.astype(F32), block_ids, nblocks)
    inverse = 1.0 / degree.astype(F32)
    agg = (totals.reshape(rows, width) * inverse[:, None]).astype(BF16)
    stacked = jnp.concatenate([features, agg], axis=1)
    weights = jnp.concatenate([w_self, w_neigh], axis=0)
    pre = lax.psum_scatter(
        lax.dot_general(weights, stacked, (((0,), (1,)), ((), ())), preferred_element_type=F32),
        "feat",
        scatter_dimension=0,
        tiled=True,
    ).T
    sigma = jax.nn.sigmoid(pre)
    out = (pre * sigma).astype(BF16)
    dpre = (cotangent.astype(F32) * sigma * (1.0 + pre * (1.0 - sigma))).astype(BF16)
    dpre_all = lax.all_gather(dpre, "feat", axis=1, tiled=True)
    dz_total = lax.dot_general(
        dpre_all, weights, (((1,), (1,)), ((), ())), preferred_element_type=F32
    )
    grad_local = lax.dot_general(
        stacked, dpre_all, (((0,), (0,)), ((), ())), preferred_element_type=F32
    )
    dx_self = dz_total[:, :width]
    dsum = (dz_total[:, width:] * inverse[:, None]).astype(BF16).reshape(nblocks, block, width)
    grad_all = lax.psum(grad_local, "dom")
    back = spread(
        tile_apply_back(local_vals[0], jnp.take(dsum, local_dst[0], axis=0)), local_src[0], nblocks
    )
    for step in range(rounds):
        picked = jnp.take(dsum, arrived_ids[step], axis=0)
        returned = shifted(picked, "dom", parts_total - offsets[step])
        back = back + spread(
            tile_apply_back(remote_vals[0, step], returned), remote_src[0, step], nblocks
        )
    grad_x = dx_self + back.reshape(rows, width)
    return (out, grad_x, grad_all[:width], grad_all[width:])


def tile_counts(rvals, lvals):
    return rvals.shape[0], rvals.shape[1], lvals.shape[0]


def round_of(offset, offsets):
    step, known = jnp.int32(0), offset < 0
    for at, this in enumerate(offsets):
        step = jnp.where(offset == this, at, step)
        known = known | (offset == this)
    return step, known


def crossed_block(block_id, mine, per_feat):
    return ((block_id // per_feat) ^ mine) * per_feat + block_id % per_feat


def tile_groups(masks, offsets, parts_total, me, groups, tiles):
    jobs = []
    for at, mask in enumerate(masks):
        if mask == 0:
            for first in range(0, tiles, groups):
                count = min(groups, tiles - first)
                jobs.append((at, None, None, first, count))
        else:
            offset = lax.rem((me ^ mask) - me + parts_total, parts_total)
            step, known = round_of(offset, offsets)
            jobs.append((at, step, known, None, groups))
    return jobs


def flat(masks):
    return [m for group in masks for m in (group if isinstance(group, list) else [group])]


def tiles_kernel(masks, offsets, parts_total, back, feats, extras, *refs):
    ids_in, (lvals, rvals), refs = refs[:4], refs[4:6], refs[6:]
    ids, id_sems, refs = refs[-5:-1], refs[-1], refs[:-5]
    id_copies = [
        pltpu.make_async_copy(ids_in[n], ids[n], id_sems.at[n]) for n in range(len(ids))
    ]
    for copy in id_copies:
        copy.start()
    groups_of, masks = masks, flat(masks)
    me = lax.axis_index("dom")
    mine = lax.axis_index("feat")
    rounds, groups, tiles = tile_counts(rvals, lvals)
    jobs = tile_groups(masks, offsets, parts_total, me, groups, tiles)
    held, prod, acc, sems = refs[-4:]
    copies = []
    for slot, (at, step, known, first, count) in enumerate(jobs):
        source = lvals.at[pl.ds(first, count)] if step is None else rvals.at[step]
        copy = pltpu.make_async_copy(source, held.at[slot, pl.ds(0, count)], sems.at[slot])
        copy.start()
        copies.append(copy)
    if back:
        own_ref, grad_ref = refs[len(masks)], refs[len(masks) + 1]
        blocks = refs[: len(masks)]
        sinks = [grad_ref] * len(masks)
        acc[0] = own_ref[...]
    else:
        blocks = [refs[0]] * len(masks)
        sinks, used = [], 1 + extras
        for group in groups_of:
            if isinstance(group, list):
                sinks += [refs[used].at[n] for n in range(len(group))]
            else:
                sinks.append(refs[used])
            used += 1
    if extras:
        pieces, pair = refs[used : used + feats], refs[used + feats]
        pair[0] = refs[2][...]
        pair[1] = refs[3][...]
        for mask, piece in enumerate(pieces):
            rows = pl.ds((mine ^ mask) * piece.shape[1], piece.shape[1])
            piece[0] = refs[0][rows]
            piece[1] = refs[1][rows]
    total = 0
    for copy in id_copies:
        copy.wait()
    ldst, lsrc, rdst, rsrc = ids
    for slot, (at, step, known, first, count) in enumerate(jobs):
        copies[slot].wait()
        if step is None:
            dst = [ldst[0, first + k] for k in range(count)]
            src = [lsrc[0, first + k] for k in range(count)]
        else:
            dst = [rdst[step, 0, k] for k in range(count)]
            src = [rsrc[step, 0, k] for k in range(count)]
        half = slot % 2
        for k in range(len(dst)):
            if back:
                per_feat = blocks[at].shape[0] // feats
                block = blocks[at][crossed_block(dst[k], mine, per_feat)]
                product = lax.dot_general(
                    held[slot, k], block, (((0,), (0,)), ((), ())), preferred_element_type=F32
                )
            else:
                product = jnp.dot(
                    held[slot, k], blocks[at][src[k]], preferred_element_type=F32
                )
            prod[half, k] = product if known is None else jnp.where(known, product, 0.0)
        fresh = not back and (slot == 0 or jobs[slot - 1][0] != at)
        if fresh:
            total = at % 2
            acc[total] = jnp.zeros(acc.shape[1:], F32)
        for k in range(len(dst)):
            into = src[k] if back else dst[k]
            acc[total, into] = acc[total, into] + prod[half, k]
        last = slot == len(jobs) - 1 or jobs[slot + 1][0] != at
        if last and (not back or slot == len(jobs) - 1):
            sinks[at][...] = acc[total].astype(sinks[at].dtype)


def tiles_call(masks, offsets, parts_total, back, feats, fixed, blocks, sinks, room):
    ids, lvals, rvals = fixed
    rounds, groups, tiles = tile_counts(rvals, lvals)
    nblocks, block, width = blocks[0].shape
    slots = sum(-(-tiles // groups) if mask == 0 else 1 for mask in flat(masks))
    extras = 0 if back else len(blocks) - 1
    return pl.pallas_call(
        functools.partial(tiles_kernel, masks, offsets, parts_total, back, feats, extras),
        out_shape=sinks,
        in_specs=[pl.BlockSpec(memory_space=pltpu.HBM)] * 6
        + [VMEM] * len(blocks),
        out_specs=jax.tree.map(lambda _: VMEM, sinks),
        scratch_shapes=[
            pltpu.VMEM((slots, groups, block, block), BF16),
            pltpu.VMEM((2, groups, block, width), F32),
            pltpu.VMEM((2, nblocks, block, width), F32),
            pltpu.SemaphoreType.DMA((slots,)),
            *[pltpu.SMEM(t.shape, jnp.int32) for t in ids],
            pltpu.SemaphoreType.DMA((len(ids),)),
        ],
        compiler_params=pltpu.CompilerParams(vmem_limit_bytes=room * 2**20),
        cost_estimate=pl.CostEstimate(flops=1, bytes_accessed=1, transcendentals=0),
    )(*ids, lvals, rvals, *blocks)


def small_call(kernel, outs, arrays, scratch=(), room=24):
    return pl.pallas_call(
        kernel,
        out_shape=outs,
        in_specs=[VMEM] * len(arrays),
        out_specs=[VMEM] * len(outs),
        scratch_shapes=scratch,
        compiler_params=pltpu.CompilerParams(vmem_limit_bytes=room * 2**20),
        cost_estimate=pl.CostEstimate(flops=1, bytes_accessed=1, transcendentals=0),
    )(*arrays)


def agg_kernel(feats, inv_ref, keep_ref, *refs):
    mine = lax.axis_index("feat")
    far_refs, agg_ref, piece_refs = refs[: -1 - feats], refs[-1 - feats], refs[-feats:]
    per_feat = piece_refs[0].shape[0]
    sums = keep_ref[...]
    for ref in far_refs:
        sums = sums + ref[...].astype(F32)
    agg_ref[...] = (sums * inv_ref[...]).astype(BF16)
    for mask, piece in enumerate(piece_refs):
        piece[...] = agg_ref[pl.ds((mine ^ mask) * per_feat, per_feat)]


def joined(parts):
    return jnp.concatenate(parts, axis=1)


def dense_kernel(feats, inv_ref, *refs):
    mine = lax.axis_index("feat")
    w_refs, early_refs, a_refs = refs[:feats], refs[feats : 2 * feats], refs[2 * feats : 3 * feats]
    sent_refs, own_ref = refs[3 * feats : 4 * feats - 1], refs[4 * feats - 1]
    dsum_refs = refs[4 * feats : 5 * feats]
    held = refs[-1]
    full = w_refs[0].shape[2]
    some, width = held.shape[1:]
    pre = jnp.zeros((some, full), F32)
    for mask in range(feats):
        early = early_refs[mask]
        pre = pre + jnp.dot(
            early[0].reshape(some, width), w_refs[mask][0], preferred_element_type=F32
        )
        pre = pre + jnp.dot(
            a_refs[mask][...].reshape(some, width), w_refs[mask][1], preferred_element_type=F32
        )
        held[mine ^ mask] = early[1].reshape(some, width)
    sigma = 1.0 / (1.0 + jnp.exp(-pre))
    out = (pre * sigma).astype(BF16)
    cot = joined([held[j] for j in range(feats)]).astype(F32)
    dpre = (cot * sigma * (1.0 + pre * (1.0 - sigma))).astype(BF16)
    for mask in range(feats):
        dagg = lax.dot_general(
            dpre, w_refs[mask][1], (((1,), (1,)), ((), ())), preferred_element_type=F32
        )
        dsum_refs[mask][...] = (dagg * inv_ref[...]).astype(BF16)
    for j in range(feats):
        cols = slice(j * width, (j + 1) * width)
        for sent in sent_refs:
            sent[j] = dpre[:, cols]
        held[j] = out[:, cols]
    own_ref[...] = held[mine]
    for mask, sent in enumerate(sent_refs, 1):
        sent[feats] = held[mine ^ mask]


def grad_kernel(feats, f_ref, a_ref, w_ref, *refs):
    me = lax.axis_index("dom")
    mine = lax.axis_index("feat")
    dpre_refs, (dx_ref, give_ref, keep_ref, held) = refs[:feats], refs[feats:]
    width = f_ref.shape[1]
    piece = held.shape[1]
    some = dpre_refs[0].shape[1]
    parts = [0.0, 0.0]
    for mask, dpre_ref in enumerate(dpre_refs):
        dpre = joined([dpre_ref[j] for j in range(feats)])
        rows = pl.ds(pl.multiple_of((mine ^ mask) * some, some), some)
        for at, ref in enumerate((f_ref, a_ref)):
            parts[at] = parts[at] + lax.dot_general(
                ref[rows], dpre, (((0,), (0,)), ((), ())), preferred_element_type=F32
            )
        dx_ref[rows] = lax.dot_general(
            dpre, w_ref[...], (((1,), (1,)), ((), ())), preferred_element_type=F32
        )
    for at, part in enumerate(parts):
        for j in range(width // piece):
            held[at * (width // piece) + j] = part[j * piece : (j + 1) * piece]
    side = me % 2
    for at in range(give_ref.shape[0]):
        give_ref[at] = held[2 * at + 1 - side].astype(BF16)
        keep_ref[at] = held[2 * at + side]


def finish_kernel(mine_ref, other_ref, self_ref, neigh_ref, held):
    side = lax.axis_index("dom") % 2
    for at in range(mine_ref.shape[0]):
        held[2 * at + side] = mine_ref[at].astype(F32)
        held[2 * at + 1 - side] = other_ref[at].astype(F32)
    some = held.shape[1]
    half = held.shape[0] // 2
    for j in range(half):
        self_ref[j * some : (j + 1) * some] = held[j]
        neigh_ref[j * some : (j + 1) * some] = held[half + j]


def place_kernel(*refs):
    mine = lax.axis_index("feat")
    own_ref, *come_refs, out_ref = refs
    out_ref[mine] = own_ref[...]
    for mask, come in enumerate(come_refs, 1):
        out_ref[mine ^ mask] = come[out_ref.shape[0]]


def swap_feat(x):
    return lax.all_to_all(x, "feat", split_axis=0, concat_axis=0, tiled=True)


def crossed(x, mask, axis="dom"):
    return lax.ppermute(x, axis, [(i, i ^ mask) for i in range(lax.axis_size(axis))])


def like(shape, dtype):
    return jax.ShapeDtypeStruct(shape, dtype)


def dense_body(
    features,
    w_self,
    w_neigh,
    degree,
    local_vals,
    local_dst,
    local_src,
    remote_vals,
    remote_dst,
    remote_src,
    cotangent,
):
    rows, width = features.shape
    block = local_vals.shape[-1]
    nblocks = rows // block
    rounds = remote_vals.shape[1]
    parts_total = lax.axis_size("dom")
    feats = lax.axis_size("feat")
    some = rows // feats
    per_feat = nblocks // feats
    full = feats * width
    offsets = round_offsets(parts_total, rounds)
    near, far = 1, list(range(parts_total - 2, 0, -2))
    bits = [1, 2, 4]
    mine = lax.axis_index("feat").astype(jnp.int32)
    inverse = 1.0 / degree.astype(F32)
    inv_rows = lax.dynamic_slice(inverse, (mine * some,), (some,))[:, None]
    ids = (
        local_dst,
        local_src,
        jnp.swapaxes(remote_dst, 0, 1),
        jnp.swapaxes(remote_src, 0, 1),
    )
    shape = (nblocks, block, width)
    blocks = features.reshape(shape)
    fixed = (ids, local_vals[0], remote_vals[0])

    def forward(masks, arrays, sinks):
        return tiles_call(
            masks, offsets, parts_total, False, feats, fixed, arrays, sinks, 62
        )

    def relayed(x):
        over = crossed(x, 2, "feat")
        return [x, crossed(x, 1, "feat"), over, crossed(over, 1, "feat")]

    def tied(x, *others):
        return lax.optimization_barrier((x, others))[0]

    sends = forward([7, 5, 3, 1], [blocks], [like(shape, BF16)] * 4)
    made = forward(
        [6, 4, 2, 0],
        [blocks, cotangent.reshape(shape), w_self, w_neigh],
        [like(shape, F32)] * 4
        + [like((2, per_feat, block, width), BF16)] * feats
        + [like((2, width, full), BF16)],
    )
    keep_6, keep_4, keep_2, keep = made[:4]
    early_pieces, pair = made[4:-1], made[-1]
    weights = relayed(pair)
    near_6, near_4, near_2 = (crossed(send, near) for send in sends[:3])
    sum_6 = (keep_6 + near_6.astype(F32)).astype(BF16)
    near_4, weights[2] = lax.optimization_barrier((near_4, weights[2]))
    sum_4 = (keep_4 + near_4.astype(F32) + crossed(sum_6, 2).astype(F32)).astype(BF16)
    far_0 = crossed(sum_4, 4)
    keep_2, send_1, early_pieces = tied((keep_2, sends[3], early_pieces), sum_4)
    near_0 = crossed(send_1, near)
    sum_2 = (keep_2 + near_2.astype(F32)).astype(BF16)
    mid_0 = crossed(sum_2, 2)
    early_2, early_3 = crossed(early_pieces[2], 2, "feat"), crossed(early_pieces[3], 3, "feat")
    far_0, early_2, early_3, early_1 = lax.optimization_barrier(
        (far_0, early_2, early_3, early_pieces[1])
    )
    early = [early_pieces[0], crossed(early_1, 1, "feat"), early_2, early_3]
    part = keep + mid_0.astype(F32) + near_0.astype(F32)
    arrived = [far_0]
    early, weights, arrived = lax.optimization_barrier((early, weights, arrived))
    agg, *agg_pieces = small_call(
        functools.partial(agg_kernel, feats),
        [like(shape, BF16)] + [like((per_feat, block, width), BF16)] * feats,
        [inverse.reshape(nblocks, block, 1), part, *arrived],
    )
    agg_rows = [agg_pieces[0]] + [crossed(agg_pieces[m], m, "feat") for m in range(1, feats)]
    *sent, own_out, p0, p1, p2, p3 = small_call(
        functools.partial(dense_kernel, feats),
        [like((feats + 1, some, width), BF16)] * (feats - 1)
        + [like((some, width), BF16)] * (1 + feats),
        [inv_rows, *weights, *early, *agg_rows],
        [pltpu.VMEM((feats, some, width), BF16)],
    )
    dsum_pieces = [p0, p1, p2, p3]
    dsum = jnp.concatenate(
        [dsum_pieces[0]] + [crossed(dsum_pieces[m], m, "feat") for m in range(1, feats)], axis=0
    ).reshape(shape)
    found = {0: dsum}
    for mask in (4, 2, 1):
        found[mask] = crossed(dsum, mask)
    sent = tied(sent, dsum)
    come_2, come_3 = crossed(sent[1], 2, "feat"), crossed(sent[2], 3, "feat")
    found[4], come_2, come_3, found[2], found[1], sent[0] = lax.optimization_barrier(
        (found[4], come_2, come_3, found[2], found[1], sent[0])
    )
    come = [crossed(sent[0], 1, "feat"), come_2, come_3]
    (out,) = small_call(place_kernel, [like((feats, some, width), BF16)], [own_out, *come])
    dpre = [sent[0], *come]
    found[6] = crossed(found[4], 2)
    found[3] = crossed(found[2], near)
    found[5] = crossed(found[4], near)
    found[7] = crossed(tied(found[5], found[6]), 2)
    piece = 2 * width // parts_total
    dx_self, give, keep = small_call(
        functools.partial(grad_kernel, feats),
        [
            like((rows, width), F32),
            like((len(far) + 1, piece, full), BF16),
            like((len(far) + 1, piece, full), F32),
        ],
        [features, agg.reshape(rows, width), w_self, *dpre],
        [pltpu.VMEM((parts_total, piece, full), F32)],
    )
    total = (keep + crossed(give, near).astype(F32)).astype(BF16)
    total = (total.astype(F32) + crossed(total, 2).astype(F32)).astype(BF16)
    total = (total.astype(F32) + crossed(total, 4).astype(F32)).astype(BF16)
    grad_x = dx_self.reshape(shape)
    half = parts_total // 2
    for order in (list(range(half)), list(range(half, parts_total))):
        grad_x = tiles_call(
            order,
            offsets,
            parts_total,
            True,
            feats,
            fixed,
            [found[mask] for mask in order] + [grad_x],
            like(shape, F32),
            24,
        )
    total, out = tied((total, out), found[3], found[6])
    grad_self, grad_neigh = small_call(
        finish_kernel,
        [like((width, full), F32)] * 2,
        [total, crossed(total, near)],
        [pltpu.VMEM((parts_total, piece, full), F32)],
    )
    return (out.reshape(rows, width), grad_x.reshape(rows, width), grad_self, grad_neigh)


def solution(mesh):
    def body(*args):
        rounds = args[7].shape[1]
        small = mesh.shape["dom"] == 8 and mesh.shape["feat"] == 4
        nearly_all = mesh.shape["dom"] <= rounds + 2
        return (dense_body if small and nearly_all else sparse_body)(*args)

    placed = (
        P("dom", "feat"),
        P("feat", None),
        P("feat", None),
        P("dom"),
        P("dom", None, None, None),
        P("dom", None),
        P("dom", None),
        P("dom", None, None, None, None),
        P("dom", None, None),
        P("dom", None, None),
        P("dom", "feat"),
    )
    return jax.shard_map(
        body,
        mesh=mesh,
        in_specs=placed,
        out_specs=(P("dom", "feat"), P("dom", "feat"), P("feat", None), P("feat", None)),
        check_vma=False,
    )
```

```python
import functools

import jax
import jax.numpy as jnp
from jax import lax
from jax.experimental import pallas as pl
from jax.experimental.pallas import tpu as pltpu
from jax.sharding import PartitionSpec as P

F32 = jnp.float32
BF16 = jnp.bfloat16
VMEM = pl.BlockSpec(memory_space=pltpu.VMEM)
SMEM = pl.BlockSpec(memory_space=pltpu.SMEM)


def shifted(x, axis, by):
    devices = lax.axis_size(axis)
    return lax.ppermute(x, axis, [(i, (i + by) % devices) for i in range(devices)])


def spread(parts, block_ids, count):
    table = (block_ids[:, None] == jnp.arange(count, dtype=jnp.int32)[None, :]).astype(F32)
    return jnp.einsum("kc,kif->cif", table, parts, precision=lax.Precision.HIGHEST)


def tile_apply(tiles, blocks):
    return jnp.einsum("kij,kjf->kif", tiles, blocks, preferred_element_type=F32)


def tile_apply_back(tiles, blocks):
    return jnp.einsum("kji,kjf->kif", tiles, blocks, preferred_element_type=F32)


def round_offsets(parts_total, rounds):
    return [(step + 1) * parts_total // (rounds + 1) for step in range(rounds)]


def sparse_body(
    features,
    w_self,
    w_neigh,
    degree,
    local_vals,
    local_dst,
    local_src,
    remote_vals,
    remote_dst,
    remote_src,
    cotangent,
):
    rows, width = features.shape
    block = local_vals.shape[-1]
    nblocks = rows // block
    rounds = remote_vals.shape[1]
    parts_total = lax.axis_size("dom")
    offsets = round_offsets(parts_total, rounds)
    blocks = features.reshape(nblocks, block, width)
    totals = spread(
        tile_apply(local_vals[0], jnp.take(blocks, local_src[0], axis=0)), local_dst[0], nblocks
    )
    arrived_ids = []
    for step in range(rounds):
        partial_blocks = tile_apply(
            remote_vals[0, step], jnp.take(blocks, remote_src[0, step], axis=0)
        ).astype(BF16)
        arrived, block_ids = shifted((partial_blocks, remote_dst[0, step]), "dom", offsets[step])
        arrived_ids.append(block_ids)
        totals = totals + spread(arrived.astype(F32), block_ids, nblocks)
    inverse = 1.0 / degree.astype(F32)
    agg = (totals.reshape(rows, width) * inverse[:, None]).astype(BF16)
    stacked = jnp.concatenate([features, agg], axis=1)
    weights = jnp.concatenate([w_self, w_neigh], axis=0)
    pre = lax.psum_scatter(
        lax.dot_general(weights, stacked, (((0,), (1,)), ((), ())), preferred_element_type=F32),
        "feat",
        scatter_dimension=0,
        tiled=True,
    ).T
    sigma = jax.nn.sigmoid(pre)
    out = (pre * sigma).astype(BF16)
    dpre = (cotangent.astype(F32) * sigma * (1.0 + pre * (1.0 - sigma))).astype(BF16)
    dpre_all = lax.all_gather(dpre, "feat", axis=1, tiled=True)
    dz_total = lax.dot_general(
        dpre_all, weights, (((1,), (1,)), ((), ())), preferred_element_type=F32
    )
    grad_local = lax.dot_general(
        stacked, dpre_all, (((0,), (0,)), ((), ())), preferred_element_type=F32
    )
    dx_self = dz_total[:, :width]
    dsum = (dz_total[:, width:] * inverse[:, None]).astype(BF16).reshape(nblocks, block, width)
    grad_all = lax.psum(grad_local, "dom")
    back = spread(
        tile_apply_back(local_vals[0], jnp.take(dsum, local_dst[0], axis=0)), local_src[0], nblocks
    )
    for step in range(rounds):
        picked = jnp.take(dsum, arrived_ids[step], axis=0)
        returned = shifted(picked, "dom", parts_total - offsets[step])
        back = back + spread(
            tile_apply_back(remote_vals[0, step], returned), remote_src[0, step], nblocks
        )
    grad_x = dx_self + back.reshape(rows, width)
    return (out, grad_x, grad_all[:width], grad_all[width:])


def tile_counts(rvals, lvals):
    return rvals.shape[0], rvals.shape[1], lvals.shape[0]


def round_of(offset, offsets):
    step, known = jnp.int32(0), offset < 0
    for at, this in enumerate(offsets):
        step = jnp.where(offset == this, at, step)
        known = known | (offset == this)
    return step, known


def crossed_block(block_id, mine, per_feat):
    return ((block_id // per_feat) ^ mine) * per_feat + block_id % per_feat


def tile_groups(masks, offsets, parts_total, me, groups, tiles):
    jobs = []
    for at, mask in enumerate(masks):
        if mask == 0:
            for first in range(0, tiles, groups):
                count = min(groups, tiles - first)
                jobs.append((at, None, None, first, count))
        else:
            offset = lax.rem((me ^ mask) - me + parts_total, parts_total)
            step, known = round_of(offset, offsets)
            jobs.append((at, step, known, None, groups))
    return jobs


def flat(masks):
    return [m for group in masks for m in (group if isinstance(group, list) else [group])]


def tiles_kernel(masks, offsets, parts_total, back, feats, extras, *refs):
    ids_in, (lvals, rvals), refs = refs[:4], refs[4:6], refs[6:]
    ids, id_sems, refs = refs[-5:-1], refs[-1], refs[:-5]
    id_copies = [
        pltpu.make_async_copy(ids_in[n], ids[n], id_sems.at[n]) for n in range(len(ids))
    ]
    for copy in id_copies:
        copy.start()
    groups_of, masks = masks, flat(masks)
    me = lax.axis_index("dom")
    mine = lax.axis_index("feat")
    rounds, groups, tiles = tile_counts(rvals, lvals)
    jobs = tile_groups(masks, offsets, parts_total, me, groups, tiles)
    held, prod, acc, sems = refs[-4:]
    copies = []
    for slot, (at, step, known, first, count) in enumerate(jobs):
        source = lvals.at[pl.ds(first, count)] if step is None else rvals.at[step]
        copy = pltpu.make_async_copy(source, held.at[slot, pl.ds(0, count)], sems.at[slot])
        copy.start()
        copies.append(copy)
    if back:
        own_ref, grad_ref = refs[len(masks)], refs[len(masks) + 1]
        blocks = refs[: len(masks)]
        sinks = [grad_ref] * len(masks)
        acc[0] = own_ref[...]
    else:
        blocks = [refs[0]] * len(masks)
        sinks, used = [], 1 + extras
        for group in groups_of:
            if isinstance(group, list):
                sinks += [refs[used].at[n] for n in range(len(group))]
            else:
                sinks.append(refs[used])
            used += 1
    if extras:
        pieces, pair = refs[used : used + feats], refs[used + feats]
        pair[0] = refs[2][...]
        pair[1] = refs[3][...]
        for mask, piece in enumerate(pieces):
            rows = pl.ds((mine ^ mask) * piece.shape[1], piece.shape[1])
            piece[0] = refs[0][rows]
            piece[1] = refs[1][rows]
    total = 0
    for copy in id_copies:
        copy.wait()
    ldst, lsrc, rdst, rsrc = ids
    for slot, (at, step, known, first, count) in enumerate(jobs):
        copies[slot].wait()
        if step is None:
            dst = [ldst[0, first + k] for k in range(count)]
            src = [lsrc[0, first + k] for k in range(count)]
        else:
            dst = [rdst[step, 0, k] for k in range(count)]
            src = [rsrc[step, 0, k] for k in range(count)]
        half = slot % 2
        for k in range(len(dst)):
            if back:
                per_feat = blocks[at].shape[0] // feats
                block = blocks[at][crossed_block(dst[k], mine, per_feat)]
                product = lax.dot_general(
                    held[slot, k], block, (((0,), (0,)), ((), ())), preferred_element_type=F32
                )
            else:
                product = jnp.dot(
                    held[slot, k], blocks[at][src[k]], preferred_element_type=F32
                )
            prod[half, k] = product if known is None else jnp.where(known, product, 0.0)
        fresh = not back and (slot == 0 or jobs[slot - 1][0] != at)
        if fresh:
            total = at % 2
            acc[total] = jnp.zeros(acc.shape[1:], F32)
        for k in range(len(dst)):
            into = src[k] if back else dst[k]
            acc[total, into] = acc[total, into] + prod[half, k]
        last = slot == len(jobs) - 1 or jobs[slot + 1][0] != at
        if last and (not back or slot == len(jobs) - 1):
            sinks[at][...] = acc[total].astype(sinks[at].dtype)


def tiles_call(masks, offsets, parts_total, back, feats, fixed, blocks, sinks, room):
    ids, lvals, rvals = fixed
    rounds, groups, tiles = tile_counts(rvals, lvals)
    nblocks, block, width = blocks[0].shape
    slots = sum(-(-tiles // groups) if mask == 0 else 1 for mask in flat(masks))
    extras = 0 if back else len(blocks) - 1
    return pl.pallas_call(
        functools.partial(tiles_kernel, masks, offsets, parts_total, back, feats, extras),
        out_shape=sinks,
        in_specs=[pl.BlockSpec(memory_space=pltpu.HBM)] * 6
        + [VMEM] * len(blocks),
        out_specs=jax.tree.map(lambda _: VMEM, sinks),
        scratch_shapes=[
            pltpu.VMEM((slots, groups, block, block), BF16),
            pltpu.VMEM((2, groups, block, width), F32),
            pltpu.VMEM((2, nblocks, block, width), F32),
            pltpu.SemaphoreType.DMA((slots,)),
            *[pltpu.SMEM(t.shape, jnp.int32) for t in ids],
            pltpu.SemaphoreType.DMA((len(ids),)),
        ],
        compiler_params=pltpu.CompilerParams(vmem_limit_bytes=room * 2**20),
        cost_estimate=pl.CostEstimate(flops=1, bytes_accessed=1, transcendentals=0),
    )(*ids, lvals, rvals, *blocks)


def small_call(kernel, outs, arrays, scratch=(), room=24):
    return pl.pallas_call(
        kernel,
        out_shape=outs,
        in_specs=[VMEM] * len(arrays),
        out_specs=[VMEM] * len(outs),
        scratch_shapes=scratch,
        compiler_params=pltpu.CompilerParams(vmem_limit_bytes=room * 2**20),
        cost_estimate=pl.CostEstimate(flops=1, bytes_accessed=1, transcendentals=0),
    )(*arrays)


def agg_kernel(feats, inv_ref, keep_ref, *refs):
    mine = lax.axis_index("feat")
    far_refs, agg_ref, piece_refs = refs[: -1 - feats], refs[-1 - feats], refs[-feats:]
    per_feat = piece_refs[0].shape[0]
    sums = keep_ref[...]
    for ref in far_refs:
        sums = sums + ref[...].astype(F32)
    agg_ref[...] = (sums * inv_ref[...]).astype(BF16)
    for mask, piece in enumerate(piece_refs):
        piece[...] = agg_ref[pl.ds((mine ^ mask) * per_feat, per_feat)]


def joined(parts):
    return jnp.concatenate(parts, axis=1)


def dense_kernel(feats, inv_ref, *refs):
    mine = lax.axis_index("feat")
    w_refs, early_refs, a_refs = refs[:feats], refs[feats : 2 * feats], refs[2 * feats : 3 * feats]
    sent_refs, own_ref = refs[3 * feats : 4 * feats - 1], refs[4 * feats - 1]
    dsum_refs = refs[4 * feats : 5 * feats]
    held = refs[-1]
    full = w_refs[0].shape[2]
    some, width = held.shape[1:]
    pre = jnp.zeros((some, full), F32)
    for mask in range(feats):
        early = early_refs[mask]
        pre = pre + jnp.dot(
            early[0].reshape(some, width), w_refs[mask][0], preferred_element_type=F32
        )
        pre = pre + jnp.dot(
            a_refs[mask][...].reshape(some, width), w_refs[mask][1], preferred_element_type=F32
        )
        held[mine ^ mask] = early[1].reshape(some, width)
    sigma = 1.0 / (1.0 + jnp.exp(-pre))
    out = (pre * sigma).astype(BF16)
    cot = joined([held[j] for j in range(feats)]).astype(F32)
    dpre = (cot * sigma * (1.0 + pre * (1.0 - sigma))).astype(BF16)
    for mask in range(feats):
        dagg = lax.dot_general(
            dpre, w_refs[mask][1], (((1,), (1,)), ((), ())), preferred_element_type=F32
        )
        dsum_refs[mask][...] = (dagg * inv_ref[...]).astype(BF16)
    for j in range(feats):
        cols = slice(j * width, (j + 1) * width)
        for sent in sent_refs:
            sent[j] = dpre[:, cols]
        held[j] = out[:, cols]
    own_ref[...] = held[mine]
    for mask, sent in enumerate(sent_refs, 1):
        sent[feats] = held[mine ^ mask]


def grad_kernel(feats, f_ref, a_ref, w_ref, *refs):
    me = lax.axis_index("dom")
    mine = lax.axis_index("feat")
    dpre_refs, (dx_ref, give_ref, keep_ref, held) = refs[:feats], refs[feats:]
    width = f_ref.shape[1]
    piece = held.shape[1]
    some = dpre_refs[0].shape[1]
    parts = [0.0, 0.0]
    for mask, dpre_ref in enumerate(dpre_refs):
        dpre = joined([dpre_ref[j] for j in range(feats)])
        rows = pl.ds(pl.multiple_of((mine ^ mask) * some, some), some)
        for at, ref in enumerate((f_ref, a_ref)):
            parts[at] = parts[at] + lax.dot_general(
                ref[rows], dpre, (((0,), (0,)), ((), ())), preferred_element_type=F32
            )
        dx_ref[rows] = lax.dot_general(
            dpre, w_ref[...], (((1,), (1,)), ((), ())), preferred_element_type=F32
        )
    for at, part in enumerate(parts):
        for j in range(width // piece):
            held[at * (width // piece) + j] = part[j * piece : (j + 1) * piece]
    side = me % 2
    for at in range(give_ref.shape[0]):
        give_ref[at] = held[2 * at + 1 - side].astype(BF16)
        keep_ref[at] = held[2 * at + side]


def finish_kernel(mine_ref, other_ref, self_ref, neigh_ref, held):
    side = lax.axis_index("dom") % 2
    for at in range(mine_ref.shape[0]):
        held[2 * at + side] = mine_ref[at].astype(F32)
        held[2 * at + 1 - side] = other_ref[at].astype(F32)
    some = held.shape[1]
    half = held.shape[0] // 2
    for j in range(half):
        self_ref[j * some : (j + 1) * some] = held[j]
        neigh_ref[j * some : (j + 1) * some] = held[half + j]


def place_kernel(*refs):
    mine = lax.axis_index("feat")
    own_ref, *come_refs, out_ref = refs
    out_ref[mine] = own_ref[...]
    for mask, come in enumerate(come_refs, 1):
        out_ref[mine ^ mask] = come[out_ref.shape[0]]


def swap_feat(x):
    return lax.all_to_all(x, "feat", split_axis=0, concat_axis=0, tiled=True)


def crossed(x, mask, axis="dom"):
    return lax.ppermute(x, axis, [(i, i ^ mask) for i in range(lax.axis_size(axis))])


def like(shape, dtype):
    return jax.ShapeDtypeStruct(shape, dtype)


def dense_body(
    features,
    w_self,
    w_neigh,
    degree,
    local_vals,
    local_dst,
    local_src,
    remote_vals,
    remote_dst,
    remote_src,
    cotangent,
):
    rows, width = features.shape
    block = local_vals.shape[-1]
    nblocks = rows // block
    rounds = remote_vals.shape[1]
    parts_total = lax.axis_size("dom")
    feats = lax.axis_size("feat")
    some = rows // feats
    per_feat = nblocks // feats
    full = feats * width
    offsets = round_offsets(parts_total, rounds)
    near, far = 1, list(range(parts_total - 2, 0, -2))
    bits = [1, 2, 4]
    mine = lax.axis_index("feat").astype(jnp.int32)
    inverse = 1.0 / degree.astype(F32)
    inv_rows = lax.dynamic_slice(inverse, (mine * some,), (some,))[:, None]
    ids = (
        local_dst,
        local_src,
        jnp.swapaxes(remote_dst, 0, 1),
        jnp.swapaxes(remote_src, 0, 1),
    )
    shape = (nblocks, block, width)
    blocks = features.reshape(shape)
    fixed = (ids, local_vals[0], remote_vals[0])

    def forward(masks, arrays, sinks):
        return tiles_call(
            masks, offsets, parts_total, False, feats, fixed, arrays, sinks, 62
        )

    def relayed(x):
        over = crossed(x, 2, "feat")
        return [x, crossed(x, 1, "feat"), over, crossed(over, 1, "feat")]

    def tied(x, *others):
        return lax.optimization_barrier((x, others))[0]

    sends = forward([7, 5, 3, 1], [blocks], [like(shape, BF16)] * 4)
    made = forward(
        [6, 4, 2, 0],
        [blocks, cotangent.reshape(shape), w_self, w_neigh],
        [like(shape, F32)] * 4
        + [like((2, per_feat, block, width), BF16)] * feats
        + [like((2, width, full), BF16)],
    )
    keep_6, keep_4, keep_2, keep = made[:4]
    early_pieces, pair = made[4:-1], made[-1]
    weights = relayed(pair)
    near_6, near_4, near_2 = (crossed(send, near) for send in sends[:3])
    sum_6 = (keep_6 + near_6.astype(F32)).astype(BF16)
    near_4, weights[2] = lax.optimization_barrier((near_4, weights[2]))
    sum_4 = (keep_4 + near_4.astype(F32) + crossed(sum_6, 2).astype(F32)).astype(BF16)
    far_0 = crossed(sum_4, 4)
    keep_2, send_1, early_pieces = tied((keep_2, sends[3], early_pieces), sum_4)
    near_0 = crossed(send_1, near)
    sum_2 = (keep_2 + near_2.astype(F32)).astype(BF16)
    mid_0 = crossed(sum_2, 2)
    early_2, early_3 = crossed(early_pieces[2], 2, "feat"), crossed(early_pieces[3], 3, "feat")
    far_0, early_2, early_3, early_1 = lax.optimization_barrier(
        (far_0, early_2, early_3, early_pieces[1])
    )
    early = [early_pieces[0], crossed(early_1, 1, "feat"), early_2, early_3]
    part = keep + mid_0.astype(F32) + near_0.astype(F32)
    arrived = [far_0]
    early, weights, arrived = lax.optimization_barrier((early, weights, arrived))
    agg, *agg_pieces = small_call(
        functools.partial(agg_kernel, feats),
        [like(shape, BF16)] + [like((per_feat, block, width), BF16)] * feats,
        [inverse.reshape(nblocks, block, 1), part, *arrived],
    )
    agg_rows = [agg_pieces[0]] + [crossed(agg_pieces[m], m, "feat") for m in range(1, feats)]
    *sent, own_out, p0, p1, p2, p3 = small_call(
        functools.partial(dense_kernel, feats),
        [like((feats + 1, some, width), BF16)] * (feats - 1)
        + [like((some, width), BF16)] * (1 + feats),
        [inv_rows, *weights, *early, *agg_rows],
        [pltpu.VMEM((feats, some, width), BF16)],
    )
    dsum_pieces = [p0, p1, p2, p3]
    dsum = jnp.concatenate(
        [dsum_pieces[0]] + [crossed(dsum_pieces[m], m, "feat") for m in range(1, feats)], axis=0
    ).reshape(shape)
    found = {0: dsum}
    for mask in (4, 2, 1):
        found[mask] = crossed(dsum, mask)
    sent = tied(sent, dsum)
    come_2, come_3 = crossed(sent[1], 2, "feat"), crossed(sent[2], 3, "feat")
    found[4], come_2, come_3, found[2], found[1], sent[0] = lax.optimization_barrier(
        (found[4], come_2, come_3, found[2], found[1], sent[0])
    )
    come = [crossed(sent[0], 1, "feat"), come_2, come_3]
    (out,) = small_call(place_kernel, [like((feats, some, width), BF16)], [own_out, *come])
    dpre = [sent[0], *come]
    found[5] = crossed(found[4], near)
    found[6] = crossed(found[4], 2)
    found[3] = crossed(found[2], near)
    found[5], found[6] = lax.optimization_barrier((found[5], found[6]))
    found[7] = crossed(found[5], 2)
    piece = 2 * width // parts_total
    dx_self, give, keep = small_call(
        functools.partial(grad_kernel, feats),
        [
            like((rows, width), F32),
            like((len(far) + 1, piece, full), BF16),
            like((len(far) + 1, piece, full), F32),
        ],
        [features, agg.reshape(rows, width), w_self, *dpre],
        [pltpu.VMEM((parts_total, piece, full), F32)],
    )
    total = (keep + crossed(give, near).astype(F32)).astype(BF16)
    total = (total.astype(F32) + crossed(total, 2).astype(F32)).astype(BF16)
    total = (total.astype(F32) + crossed(total, 4).astype(F32)).astype(BF16)
    grad_x = dx_self.reshape(shape)
    half = parts_total // 2
    for order in (list(range(half)), list(range(half, parts_total))):
        grad_x = tiles_call(
            order,
            offsets,
            parts_total,
            True,
            feats,
            fixed,
            [found[mask] for mask in order] + [grad_x],
            like(shape, F32),
            24,
        )
    total, out = tied((total, out), found[3], found[6])
    grad_self, grad_neigh = small_call(
        finish_kernel,
        [like((width, full), F32)] * 2,
        [total, crossed(total, near)],
        [pltpu.VMEM((parts_total, piece, full), F32)],
    )
    return (out.reshape(rows, width), grad_x.reshape(rows, width), grad_self, grad_neigh)


def solution(mesh):
    def body(*args):
        rounds = args[7].shape[1]
        small = mesh.shape["dom"] == 8 and mesh.shape["feat"] == 4
        nearly_all = mesh.shape["dom"] <= rounds + 2
        return (dense_body if small and nearly_all else sparse_body)(*args)

    placed = (
        P("dom", "feat"),
        P("feat", None),
        P("feat", None),
        P("dom"),
        P("dom", None, None, None),
        P("dom", None),
        P("dom", None),
        P("dom", None, None, None, None),
        P("dom", None, None),
        P("dom", None, None),
        P("dom", "feat"),
    )
    return jax.shard_map(
        body,
        mesh=mesh,
        in_specs=placed,
        out_specs=(P("dom", "feat"), P("dom", "feat"), P("feat", None), P("feat", None)),
        check_vma=False,
    )
```

```python
import functools

import jax
import jax.numpy as jnp
from jax import lax
from jax.experimental import pallas as pl
from jax.experimental.pallas import tpu as pltpu
from jax.sharding import PartitionSpec as P

F32 = jnp.float32
BF16 = jnp.bfloat16
VMEM = pl.BlockSpec(memory_space=pltpu.VMEM)
SMEM = pl.BlockSpec(memory_space=pltpu.SMEM)


def shifted(x, axis, by):
    devices = lax.axis_size(axis)
    return lax.ppermute(x, axis, [(i, (i + by) % devices) for i in range(devices)])


def spread(parts, block_ids, count):
    table = (block_ids[:, None] == jnp.arange(count, dtype=jnp.int32)[None, :]).astype(F32)
    return jnp.einsum("kc,kif->cif", table, parts, precision=lax.Precision.HIGHEST)


def tile_apply(tiles, blocks):
    return jnp.einsum("kij,kjf->kif", tiles, blocks, preferred_element_type=F32)


def tile_apply_back(tiles, blocks):
    return jnp.einsum("kji,kjf->kif", tiles, blocks, preferred_element_type=F32)


def round_offsets(parts_total, rounds):
    return [(step + 1) * parts_total // (rounds + 1) for step in range(rounds)]


def sparse_body(
    features,
    w_self,
    w_neigh,
    degree,
    local_vals,
    local_dst,
    local_src,
    remote_vals,
    remote_dst,
    remote_src,
    cotangent,
):
    rows, width = features.shape
    block = local_vals.shape[-1]
    nblocks = rows // block
    rounds = remote_vals.shape[1]
    parts_total = lax.axis_size("dom")
    offsets = round_offsets(parts_total, rounds)
    blocks = features.reshape(nblocks, block, width)
    totals = spread(
        tile_apply(local_vals[0], jnp.take(blocks, local_src[0], axis=0)), local_dst[0], nblocks
    )
    arrived_ids = []
    for step in range(rounds):
        partial_blocks = tile_apply(
            remote_vals[0, step], jnp.take(blocks, remote_src[0, step], axis=0)
        ).astype(BF16)
        arrived, block_ids = shifted((partial_blocks, remote_dst[0, step]), "dom", offsets[step])
        arrived_ids.append(block_ids)
        totals = totals + spread(arrived.astype(F32), block_ids, nblocks)
    inverse = 1.0 / degree.astype(F32)
    agg = (totals.reshape(rows, width) * inverse[:, None]).astype(BF16)
    stacked = jnp.concatenate([features, agg], axis=1)
    weights = jnp.concatenate([w_self, w_neigh], axis=0)
    pre = lax.psum_scatter(
        lax.dot_general(weights, stacked, (((0,), (1,)), ((), ())), preferred_element_type=F32),
        "feat",
        scatter_dimension=0,
        tiled=True,
    ).T
    sigma = jax.nn.sigmoid(pre)
    out = (pre * sigma).astype(BF16)
    dpre = (cotangent.astype(F32) * sigma * (1.0 + pre * (1.0 - sigma))).astype(BF16)
    dpre_all = lax.all_gather(dpre, "feat", axis=1, tiled=True)
    dz_total = lax.dot_general(
        dpre_all, weights, (((1,), (1,)), ((), ())), preferred_element_type=F32
    )
    grad_local = lax.dot_general(
        stacked, dpre_all, (((0,), (0,)), ((), ())), preferred_element_type=F32
    )
    dx_self = dz_total[:, :width]
    dsum = (dz_total[:, width:] * inverse[:, None]).astype(BF16).reshape(nblocks, block, width)
    grad_all = lax.psum(grad_local, "dom")
    back = spread(
        tile_apply_back(local_vals[0], jnp.take(dsum, local_dst[0], axis=0)), local_src[0], nblocks
    )
    for step in range(rounds):
        picked = jnp.take(dsum, arrived_ids[step], axis=0)
        returned = shifted(picked, "dom", parts_total - offsets[step])
        back = back + spread(
            tile_apply_back(remote_vals[0, step], returned), remote_src[0, step], nblocks
        )
    grad_x = dx_self + back.reshape(rows, width)
    return (out, grad_x, grad_all[:width], grad_all[width:])


def tile_counts(rvals, lvals):
    return rvals.shape[0], rvals.shape[1], lvals.shape[0]


def round_of(offset, offsets):
    step, known = jnp.int32(0), offset < 0
    for at, this in enumerate(offsets):
        step = jnp.where(offset == this, at, step)
        known = known | (offset == this)
    return step, known


def crossed_block(block_id, mine, per_feat):
    return ((block_id // per_feat) ^ mine) * per_feat + block_id % per_feat


def tile_groups(masks, offsets, parts_total, me, groups, tiles):
    jobs = []
    for at, mask in enumerate(masks):
        if mask == 0:
            for first in range(0, tiles, groups):
                count = min(groups, tiles - first)
                jobs.append((at, None, None, first, count))
        else:
            offset = lax.rem((me ^ mask) - me + parts_total, parts_total)
            step, known = round_of(offset, offsets)
            jobs.append((at, step, known, None, groups))
    return jobs


def flat(masks):
    return [m for group in masks for m in (group if isinstance(group, list) else [group])]


def tiles_kernel(masks, offsets, parts_total, back, feats, extras, *refs):
    ids_in, (lvals, rvals), refs = refs[:4], refs[4:6], refs[6:]
    ids, id_sems, refs = refs[-5:-1], refs[-1], refs[:-5]
    id_copies = [
        pltpu.make_async_copy(ids_in[n], ids[n], id_sems.at[n]) for n in range(len(ids))
    ]
    for copy in id_copies:
        copy.start()
    groups_of, masks = masks, flat(masks)
    me = lax.axis_index("dom")
    mine = lax.axis_index("feat")
    rounds, groups, tiles = tile_counts(rvals, lvals)
    jobs = tile_groups(masks, offsets, parts_total, me, groups, tiles)
    held, prod, acc, sems = refs[-4:]
    copies = []
    for slot, (at, step, known, first, count) in enumerate(jobs):
        source = lvals.at[pl.ds(first, count)] if step is None else rvals.at[step]
        copy = pltpu.make_async_copy(source, held.at[slot, pl.ds(0, count)], sems.at[slot])
        copy.start()
        copies.append(copy)
    if back:
        own_ref, grad_ref = refs[len(masks)], refs[len(masks) + 1]
        blocks = refs[: len(masks)]
        sinks = [grad_ref] * len(masks)
        acc[0] = own_ref[...]
    else:
        blocks = [refs[0]] * len(masks)
        sinks, used = [], 1 + extras
        for group in groups_of:
            if isinstance(group, list):
                sinks += [refs[used].at[n] for n in range(len(group))]
            else:
                sinks.append(refs[used])
            used += 1
    if extras:
        pieces, pair = refs[used : used + feats], refs[used + feats]
        pair[0] = refs[2][...]
        pair[1] = refs[3][...]
        for mask, piece in enumerate(pieces):
            rows = pl.ds((mine ^ mask) * piece.shape[1], piece.shape[1])
            piece[0] = refs[0][rows]
            piece[1] = refs[1][rows]
    total = 0
    for copy in id_copies:
        copy.wait()
    ldst, lsrc, rdst, rsrc = ids
    for slot, (at, step, known, first, count) in enumerate(jobs):
        copies[slot].wait()
        if step is None:
            dst = [ldst[0, first + k] for k in range(count)]
            src = [lsrc[0, first + k] for k in range(count)]
        else:
            dst = [rdst[step, 0, k] for k in range(count)]
            src = [rsrc[step, 0, k] for k in range(count)]
        half = slot % 2
        for k in range(len(dst)):
            if back:
                per_feat = blocks[at].shape[0] // feats
                block = blocks[at][crossed_block(dst[k], mine, per_feat)]
                product = lax.dot_general(
                    held[slot, k], block, (((0,), (0,)), ((), ())), preferred_element_type=F32
                )
            else:
                product = jnp.dot(
                    held[slot, k], blocks[at][src[k]], preferred_element_type=F32
                )
            prod[half, k] = product if known is None else jnp.where(known, product, 0.0)
        fresh = not back and (slot == 0 or jobs[slot - 1][0] != at)
        if fresh:
            total = at % 2
            acc[total] = jnp.zeros(acc.shape[1:], F32)
        for k in range(len(dst)):
            into = src[k] if back else dst[k]
            acc[total, into] = acc[total, into] + prod[half, k]
        last = slot == len(jobs) - 1 or jobs[slot + 1][0] != at
        if last and (not back or slot == len(jobs) - 1):
            sinks[at][...] = acc[total].astype(sinks[at].dtype)


def tiles_call(masks, offsets, parts_total, back, feats, fixed, blocks, sinks, room):
    ids, lvals, rvals = fixed
    rounds, groups, tiles = tile_counts(rvals, lvals)
    nblocks, block, width = blocks[0].shape
    slots = sum(-(-tiles // groups) if mask == 0 else 1 for mask in flat(masks))
    extras = 0 if back else len(blocks) - 1
    return pl.pallas_call(
        functools.partial(tiles_kernel, masks, offsets, parts_total, back, feats, extras),
        out_shape=sinks,
        in_specs=[pl.BlockSpec(memory_space=pltpu.HBM)] * 6
        + [VMEM] * len(blocks),
        out_specs=jax.tree.map(lambda _: VMEM, sinks),
        scratch_shapes=[
            pltpu.VMEM((slots, groups, block, block), BF16),
            pltpu.VMEM((2, groups, block, width), F32),
            pltpu.VMEM((2, nblocks, block, width), F32),
            pltpu.SemaphoreType.DMA((slots,)),
            *[pltpu.SMEM(t.shape, jnp.int32) for t in ids],
            pltpu.SemaphoreType.DMA((len(ids),)),
        ],
        compiler_params=pltpu.CompilerParams(vmem_limit_bytes=room * 2**20),
        cost_estimate=pl.CostEstimate(flops=1, bytes_accessed=1, transcendentals=0),
    )(*ids, lvals, rvals, *blocks)


def small_call(kernel, outs, arrays, scratch=(), room=24):
    return pl.pallas_call(
        kernel,
        out_shape=outs,
        in_specs=[VMEM] * len(arrays),
        out_specs=[VMEM] * len(outs),
        scratch_shapes=scratch,
        compiler_params=pltpu.CompilerParams(vmem_limit_bytes=room * 2**20),
        cost_estimate=pl.CostEstimate(flops=1, bytes_accessed=1, transcendentals=0),
    )(*arrays)


def agg_kernel(feats, inv_ref, keep_ref, *refs):
    mine = lax.axis_index("feat")
    far_refs, agg_ref, piece_refs = refs[: -1 - feats], refs[-1 - feats], refs[-feats:]
    per_feat = piece_refs[0].shape[0]
    sums = keep_ref[...]
    for ref in far_refs:
        sums = sums + ref[...].astype(F32)
    agg_ref[...] = (sums * inv_ref[...]).astype(BF16)
    for mask, piece in enumerate(piece_refs):
        piece[...] = agg_ref[pl.ds((mine ^ mask) * per_feat, per_feat)]


def joined(parts):
    return jnp.concatenate(parts, axis=1)


def dense_kernel(feats, inv_ref, *refs):
    mine = lax.axis_index("feat")
    w_refs, early_refs, a_refs = refs[:feats], refs[feats : 2 * feats], refs[2 * feats : 3 * feats]
    sent_refs, own_ref = refs[3 * feats : 4 * feats - 1], refs[4 * feats - 1]
    dsum_refs = refs[4 * feats : 5 * feats]
    held = refs[-1]
    full = w_refs[0].shape[2]
    some, width = held.shape[1:]
    pre = jnp.zeros((some, full), F32)
    for mask in range(feats):
        early = early_refs[mask]
        pre = pre + jnp.dot(
            early[0].reshape(some, width), w_refs[mask][0], preferred_element_type=F32
        )
        pre = pre + jnp.dot(
            a_refs[mask][...].reshape(some, width), w_refs[mask][1], preferred_element_type=F32
        )
        held[mine ^ mask] = early[1].reshape(some, width)
    sigma = 1.0 / (1.0 + jnp.exp(-pre))
    out = (pre * sigma).astype(BF16)
    cot = joined([held[j] for j in range(feats)]).astype(F32)
    dpre = (cot * sigma * (1.0 + pre * (1.0 - sigma))).astype(BF16)
    for mask in range(feats):
        dagg = lax.dot_general(
            dpre, w_refs[mask][1], (((1,), (1,)), ((), ())), preferred_element_type=F32
        )
        dsum_refs[mask][...] = (dagg * inv_ref[...]).astype(BF16)
    for j in range(feats):
        cols = slice(j * width, (j + 1) * width)
        for sent in sent_refs:
            sent[j] = dpre[:, cols]
        held[j] = out[:, cols]
    own_ref[...] = held[mine]
    for mask, sent in enumerate(sent_refs, 1):
        sent[feats] = held[mine ^ mask]


def grad_kernel(feats, f_ref, a_ref, w_ref, *refs):
    me = lax.axis_index("dom")
    mine = lax.axis_index("feat")
    dpre_refs, (dx_ref, give_ref, keep_ref, held) = refs[:feats], refs[feats:]
    width = f_ref.shape[1]
    piece = held.shape[1]
    some = dpre_refs[0].shape[1]
    parts = [0.0, 0.0]
    for mask, dpre_ref in enumerate(dpre_refs):
        dpre = joined([dpre_ref[j] for j in range(feats)])
        rows = pl.ds(pl.multiple_of((mine ^ mask) * some, some), some)
        for at, ref in enumerate((f_ref, a_ref)):
            parts[at] = parts[at] + lax.dot_general(
                ref[rows], dpre, (((0,), (0,)), ((), ())), preferred_element_type=F32
            )
        dx_ref[rows] = lax.dot_general(
            dpre, w_ref[...], (((1,), (1,)), ((), ())), preferred_element_type=F32
        )
    for at, part in enumerate(parts):
        for j in range(width // piece):
            held[at * (width // piece) + j] = part[j * piece : (j + 1) * piece]
    side = me % 2
    for at in range(give_ref.shape[0]):
        give_ref[at] = held[2 * at + 1 - side].astype(BF16)
        keep_ref[at] = held[2 * at + side]


def finish_kernel(mine_ref, other_ref, self_ref, neigh_ref, held):
    side = lax.axis_index("dom") % 2
    for at in range(mine_ref.shape[0]):
        held[2 * at + side] = mine_ref[at].astype(F32)
        held[2 * at + 1 - side] = other_ref[at].astype(F32)
    some = held.shape[1]
    half = held.shape[0] // 2
    for j in range(half):
        self_ref[j * some : (j + 1) * some] = held[j]
        neigh_ref[j * some : (j + 1) * some] = held[half + j]


def place_kernel(*refs):
    mine = lax.axis_index("feat")
    own_ref, *come_refs, out_ref = refs
    out_ref[mine] = own_ref[...]
    for mask, come in enumerate(come_refs, 1):
        out_ref[mine ^ mask] = come[out_ref.shape[0]]


def swap_feat(x):
    return lax.all_to_all(x, "feat", split_axis=0, concat_axis=0, tiled=True)


def crossed(x, mask, axis="dom"):
    return lax.ppermute(x, axis, [(i, i ^ mask) for i in range(lax.axis_size(axis))])


def like(shape, dtype):
    return jax.ShapeDtypeStruct(shape, dtype)


def dense_body(
    features,
    w_self,
    w_neigh,
    degree,
    local_vals,
    local_dst,
    local_src,
    remote_vals,
    remote_dst,
    remote_src,
    cotangent,
):
    rows, width = features.shape
    block = local_vals.shape[-1]
    nblocks = rows // block
    rounds = remote_vals.shape[1]
    parts_total = lax.axis_size("dom")
    feats = lax.axis_size("feat")
    some = rows // feats
    per_feat = nblocks // feats
    full = feats * width
    offsets = round_offsets(parts_total, rounds)
    near, far = 1, list(range(parts_total - 2, 0, -2))
    bits = [1, 2, 4]
    mine = lax.axis_index("feat").astype(jnp.int32)
    inverse = 1.0 / degree.astype(F32)
    inv_rows = lax.dynamic_slice(inverse, (mine * some,), (some,))[:, None]
    ids = (
        local_dst,
        local_src,
        jnp.swapaxes(remote_dst, 0, 1),
        jnp.swapaxes(remote_src, 0, 1),
    )
    shape = (nblocks, block, width)
    blocks = features.reshape(shape)
    fixed = (ids, local_vals[0], remote_vals[0])

    def forward(masks, arrays, sinks):
        return tiles_call(
            masks, offsets, parts_total, False, feats, fixed, arrays, sinks, 62
        )

    def relayed(x):
        over = crossed(x, 2, "feat")
        return [x, crossed(x, 1, "feat"), over, crossed(over, 1, "feat")]

    def tied(x, *others):
        return lax.optimization_barrier((x, others))[0]

    sends = forward([7, 5, 3, 1], [blocks], [like(shape, BF16)] * 4)
    made = forward(
        [6, 4, 2, 0],
        [blocks, cotangent.reshape(shape), w_self, w_neigh],
        [like(shape, F32)] * 4
        + [like((2, per_feat, block, width), BF16)] * feats
        + [like((2, width, full), BF16)],
    )
    keep_6, keep_4, keep_2, keep = made[:4]
    early_pieces, pair = made[4:-1], made[-1]
    weights = relayed(pair)
    near_6, near_4, near_2 = (crossed(send, near) for send in sends[:3])
    sum_6 = (keep_6 + near_6.astype(F32)).astype(BF16)
    near_4, weights[2] = lax.optimization_barrier((near_4, weights[2]))
    sum_4 = (keep_4 + near_4.astype(F32) + crossed(sum_6, 2).astype(F32)).astype(BF16)
    far_0 = crossed(sum_4, 4)
    keep_2, send_1, early_pieces = tied((keep_2, sends[3], early_pieces), sum_4)
    near_0 = crossed(send_1, near)
    sum_2 = (keep_2 + near_2.astype(F32)).astype(BF16)
    mid_0 = crossed(sum_2, 2)
    early_2, early_3 = crossed(early_pieces[2], 2, "feat"), crossed(early_pieces[3], 3, "feat")
    part = keep + near_0.astype(F32)
    far_0, early_2, early_3, early_1, part = lax.optimization_barrier(
        (far_0, early_2, early_3, early_pieces[1], part)
    )
    early = [early_pieces[0], crossed(early_1, 1, "feat"), early_2, early_3]
    part = part + mid_0.astype(F32)
    arrived = [far_0]
    early, weights, arrived = lax.optimization_barrier((early, weights, arrived))
    agg, *agg_pieces = small_call(
        functools.partial(agg_kernel, feats),
        [like(shape, BF16)] + [like((per_feat, block, width), BF16)] * feats,
        [inverse.reshape(nblocks, block, 1), part, *arrived],
    )
    agg_rows = [agg_pieces[0]] + [crossed(agg_pieces[m], m, "feat") for m in range(1, feats)]
    *sent, own_out, p0, p1, p2, p3 = small_call(
        functools.partial(dense_kernel, feats),
        [like((feats + 1, some, width), BF16)] * (feats - 1)
        + [like((some, width), BF16)] * (1 + feats),
        [inv_rows, *weights, *early, *agg_rows],
        [pltpu.VMEM((feats, some, width), BF16)],
    )
    dsum_pieces = [p0, p1, p2, p3]
    dsum = jnp.concatenate(
        [dsum_pieces[0]] + [crossed(dsum_pieces[m], m, "feat") for m in range(1, feats)], axis=0
    ).reshape(shape)
    found = {0: dsum}
    for mask in (4, 2, 1):
        found[mask] = crossed(dsum, mask)
    sent = tied(sent, dsum)
    come_2, come_3 = crossed(sent[1], 2, "feat"), crossed(sent[2], 3, "feat")
    found[4], come_2, come_3, found[2], found[1], sent[0] = lax.optimization_barrier(
        (found[4], come_2, come_3, found[2], found[1], sent[0])
    )
    come = [crossed(sent[0], 1, "feat"), come_2, come_3]
    (out,) = small_call(place_kernel, [like((feats, some, width), BF16)], [own_out, *come])
    dpre = [sent[0], *come]
    found[6] = crossed(found[4], 2)
    found[3] = crossed(found[2], near)
    found[5] = crossed(found[4], near)
    found[7] = crossed(tied(found[5], found[6]), 2)
    piece = 2 * width // parts_total
    dx_self, give, keep = small_call(
        functools.partial(grad_kernel, feats),
        [
            like((rows, width), F32),
            like((len(far) + 1, piece, full), BF16),
            like((len(far) + 1, piece, full), F32),
        ],
        [features, agg.reshape(rows, width), w_self, *dpre],
        [pltpu.VMEM((parts_total, piece, full), F32)],
    )
    total = (keep + crossed(give, near).astype(F32)).astype(BF16)
    total = (total.astype(F32) + crossed(total, 2).astype(F32)).astype(BF16)
    total = (total.astype(F32) + crossed(total, 4).astype(F32)).astype(BF16)
    grad_x = dx_self.reshape(shape)
    half = parts_total // 2
    for order in (list(range(half)), list(range(half, parts_total))):
        grad_x = tiles_call(
            order,
            offsets,
            parts_total,
            True,
            feats,
            fixed,
            [found[mask] for mask in order] + [grad_x],
            like(shape, F32),
            24,
        )
    total, out = tied((total, out), found[3], found[6])
    grad_self, grad_neigh = small_call(
        finish_kernel,
        [like((width, full), F32)] * 2,
        [total, crossed(total, near)],
        [pltpu.VMEM((parts_total, piece, full), F32)],
    )
    return (out.reshape(rows, width), grad_x.reshape(rows, width), grad_self, grad_neigh)


def solution(mesh):
    def body(*args):
        rounds = args[7].shape[1]
        small = mesh.shape["dom"] == 8 and mesh.shape["feat"] == 4
        nearly_all = mesh.shape["dom"] <= rounds + 2
        return (dense_body if small and nearly_all else sparse_body)(*args)

    placed = (
        P("dom", "feat"),
        P("feat", None),
        P("feat", None),
        P("dom"),
        P("dom", None, None, None),
        P("dom", None),
        P("dom", None),
        P("dom", None, None, None, None),
        P("dom", None, None),
        P("dom", None, None),
        P("dom", "feat"),
    )
    return jax.shard_map(
        body,
        mesh=mesh,
        in_specs=placed,
        out_specs=(P("dom", "feat"), P("dom", "feat"), P("feat", None), P("feat", None)),
        check_vma=False,
    )
```
